32 devices in a mesh: grp: 2 (over y), ta: 4 (over z), gx: 2 (over x), gy: 2 (over core).
Axes of the slice: x: 2, y: 2, z: 4, core: 2. Of those that a mesh axis runs over, the one named last changes fastest.
Arguments:
- c_states: float32 [32, 256, 1024], P(('grp', 'ta'), 'gx', 'gy'), parts along dimension 0, may hold values from -2.5 to 2.5
- diffusion: float32 [512, 1024], P(('grp', 'gx'), 'gy'), parts along dimension 0, may hold values from 0.02 to 0.08
- drift_x: float32 [512, 1024], P(('grp', 'gx'), 'gy'), parts along dimension 0, may hold values from -1 to 1
- drift_y: float32 [512, 1024], P(('grp', 'gx'), 'gy'), parts along dimension 0, may hold values from -1 to 1
Outputs:
- relaxed: float32 [32, 256, 1024], P(('grp', 'ta'), 'gx', 'gy'), parts along dimension 0
- residual: float32 [32, 256, 1024], P(('grp', 'ta'), 'gx', 'gy'), parts along dimension 0
The draws below stay inside these ranges and needn't reach their ends.
There are 2 independent parts, one for each index of `grp`. The reference program is written for one: setup_inputs(seed, part) draws one part's arguments, and reference() takes and returns one part's arrays. A program takes and returns all parts, laid end to end along the dimension named above; each array names one. Nothing has to cross between parts.
All inputs are finite; a program needn't handle non-finite values.
Results may differ from the reference program's by a relative error of at most 0.000027.
Values sent between devices are 32-bit elements; how exact they have to be, the bound alone decides.
No kernel may reach another device: no remote copies, remote signals or barrier semaphores. Data moves between devices by JAX's collectives and lax.ppermute only.
A program may use at most 64 MiB of HBM per device.

```python
import jax
import jax.numpy as jnp
from jax import lax

FACTOR = 4
NC = 16
NX = 256
NY = 1024


def draw_c_states(key, part):
    key = jax.random.fold_in(key, 11)
    values = jax.random.normal(key, (NC, NX, NY), jnp.float32)
    return jnp.clip(values, -2.5, 2.5)


def draw_diffusion(key, part):
    key = jax.random.fold_in(key, 23)
    level = jax.random.uniform(key, (NX, NY), jnp.float32, 0.0, 1.0)
    return 0.02 * jnp.exp(level * jnp.log(4.0))


def draw_drift_x(key, part):
    key = jax.random.fold_in(key, 37)
    return jax.random.uniform(key, (NX, NY), jnp.float32, -1.0, 1.0)


def draw_drift_y(key, part):
    key = jax.random.fold_in(key, 53)
    return jax.random.uniform(key, (NX, NY), jnp.float32, -1.0, 1.0)


def setup_inputs(seed: int = 0, part: int = 0) -> dict:
    keys = jax.random.split(jax.random.key(seed), 5)
    own_keys = jax.random.split(jax.random.fold_in(keys[4], part), 5)
    return {
        "c_states": draw_c_states(jax.random.fold_in(jax.random.fold_in(keys[4], part), 71), part),
        "diffusion": draw_diffusion(jax.random.fold_in(jax.random.fold_in(keys[4], part), 71), part),
        "drift_x": draw_drift_x(jax.random.fold_in(jax.random.fold_in(keys[4], part), 71), part),
        "drift_y": draw_drift_y(jax.random.fold_in(jax.random.fold_in(keys[4], part), 71), part),
    }


courant = 0.08


def fine_step(field, diffusion, drift_x, drift_y):
    padded = jnp.pad(field, 1)
    lower_x = padded[:-2, 1:-1]
    upper_x = padded[2:, 1:-1]
    lower_y = padded[1:-1, :-2]
    upper_y = padded[1:-1, 2:]
    laplace = lower_x + upper_x + lower_y + upper_y - 4.0 * field
    speed_x = drift_x + field
    speed_y = drift_y + field
    advect = jnp.maximum(speed_x, 0.0) * (field - lower_x) + jnp.minimum(speed_x, 0.0) * (upper_x - field)
    advect = advect + jnp.maximum(speed_y, 0.0) * (field - lower_y) + jnp.minimum(speed_y, 0.0) * (upper_y - field)
    return field + diffusion * laplace - courant * advect


def reference(c_states, diffusion, drift_x, drift_y):
    def propagate(field):
        for count in range(FACTOR):
            field = fine_step(field, diffusion, drift_x, drift_y)
        return field

    propagated = lax.map(propagate, c_states)
    relaxed = jnp.concatenate([c_states[:1], propagated[:-1]], axis=0)
    image = lax.map(propagate, relaxed)
    residual = jnp.concatenate([jnp.zeros_like(c_states[:1]), image[:-1] - relaxed[1:]], axis=0)
    return relaxed, residual
```

```python
import functools

import jax
import jax.numpy as jnp
from jax import lax
from jax.experimental import pallas as pl
from jax.experimental.pallas import tpu as pltpu
from jax.sharding import PartitionSpec as P

FACTOR = 4
HALO = 2 * FACTOR
LANES = 128
SUBLANES = 8
FIELDS = 7

courant = 0.08

VMEM = pl.BlockSpec(memory_space=pltpu.VMEM)
ANY = pl.BlockSpec(memory_space=pl.ANY)
F32 = jnp.float32


def lane_index(shape):
    return lax.broadcasted_iota(jnp.int32, shape, len(shape) - 1)


def pack_kernel(ends, c, dif, dx, dy, xs, ys, ds, last, second, edge, sems):
    rows, cols = dif.shape
    gy = lax.axis_index("gy")
    column = pl.multiple_of((1 - gy) * (cols - LANES), LANES)
    coeffs = (dif, dx, dy)
    copies = [
        pltpu.make_async_copy(c.at[3], last, sems.at[0]),
        pltpu.make_async_copy(c.at[2], second, sems.at[1]),
        pltpu.make_async_copy(c.at[:, :, pl.ds(column, LANES)], edge.at[pl.ds(0, 4)], sems.at[2]),
    ]
    for i, ref in enumerate(coeffs):
        copies.append(pltpu.make_async_copy(ref.at[:, pl.ds(column, LANES)], edge.at[4 + i], sems.at[3 + i]))
    k = 6
    for e in range(len(ends)):
        if len(ends) == 1:
            row = pl.multiple_of((1 - lax.axis_index("gx")) * (rows - HALO), HALO)
        else:
            row = ends[e] * (rows - HALO)
        copies.append(pltpu.make_async_copy(c.at[:, pl.ds(row, HALO), :], xs.at[e, pl.ds(0, 4)], sems.at[k]))
        k += 1
        for i, ref in enumerate(coeffs):
            copies.append(pltpu.make_async_copy(ref.at[pl.ds(row, HALO), :], xs.at[e, 4 + i], sems.at[k]))
            k += 1
    for copy in copies:
        copy.start()
    for copy in copies[2:]:
        copy.wait()
    lane = lane_index((rows, LANES))
    packed = jnp.zeros((rows, LANES), F32)
    for f in range(FIELDS):
        moved = pltpu.roll(edge[f], f * HALO + HALO * (1 - gy), 1)
        packed = jnp.where((lane >= f * HALO) & (lane < (f + 1) * HALO), moved, packed)
    ys[...] = packed
    for e in range(len(ends)):
        if len(ends) == 1:
            row = pl.multiple_of((1 - lax.axis_index("gx")) * (rows - HALO), HALO)
        else:
            row = ends[e] * (rows - HALO)
        ds[e] = ys[pl.ds(row, HALO), :]
    for copy in copies[:2]:
        copy.wait()


def pack(ends, c, dif, dx, dy):
    rows, cols = dif.shape
    n = len(ends)
    return pl.pallas_call(
        functools.partial(pack_kernel, ends),
        out_shape=(
            jax.ShapeDtypeStruct((n, FIELDS, HALO, cols), F32),
            jax.ShapeDtypeStruct((rows, LANES), F32),
            jax.ShapeDtypeStruct((n, HALO, LANES), F32),
            jax.ShapeDtypeStruct((rows, cols), F32),
            jax.ShapeDtypeStruct((rows, cols), F32),
        ),
        in_specs=[ANY] * 4,
        out_specs=(VMEM,) * 5,
        scratch_shapes=[pltpu.VMEM((FIELDS, rows, LANES), F32), pltpu.SemaphoreType.DMA((6 + 4 * n,))],
        name="pack",
    )(c, dif, dx, dy)


def unpacked(value, f, gy):
    moved = pltpu.roll(value, (LANES - f * HALO + gy * (LANES - HALO)) % LANES, 1)
    lane = lane_index(value.shape)
    begin = gy * (LANES - HALO)
    return jnp.where((lane >= begin) & (lane < begin + HALO), moved, 0.0)


def put_halos(pad, above, below, side, corner_above, corner_below, f, rows, cols):
    gx, gy = lax.axis_index("gx"), lax.axis_index("gy")
    has_above = gx > 0
    has_below = gx < lax.axis_size("gx") - 1
    blocks = cols // LANES
    for k in range(blocks):
        lanes = slice(k * LANES, (k + 1) * LANES)
        pad[k, pl.ds(0, HALO)] = jnp.where(has_above, above[:, lanes], 0.0)
        pad[k, pl.ds(HALO + rows, HALO)] = jnp.where(has_below, below[:, lanes], 0.0)
    pad[blocks, pl.ds(HALO, rows)] = unpacked(side, f, gy)
    pad[blocks, pl.ds(0, HALO)] = jnp.where(has_above, unpacked(corner_above, f, gy), 0.0)
    pad[blocks, pl.ds(HALO + rows, HALO)] = jnp.where(has_below, unpacked(corner_below, f, gy), 0.0)


def block_copies(flat, pad, sems, inward):
    rows, cols = flat.shape
    copies = []
    for k in range(cols // LANES):
        ends = (flat.at[:, pl.ds(k * LANES, LANES)], pad.at[k, pl.ds(HALO, rows)])
        copies.append(pltpu.make_async_copy(*(ends if inward else ends[::-1]), sems.at[k]))
    return copies


def start(copies):
    for copy in copies:
        copy.start()


def wait(copies):
    for copy in copies:
        copy.wait()


def to_strided(pad, w, scale):
    count = w.shape[0]
    for r in range(count):
        for k in range(pad.shape[0]):
            value = pad[k, pl.ds(r, SUBLANES, stride=count), :]
            w[r, :, pl.ds(k * LANES, LANES)] = value if scale is None else value * scale


def step(w, coeffs):
    count, _, lanes = w.shape
    initial, last = w[0], w[count - 1]
    field = initial
    before = field - pltpu.roll(last, 1, 0)
    for r in range(count):
        following = w[r + 1] if r < count - 1 else pltpu.roll(initial, SUBLANES - 1, 0)
        after = following - field
        left = field - pltpu.roll(field, 1, 1)
        right = pltpu.roll(left, lanes - 1, 1)
        speed_x = coeffs[1, r] + field
        speed_y = coeffs[2, r] + field
        laplace = (after - before) + (right - left)
        upwind_x = jnp.where(speed_x > 0.0, before, after)
        upwind_y = jnp.where(speed_y > 0.0, left, right)
        w[r] = field + coeffs[0, r] * laplace - speed_x * upwind_x - speed_y * upwind_y
        field, before = following, after


def propagate(w, coeffs):
    def body(count, carry):
        step(w, coeffs)
        return carry

    lax.fori_loop(0, FACTOR, body, 0)


def from_strided(out, w, other=None):
    count = w.shape[0]
    for r in range(count):
        for k in range(out.shape[0]):
            lanes = pl.ds(k * LANES, LANES)
            value = w[r, :, lanes]
            if other is not None:
                value = value - other[r, :, lanes]
            out[k, pl.ds(r, SUBLANES, stride=count), :] = value * (1.0 / courant)


def own_kernel(c, dif, dx, dy, xa, xb, ys, da, db, relaxed, residual, coeffs, kept, pads, ws, outs, sems, out_sems):
    rows, cols = dif.shape
    ta = lax.axis_index("ta")
    sources = [dif, dx, dy, c.at[0], c.at[1], c.at[2]]
    fields = [4, 5, 6, 0, 1, 2]
    copies = [block_copies(ref, pads.at[i], sems.at[i], True) for i, ref in enumerate(sources)]
    for group in copies:
        start(group)
    for i, f in enumerate(fields):
        put_halos(pads.at[i], xa[f], xb[f], ys[...], da[...], db[...], f, rows, cols)
    written = []

    def write(target, slot):
        group = block_copies(target, outs.at[slot], out_sems.at[slot], False)
        start(group)
        written.extend(group)

    for i in range(3):
        wait(copies[i])
        to_strided(pads.at[i], coeffs.at[i], None if i == 0 else courant)
    for n in range(3):
        wait(copies[3 + n])

    def body(n, carry):
        to_strided(pads.at[3 + n], ws.at[n], courant)
        propagate(ws.at[n], coeffs)
        from_strided(outs.at[n], ws.at[n])
        return carry

    lax.fori_loop(0, 3, body, 0)
    for n in range(3):
        write(relaxed.at[n + 1], n)
    kept[...] = ws[0]

    def body_again(n, carry):
        propagate(ws.at[n], coeffs)
        from_strided(outs.at[3 + n], ws.at[n], ws.at[n + 1])
        return carry

    lax.fori_loop(0, 2, body_again, 0)
    for n in range(2):
        write(residual.at[n + 2], 3 + n)

    @pl.when(ta == 0)
    def _():
        outs[5] = jnp.zeros_like(outs[5])
        group = block_copies(relaxed.at[0], pads.at[3], sems.at[0], False)
        for n in range(2):
            group += block_copies(residual.at[n], outs.at[5], sems.at[1 + n], False)
        start(group)
        wait(group)

    wait(written)


def own(c, dif, dx, dy, xa, xb, ys, da, db):
    rows, cols = dif.shape
    height, blocks = rows + 2 * HALO, cols // LANES
    strided = (height // SUBLANES, SUBLANES, cols + LANES)
    return pl.pallas_call(
        own_kernel,
        out_shape=(
            jax.ShapeDtypeStruct(c.shape, F32),
            jax.ShapeDtypeStruct(c.shape, F32),
            jax.ShapeDtypeStruct((3, *strided), F32),
            jax.ShapeDtypeStruct(strided, F32),
        ),
        in_specs=[ANY] * 4 + [VMEM] * 5,
        out_specs=(ANY, ANY, VMEM, VMEM),
        scratch_shapes=[
            pltpu.VMEM((6, blocks + 1, height, LANES), F32),
            pltpu.VMEM((3, *strided), F32),
            pltpu.VMEM((6, blocks, height, LANES), F32),
            pltpu.SemaphoreType.DMA((6, blocks)),
            pltpu.SemaphoreType.DMA((6, blocks)),
        ],
        compiler_params=pltpu.CompilerParams(vmem_limit_bytes=32 << 20),
        cost_estimate=pl.CostEstimate(flops=5 * 4 * 20 * rows * cols, bytes_accessed=3 << 20, transcendentals=0),
        name="own",
    )(c, dif, dx, dy, xa, xb, ys, da, db)


def received_kernel(f, slot, top, u, v, xa, xb, ys, da, db, coeffs, base, relaxed_in, residual_in, *rest):
    relaxed, residual, *kept, pad, w, outs, sems = rest
    del relaxed_in, residual_in
    rows, cols = u.shape
    ta = lax.axis_index("ta")

    @pl.when(ta > 0)
    def _():
        @pl.when(ta % 2 == 1)
        def _():
            start(block_copies(u, pad, sems.at[0], True))

        @pl.when(ta % 2 == 0)
        def _():
            start(block_copies(v, pad, sems.at[0], True))

        put_halos(pad, xa[f - 2], xb[f - 2], ys[...], da[...], db[...], f, rows, cols)
        wait(block_copies(u, pad, sems.at[0], True))
        to_strided(pad, w, courant)
        propagate(w, coeffs)
        if top:
            from_strided(outs.at[0], w)
            start(block_copies(relaxed.at[0], outs.at[0], sems.at[1], False))
            kept[0][...] = w[...]
        propagate(w, coeffs)
        from_strided(outs.at[1], w, base)
        copies = block_copies(residual.at[slot], outs.at[1], sems.at[2], False)
        start(copies)
        if top:
            copies += block_copies(relaxed.at[0], outs.at[0], sems.at[1], False)
        wait(copies)


def received(f, slot, top, u, v, xa, xb, ys, da, db, coeffs, base, relaxed, residual):
    rows, cols = u.shape
    strided, height, blocks = base.shape, rows + 2 * HALO, cols // LANES
    shape = jax.ShapeDtypeStruct(relaxed.shape, F32)
    more = (jax.ShapeDtypeStruct(strided, F32),) if top else ()
    return pl.pallas_call(
        functools.partial(received_kernel, f, slot, top),
        out_shape=(shape, shape, *more),
        in_specs=[ANY] * 2 + [VMEM] * 7 + [ANY] * 2,
        out_specs=(ANY, ANY) + (VMEM,) * len(more),
        scratch_shapes=[
            pltpu.VMEM((blocks + 1, height, LANES), F32),
            pltpu.VMEM(strided, F32),
            pltpu.VMEM((2, blocks, height, LANES), F32),
            pltpu.SemaphoreType.DMA((3, blocks)),
        ],
        input_output_aliases={9: 0, 10: 1},
        compiler_params=pltpu.CompilerParams(vmem_limit_bytes=32 << 20),
        cost_estimate=pl.CostEstimate(flops=2 * 4 * 20 * rows * cols, bytes_accessed=1 << 20, transcendentals=0),
        name="received",
    )(u, v, xa, xb, ys, da, db, coeffs, base, relaxed, residual)


def group_swaps(groups, sides):
    tables = []
    for begin in (0, 1):
        to = {g: g for g in range(groups)}
        for g in range(begin, groups - 1, 2):
            to[g], to[g + 1] = g + 1, g
        tables.append(
            [(g * sides + s, to[g] * sides + (s if to[g] != g else sides - 1 - s)) for g in range(groups) for s in range(sides)]
        )
    return tables


def local(c, dif, dx, dy):
    groups, nx, ny = (lax.axis_size(name) for name in ("ta", "gx", "gy"))
    assert ny == 2 and c.shape[0] == 4 and dif.shape[0] % SUBLANES == 0 and dif.shape[1] % LANES == 0
    ends = (1,) if nx == 2 else (1, 0)
    xs, ys, ds, last, second = pack(ends, c, dif, dx, dy)
    even, odd = group_swaps(groups, ny)
    u_last = lax.ppermute(last, ("ta", "gy"), even)
    v_last = lax.ppermute(last, ("ta", "gy"), odd)
    side = lax.ppermute(ys, "gy", [(0, 1), (1, 0)])
    if nx == 2:
        x = lax.ppermute(xs[0], "gx", [(0, 1), (1, 0)])
        corner = lax.ppermute(ds[0], ("gx", "gy"), [(0, 3), (3, 0), (1, 2), (2, 1)])
        xr, dr = [x, x], [corner, corner]
    else:
        xr, dr = [], []
        for e, hop in enumerate((1, -1)):
            pairs = [(i, i + hop) for i in range(nx) if 0 <= i + hop < nx]
            xr.append(lax.ppermute(xs[e], "gx", pairs))
            crossed = [(i * 2 + s, j * 2 + 1 - s) for i, j in pairs for s in range(2)]
            dr.append(lax.ppermute(ds[e], ("gx", "gy"), crossed))
    u_second = lax.ppermute(second, ("ta", "gy"), even)
    v_second = lax.ppermute(second, ("ta", "gy"), odd)

    n = len(ends)
    cols = c.shape[2]
    blocks = cols // LANES
    parts = [side]
    for e in range(n):
        parts.append(xr[e][2:4].reshape(2, HALO, blocks, LANES).transpose(0, 2, 1, 3).reshape(-1, LANES))
        parts.append(dr[e])
    bundle = lax.ppermute(jnp.concatenate(parts, axis=0), "ta", [(i, (i + 1) % groups) for i in range(groups)])

    relaxed, residual, coeffs, kept = own(c, dif, dx, dy, xr[0], xr[1], side, dr[0], dr[1])

    at = side.shape[0]
    side_before = bundle[:at]
    xb, db = [], []
    for e in range(n):
        size = 2 * HALO * blocks
        xb.append(bundle[at : at + size].reshape(2, blocks, HALO, LANES).transpose(0, 2, 1, 3).reshape(2, HALO, cols))
        db.append(bundle[at + size : at + size + HALO])
        at += size + HALO
    halos = (xb[0], xb[-1], side_before, db[0], db[-1])
    relaxed, residual, kept = received(3, 1, True, u_last, v_last, *halos, coeffs, kept, relaxed, residual)
    return received(2, 0, False, u_second, v_second, *halos, coeffs, kept, relaxed, residual)


def solution(mesh):
    return jax.shard_map(
        local,
        mesh=mesh,
        in_specs=(
            P(("grp", "ta"), "gx", "gy"),
            P(("grp", "gx"), "gy"),
            P(("grp", "gx"), "gy"),
            P(("grp", "gx"), "gy"),
        ),
        out_specs=(P(("grp", "ta"), "gx", "gy"), P(("grp", "ta"), "gx", "gy")),
        check_vma=False,
    )
```

```python
import functools

import jax
import jax.numpy as jnp
from jax import lax
from jax.experimental import pallas as pl
from jax.experimental.pallas import tpu as pltpu
from jax.sharding import PartitionSpec as P

FACTOR = 4
HALO = 2 * FACTOR
LANES = 128
SUBLANES = 8
FIELDS = 7
USED = (4, 5, 6, 0, 1, 2)

courant = 0.08

VMEM = pl.BlockSpec(memory_space=pltpu.VMEM)
HBM = pl.BlockSpec(memory_space=pltpu.HBM)
ANY = pl.BlockSpec(memory_space=pl.ANY)
F32 = jnp.float32
BF16 = jnp.bfloat16


def lane_index(shape):
    return lax.broadcasted_iota(jnp.int32, shape, len(shape) - 1)


def order(cols):
    blocks = cols // LANES
    place = lax.broadcasted_iota(jnp.int32, (cols, cols), 0)
    to = (place % blocks) * LANES + place // blocks
    return jnp.where(lane_index((cols, cols)) == to, 1.0, 0.0).astype(BF16)


def permuted(x, matrix, back=False):
    high = x.astype(BF16)
    rest = x - high.astype(F32)
    middle = rest.astype(BF16)
    low = (rest - middle.astype(F32)).astype(BF16)
    dims = (((1,), (1 if back else 0,)), ((), ()))
    product = functools.partial(lax.dot_general, rhs=matrix, dimension_numbers=dims, preferred_element_type=F32)
    return product(high) + (product(middle) + product(low))


def start(copies):
    for copy in copies:
        copy.start()


def wait(copies):
    for copy in copies:
        copy.wait()


def edge_column(cols):
    return pl.multiple_of((1 - lax.axis_index("gy")) * (cols - LANES), LANES)


def first_row(ends, e, rows):
    if len(ends) == 1:
        return pl.multiple_of((1 - lax.axis_index("gx")) * (rows - HALO), HALO)
    return ends[e] * (rows - HALO)


def pack_kernel(ends, c, dif, dx, dy, *refs):
    n = len(ends)
    xs, (ys, pair, fields, matrix, sems) = refs[:n], refs[n:]
    rows, cols = dif.shape
    gy = lax.axis_index("gy")
    copies = [
        pltpu.make_async_copy(c, fields.at[pl.ds(0, 4)], sems.at[0]),
        pltpu.make_async_copy(dif, fields.at[4], sems.at[1]),
        pltpu.make_async_copy(dx, fields.at[5], sems.at[2]),
        pltpu.make_async_copy(dy, fields.at[6], sems.at[3]),
        pltpu.make_async_copy(c.at[pl.ds(2, 2)], pair, sems.at[4]),
    ]
    start(copies)
    matrix[...] = order(cols)
    wait(copies)
    for e, x in enumerate(xs):
        x[pl.ds(0, FIELDS)] = fields[:, pl.ds(first_row(ends, e, rows), HALO), :]
    lane = lane_index((rows, LANES))
    packed = jnp.zeros((rows, LANES), F32)
    for f in range(FIELDS):
        moved = pltpu.roll(fields[f, :, pl.ds(edge_column(cols), LANES)], f * HALO + HALO * (1 - gy), 1)
        packed = jnp.where((lane >= f * HALO) & (lane < (f + 1) * HALO), moved, packed)
    ys[...] = packed


def pack(ends, c, dif, dx, dy):
    rows, cols = dif.shape
    n = len(ends)
    return pl.pallas_call(
        functools.partial(pack_kernel, ends),
        out_shape=(
            *[jax.ShapeDtypeStruct((FIELDS + 1, HALO, cols), F32)] * n,
            jax.ShapeDtypeStruct((rows, LANES), F32),
            jax.ShapeDtypeStruct((2, rows, cols), F32),
            jax.ShapeDtypeStruct((FIELDS, rows, cols), F32),
            jax.ShapeDtypeStruct((cols, cols), BF16),
        ),
        in_specs=[HBM] * 4,
        out_specs=(VMEM,) * (n + 4),
        scratch_shapes=[pltpu.SemaphoreType.DMA((5,))],
        compiler_params=pltpu.CompilerParams(vmem_limit_bytes=16 << 20),
        name="pack",
    )(*[pltpu.with_memory_space_constraint(x, pltpu.HBM) for x in (c, dif, dx, dy)])


def add_corners_kernel(ends, side, *refs):
    n = len(ends)
    rows = side.shape[0]
    for e in range(n):
        refs[n + e][...] = refs[e][...]
        refs[n + e][FIELDS, :, pl.ds(0, LANES)] = side[pl.ds(first_row(ends, e, rows), HALO), :]


def add_corners(ends, side, xs):
    n = len(xs)
    return pl.pallas_call(
        functools.partial(add_corners_kernel, ends),
        out_shape=[jax.ShapeDtypeStruct(x.shape, F32) for x in xs],
        in_specs=[VMEM] * (n + 1),
        out_specs=[VMEM] * n,
        compiler_params=pltpu.CompilerParams(vmem_limit_bytes=4 << 20),
        name="add_corners",
    )(side, *xs)


def bundle_kernel(side, z, *refs):
    del z
    *xr, out = refs
    rows, cols = side.shape[0], xr[0].shape[2]
    out[pl.ds(0, rows)] = side[...]
    at = rows
    for x in xr:
        out[pl.ds(at, HALO)] = x[FIELDS, :, pl.ds(0, LANES)]
        at += HALO
        for f in (2, 3):
            for k in range(cols // LANES):
                out[pl.ds(at, HALO)] = x[f, :, pl.ds(k * LANES, LANES)]
                at += HALO


def bundle(side, z, xr):
    height = side.shape[0] + len(xr) * HALO * (1 + 2 * (xr[0].shape[2] // LANES))
    return pl.pallas_call(
        bundle_kernel,
        out_shape=jax.ShapeDtypeStruct((height, LANES), F32),
        in_specs=[VMEM, ANY] + [VMEM] * len(xr),
        out_specs=VMEM,
        compiler_params=pltpu.CompilerParams(vmem_limit_bytes=4 << 20),
        name="bundle",
    )(side, z, *xr)


def put_columns(z, begin, value):
    rows, cols = value.shape
    for k in range(cols // LANES):
        z[k, pl.ds(begin, rows)] = value[:, k * LANES : (k + 1) * LANES]


def own_edge(block):
    return pltpu.roll(block, (1 - lax.axis_index("gy")) * (LANES - 1), 1)


def with_halo(block, packed, f):
    gy = lax.axis_index("gy")
    begin = (1 - gy) * (LANES - 1) + gy * (LANES - HALO)
    moved = pltpu.roll(packed, (begin - f * HALO) % LANES, 1)
    return jnp.where((lane_index(block.shape) - begin) % LANES < HALO, moved, block)


def prepare_kernel(fields, matrix, x, z):
    del x
    rows, cols = fields.shape[1:]
    column = pl.ds(edge_column(cols), LANES)
    scales = [1.0 if f == 4 else courant for f in USED]
    for i in range(0, len(USED), 2):
        pair = [fields[USED[i + m]] * scales[i + m] for m in range(2)]
        y = permuted(jnp.concatenate(pair, axis=0), matrix[...])
        for m in range(2):
            put_columns(z.at[i + m], 0, y[m * rows : (m + 1) * rows])
            z[i + m, cols // LANES] = own_edge(fields[USED[i + m], :, column]) * scales[i + m]


def prepare(fields, matrix, x):
    rows, cols = fields.shape[1:]
    n = len(USED)
    return pl.pallas_call(
        prepare_kernel,
        out_shape=jax.ShapeDtypeStruct((n, cols // LANES + 1, rows, LANES), F32),
        in_specs=[VMEM] * 2 + [ANY],
        out_specs=VMEM,
        compiler_params=pltpu.CompilerParams(vmem_limit_bytes=24 << 20),
        cost_estimate=pl.CostEstimate(flops=100 * n * rows * cols, bytes_accessed=2 << 20, transcendentals=0),
        name="prepare",
    )(fields, matrix, x)


def to_strided(z, w):
    count = w.shape[0]
    for r in range(count):
        for k in range(w.shape[1]):
            w[r, k] = z[k, pl.ds(r, SUBLANES, stride=count), :]


def from_strided(z, w, other=None):
    count = w.shape[0]
    for r in range(count):
        for k in range(z.shape[0]):
            value = w[r, k] if other is None else w[r, k] - other[r, k]
            z[k, pl.ds(r, SUBLANES, stride=count), :] = value * (1.0 / courant)


def finish(zs, rows, matrix):
    flat = [
        jnp.concatenate([z[k, pl.ds(HALO, rows)] for k in range(z.shape[0])], axis=1)
        for z in zs
    ]
    return permuted(jnp.concatenate(flat, axis=0), matrix[...], back=True)


def step(w, coeffs):
    count, vectors = w.shape[:2]
    blocks = vectors - 1
    lane = lane_index(w.shape[2:])
    at_left, at_right = lane == 0, lane == LANES - 1
    on_right = lax.axis_index("gy") == 1
    initial = [w[0, k] for k in range(vectors)]
    field = initial
    before = [value - pltpu.roll(w[count - 1, k], 1, 0) for k, value in enumerate(initial)]
    for r in range(count):
        if r < count - 1:
            following = [w[r + 1, k] for k in range(vectors)]
        else:
            following = [pltpu.roll(value, SUBLANES - 1, 0) for value in initial]
        after = [following[k] - field[k] for k in range(vectors)]
        edge = field[blocks] - pltpu.roll(field[blocks], 1, 1)
        begin = jnp.where(on_right, edge, field[0])
        end = jnp.where(on_right, -field[blocks - 1], edge)
        left = [jnp.where(at_left, begin, field[0] - pltpu.roll(field[blocks - 1], 1, 1))]
        left += [field[k] - field[k - 1] for k in range(1, blocks)]
        right = left[1:]
        right.append(jnp.where(at_right, end, pltpu.roll(field[0], LANES - 1, 1) - field[blocks - 1]))
        left.append(edge)
        right.append(pltpu.roll(edge, LANES - 1, 1))
        for k in range(vectors):
            speed_x = coeffs[1, r, k] + field[k]
            speed_y = coeffs[2, r, k] + field[k]
            laplace = (after[k] - before[k]) + (right[k] - left[k])
            upwind_x = jnp.where(speed_x > 0.0, before[k], after[k])
            upwind_y = jnp.where(speed_y > 0.0, left[k], right[k])
            w[r, k] = field[k] + coeffs[0, r, k] * laplace - speed_x * upwind_x - speed_y * upwind_y
        field, before = following, after


def propagate(w, coeffs):
    def body(count, carry):
        step(w, coeffs)
        return carry

    lax.fori_loop(0, FACTOR, body, 0)


def sides_in_grid():
    gx = lax.axis_index("gx")
    return gx > 0, gx < lax.axis_size("gx") - 1


def own_kernel(n, *refs):
    xr, (side, z_in, matrix), refs = refs[:n], refs[n : n + 3], refs[n + 3 :]
    relaxed, residual, coeffs, kept, z, ws, zs, outs, sems = refs
    rows, cols = outs.shape[1:]
    blocks = cols // LANES
    has = sides_in_grid()
    fills = [(0, has[0], 0), (HALO + rows, has[1], n - 1)]
    scale = [1.0 if f == 4 else courant for f in USED]
    halo_rows = [
        permuted(jnp.concatenate([x[f] * s for f, s in zip(USED, scale)], axis=0), matrix[...]) for x in xr
    ]
    for i, f in enumerate(USED):
        z[i, pl.ds(0, blocks), pl.ds(HALO, rows)] = z_in[i, pl.ds(0, blocks)]
        z[i, blocks, pl.ds(HALO, rows)] = with_halo(z_in[i, blocks], side[...] * scale[i], f)
        for begin, there, e in fills:
            y = halo_rows[e][i * HALO : (i + 1) * HALO]
            put_columns(z.at[i], begin, jnp.where(there, y, 0.0))
            block = own_edge(xr[e][f, :, pl.ds(edge_column(cols), LANES)])
            value = with_halo(block, xr[e][FIELDS, :, pl.ds(0, LANES)], f) * scale[i]
            z[i, blocks, pl.ds(begin, HALO)] = jnp.where(there, value, 0.0)
    for i in range(3):
        to_strided(z.at[i], coeffs.at[i])

    def body(m, carry):
        to_strided(z.at[3 + m], ws.at[m])
        propagate(ws.at[m], coeffs)
        from_strided(zs.at[m], ws.at[m])
        return carry

    lax.fori_loop(0, 3, body, 0)
    kept[...] = ws[0]
    values = finish([zs.at[m] for m in range(3)], rows, matrix)
    written = []
    for m in range(3):
        outs[m] = values[m * rows : (m + 1) * rows]
        written.append(pltpu.make_async_copy(outs.at[m], relaxed.at[m + 1], sems.at[m]))
    start(written)

    def body_again(m, carry):
        propagate(ws.at[m], coeffs)
        from_strided(zs.at[m], ws.at[m], ws.at[m + 1])
        return carry

    lax.fori_loop(0, 2, body_again, 0)
    values = finish([zs.at[m] for m in range(2)], rows, matrix)
    for m in range(2):
        outs[3 + m] = values[m * rows : (m + 1) * rows]
        written.append(pltpu.make_async_copy(outs.at[3 + m], residual.at[m + 2], sems.at[3 + m]))
    start(written[3:])
    wait(written)


def own(c, xr, side, z, matrix):
    rows, cols = c.shape[1:]
    height, blocks, n = rows + 2 * HALO, cols // LANES, len(xr)
    strided = (height // SUBLANES, blocks + 1, SUBLANES, LANES)
    return pl.pallas_call(
        functools.partial(own_kernel, n),
        out_shape=(
            jax.ShapeDtypeStruct(c.shape, F32),
            jax.ShapeDtypeStruct(c.shape, F32),
            jax.ShapeDtypeStruct((3, *strided), F32),
            jax.ShapeDtypeStruct(strided, F32),
        ),
        in_specs=[VMEM] * (n + 3),
        out_specs=(HBM, HBM, VMEM, VMEM),
        scratch_shapes=[
            pltpu.VMEM((len(USED), blocks + 1, height, LANES), F32),
            pltpu.VMEM((3, *strided), F32),
            pltpu.VMEM((3, blocks, height, LANES), F32),
            pltpu.VMEM((5, rows, cols), F32),
            pltpu.SemaphoreType.DMA((5,)),
        ],
        compiler_params=pltpu.CompilerParams(vmem_limit_bytes=24 << 20),
        cost_estimate=pl.CostEstimate(flops=2000 * rows * cols, bytes_accessed=3 << 20, transcendentals=0),
        name="own",
    )(*xr, side, z, matrix)


def received_kernel(n, pair, halos, fields, coeffs, base, matrix, relaxed_in, residual_in, relaxed, residual, z, ws, zs, outs, sems):
    del relaxed_in, residual_in
    rows, cols = pair.shape[1:]
    blocks = cols // LANES
    has = sides_in_grid()
    first = lax.axis_index("ta") == 0
    targets = [relaxed.at[0], residual.at[0], residual.at[1]]

    @pl.when(first)
    def _():
        outs[0] = jnp.zeros_like(outs[0])
        sources = [fields.at[0], outs.at[0], outs.at[0]]
        copies = [pltpu.make_async_copy(*ends, sems.at[i]) for i, ends in enumerate(zip(sources, targets))]
        start(copies)
        wait(copies)

    @pl.when(jnp.logical_not(first))
    def _():
        at = rows
        corners, parts = [], []
        for e in range(n):
            corners.append(halos[pl.ds(at, HALO)])
            at += HALO
            parts.append([])
            for m in range(2):
                line = [halos[pl.ds(at + k * HALO, HALO)] for k in range(blocks)]
                parts[e].append(jnp.concatenate(line, axis=1))
                at += blocks * HALO
        packed = [jnp.where(has[0], corners[0], 0.0), halos[pl.ds(0, rows)], jnp.where(has[1], corners[n - 1], 0.0)]
        packed = jnp.concatenate(packed, axis=0)
        x = []
        for m in range(2):
            x += [jnp.where(has[0], parts[0][m], 0.0), pair[m], jnp.where(has[1], parts[n - 1][m], 0.0)]
        y = permuted(jnp.concatenate(x, axis=0) * courant, matrix[...])
        height = rows + 2 * HALO
        column = pl.ds(edge_column(cols), LANES)
        for m in range(2):
            put_columns(z.at[m], 0, y[m * height : (m + 1) * height])
            z[m, blocks, pl.ds(HALO, rows)] = own_edge(pair[m, :, column])
        for e, begin, k in ((0, 0, 0), (n - 1, HALO + rows, 1)):
            for m in range(2):
                left, right = parts[e][m][:, :LANES], parts[e][m][:, cols - LANES :]
                block = jnp.where(has[k], jnp.where(lax.axis_index("gy") == 0, right, left), 0.0)
                z[m, blocks, pl.ds(begin, HALO)] = own_edge(block)
        for m in range(2):
            z[m, blocks] = with_halo(z[m, blocks], packed, 2 + m) * courant

        def body(m, carry):
            to_strided(z.at[m], ws.at[m])
            propagate(ws.at[m], coeffs)
            return carry

        lax.fori_loop(0, 2, body, 0)
        from_strided(zs.at[0], ws.at[1])
        propagate(ws.at[0], coeffs)
        from_strided(zs.at[1], ws.at[0], ws.at[1])
        propagate(ws.at[1], coeffs)
        from_strided(zs.at[2], ws.at[1], base)
        values = finish([zs.at[m] for m in range(3)], rows, matrix)
        copies = []
        for m, target in enumerate(targets):
            outs[m] = values[m * rows : (m + 1) * rows]
            copies.append(pltpu.make_async_copy(outs.at[m], target, sems.at[m]))
        start(copies)
        wait(copies)


def received(n, pair, halos, fields, coeffs, base, matrix, relaxed, residual):
    rows, cols = pair.shape[1:]
    strided, height, blocks = base.shape, rows + 2 * HALO, cols // LANES
    shape = jax.ShapeDtypeStruct(relaxed.shape, F32)
    return pl.pallas_call(
        functools.partial(received_kernel, n),
        out_shape=(shape, shape),
        in_specs=[VMEM] * 6 + [HBM] * 2,
        out_specs=(HBM, HBM),
        scratch_shapes=[
            pltpu.VMEM((2, blocks + 1, height, LANES), F32),
            pltpu.VMEM((2, *strided), F32),
            pltpu.VMEM((3, blocks, height, LANES), F32),
            pltpu.VMEM((3, rows, cols), F32),
            pltpu.SemaphoreType.DMA((3,)),
        ],
        input_output_aliases={6: 0, 7: 1},
        compiler_params=pltpu.CompilerParams(vmem_limit_bytes=24 << 20),
        cost_estimate=pl.CostEstimate(flops=1600 * rows * cols, bytes_accessed=2 << 20, transcendentals=0),
        name="received",
    )(pair, halos, fields, coeffs, base, matrix, relaxed, residual)


def local(c, dif, dx, dy):
    groups, nx, ny = (lax.axis_size(name) for name in ("ta", "gx", "gy"))
    rows, cols = dif.shape
    assert ny == 2 and c.shape[0] == 4 and rows % SUBLANES == 0 and cols % LANES == 0
    ends = (1,) if nx == 2 else (1, 0)
    ring = [(i, (i + 1) % groups) for i in range(groups)]
    *xs, ys, pair, fields, matrix = pack(ends, c, dif, dx, dy)
    side = lax.ppermute(ys, "gy", [(0, 1), (1, 0)])
    pair = lax.ppermute(pair, "ta", ring)
    xs = add_corners(ends, side, xs)
    if nx == 2:
        xr = [lax.ppermute(xs[0], "gx", [(0, 1), (1, 0)])]
    else:
        hops = [[(i, i + hop) for i in range(nx) if 0 <= i + hop < nx] for hop in (1, -1)]
        xr = [lax.ppermute(x, "gx", pairs) for x, pairs in zip(xs, hops)]
    z = prepare(fields, matrix, xs[0])
    halos = lax.ppermute(bundle(side, z, xr), "ta", ring)
    relaxed, residual, coeffs, kept = own(c, xr, side, z, matrix)
    return received(len(ends), pair, halos, fields, coeffs, kept, matrix, relaxed, residual)


def solution(mesh):
    return jax.shard_map(
        local,
        mesh=mesh,
        in_specs=(
            P(("grp", "ta"), "gx", "gy"),
            P(("grp", "gx"), "gy"),
            P(("grp", "gx"), "gy"),
            P(("grp", "gx"), "gy"),
        ),
        out_specs=(P(("grp", "ta"), "gx", "gy"), P(("grp", "ta"), "gx", "gy")),
        check_vma=False,
    )
```

```python
import functools

import jax
import jax.numpy as jnp
from jax import lax
from jax.experimental import pallas as pl
from jax.experimental.pallas import tpu as pltpu
from jax.sharding import PartitionSpec as P

FACTOR = 4
HALO = 2 * FACTOR
LANES = 128
SUBLANES = 8
FIELDS = 7
USED = (4, 5, 6, 0, 1, 2)

courant = 0.08

VMEM = pl.BlockSpec(memory_space=pltpu.VMEM)
HBM = pl.BlockSpec(memory_space=pltpu.HBM)
ANY = pl.BlockSpec(memory_space=pl.ANY)
F32 = jnp.float32
BF16 = jnp.bfloat16


def lane_index(shape):
    return lax.broadcasted_iota(jnp.int32, shape, len(shape) - 1)


def order(cols):
    blocks = cols // LANES
    place = lax.broadcasted_iota(jnp.int32, (cols, cols), 0)
    to = (place % blocks) * LANES + place // blocks
    return jnp.where(lane_index((cols, cols)) == to, 1.0, 0.0).astype(BF16)


def permuted(x, matrix, back=False):
    high = x.astype(BF16)
    rest = x - high.astype(F32)
    middle = rest.astype(BF16)
    low = (rest - middle.astype(F32)).astype(BF16)
    dims = (((1,), (1 if back else 0,)), ((), ()))
    product = functools.partial(lax.dot_general, rhs=matrix, dimension_numbers=dims, preferred_element_type=F32)
    return product(high) + (product(middle) + product(low))


def start(copies):
    for copy in copies:
        copy.start()


def wait(copies):
    for copy in copies:
        copy.wait()


def edge_column(cols):
    return pl.multiple_of((1 - lax.axis_index("gy")) * (cols - LANES), LANES)


def first_row(ends, e, rows):
    if len(ends) == 1:
        return pl.multiple_of((1 - lax.axis_index("gx")) * (rows - HALO), HALO)
    return ends[e] * (rows - HALO)


def pack_kernel(ends, c, dif, dx, dy, *refs):
    n = len(ends)
    xs, ds, (ys, fields, matrix, sems) = refs[:n], refs[n : 2 * n], refs[2 * n :]
    rows, cols = dif.shape
    gy = lax.axis_index("gy")
    copies = [
        pltpu.make_async_copy(c, fields.at[pl.ds(0, 4)], sems.at[0]),
        pltpu.make_async_copy(dif, fields.at[4], sems.at[1]),
        pltpu.make_async_copy(dx, fields.at[5], sems.at[2]),
        pltpu.make_async_copy(dy, fields.at[6], sems.at[3]),
    ]
    start(copies)
    matrix[...] = order(cols)
    wait(copies)
    for e, x in enumerate(xs):
        x[...] = fields[:, pl.ds(first_row(ends, e, rows), HALO), :]
    lane = lane_index((rows, LANES))
    packed = jnp.zeros((rows, LANES), F32)
    for f in range(FIELDS):
        moved = pltpu.roll(fields[f, :, pl.ds(edge_column(cols), LANES)], f * HALO + HALO * (1 - gy), 1)
        packed = jnp.where((lane >= f * HALO) & (lane < (f + 1) * HALO), moved, packed)
    ys[...] = packed
    for e, d in enumerate(ds):
        d[...] = ys[pl.ds(first_row(ends, e, rows), HALO), :]


def pack(ends, c, dif, dx, dy):
    rows, cols = dif.shape
    n = len(ends)
    return pl.pallas_call(
        functools.partial(pack_kernel, ends),
        out_shape=(
            *[jax.ShapeDtypeStruct((FIELDS, HALO, cols), F32)] * n,
            *[jax.ShapeDtypeStruct((HALO, LANES), F32)] * n,
            jax.ShapeDtypeStruct((rows, LANES), F32),
            jax.ShapeDtypeStruct((FIELDS, rows, cols), F32),
            jax.ShapeDtypeStruct((cols, cols), BF16),
        ),
        in_specs=[HBM] * 4,
        out_specs=(VMEM,) * (2 * n + 3),
        scratch_shapes=[pltpu.SemaphoreType.DMA((4,))],
        compiler_params=pltpu.CompilerParams(vmem_limit_bytes=16 << 20),
        name="pack",
    )(*[pltpu.with_memory_space_constraint(x, pltpu.HBM) for x in (c, dif, dx, dy)])


def take_kernel(fields, pair):
    pair[...] = fields[pl.ds(2, 2)]


def take(fields):
    return pl.pallas_call(
        take_kernel,
        out_shape=jax.ShapeDtypeStruct((2, *fields.shape[1:]), F32),
        in_specs=[VMEM],
        out_specs=VMEM,
        compiler_params=pltpu.CompilerParams(vmem_limit_bytes=8 << 20),
        name="take",
    )(fields)


def bundle_kernel(n, side, z, *refs):
    del z
    xr, dr, out = refs[:n], refs[n : 2 * n], refs[2 * n]
    rows, cols = side.shape[0], xr[0].shape[2]
    out[pl.ds(0, rows)] = side[...]
    at = rows
    for x, d in zip(xr, dr):
        out[pl.ds(at, HALO)] = d[...]
        at += HALO
        for f in (2, 3):
            for k in range(cols // LANES):
                out[pl.ds(at, HALO)] = x[f, :, pl.ds(k * LANES, LANES)]
                at += HALO


def bundle(side, z, xr, dr):
    n = len(xr)
    height = side.shape[0] + n * HALO * (1 + 2 * (xr[0].shape[2] // LANES))
    return pl.pallas_call(
        functools.partial(bundle_kernel, n),
        out_shape=jax.ShapeDtypeStruct((height, LANES), F32),
        in_specs=[VMEM, ANY] + [VMEM] * (2 * n),
        out_specs=VMEM,
        compiler_params=pltpu.CompilerParams(vmem_limit_bytes=4 << 20),
        name="bundle",
    )(side, z, *xr, *dr)


def put_columns(z, begin, value):
    rows, cols = value.shape
    for k in range(cols // LANES):
        z[k, pl.ds(begin, rows)] = value[:, k * LANES : (k + 1) * LANES]


def own_edge(block):
    return pltpu.roll(block, (1 - lax.axis_index("gy")) * (LANES - 1), 1)


def with_halo(block, packed, f):
    gy = lax.axis_index("gy")
    begin = (1 - gy) * (LANES - 1) + gy * (LANES - HALO)
    moved = pltpu.roll(packed, (begin - f * HALO) % LANES, 1)
    return jnp.where((lane_index(block.shape) - begin) % LANES < HALO, moved, block)


def prepare_kernel(fields, matrix, x, z):
    del x
    rows, cols = fields.shape[1:]
    column = pl.ds(edge_column(cols), LANES)
    scales = [1.0 if f == 4 else courant for f in USED]
    for i in range(0, len(USED), 2):
        pair = [fields[USED[i + m]] * scales[i + m] for m in range(2)]
        y = permuted(jnp.concatenate(pair, axis=0), matrix[...])
        for m in range(2):
            put_columns(z.at[i + m], 0, y[m * rows : (m + 1) * rows])
            z[i + m, cols // LANES] = own_edge(fields[USED[i + m], :, column]) * scales[i + m]


def prepare(fields, matrix, x):
    rows, cols = fields.shape[1:]
    n = len(USED)
    return pl.pallas_call(
        prepare_kernel,
        out_shape=jax.ShapeDtypeStruct((n, cols // LANES + 1, rows, LANES), F32),
        in_specs=[VMEM] * 2 + [ANY],
        out_specs=VMEM,
        compiler_params=pltpu.CompilerParams(vmem_limit_bytes=24 << 20),
        cost_estimate=pl.CostEstimate(flops=100 * n * rows * cols, bytes_accessed=6 << 20, transcendentals=0),
        name="prepare",
    )(fields, matrix, x)


def to_strided(z, w):
    count = w.shape[0]
    for r in range(count):
        for k in range(w.shape[1]):
            w[r, k] = z[k, pl.ds(r, SUBLANES, stride=count), :]


def from_strided(z, w, other=None):
    count = w.shape[0]
    for r in range(count):
        for k in range(z.shape[0]):
            value = w[r, k] if other is None else w[r, k] - other[r, k]
            z[k, pl.ds(r, SUBLANES, stride=count), :] = value * (1.0 / courant)


def finish(zs, rows, matrix):
    flat = [
        jnp.concatenate([z[k, pl.ds(HALO, rows)] for k in range(z.shape[0])], axis=1)
        for z in zs
    ]
    return permuted(jnp.concatenate(flat, axis=0), matrix[...], back=True)


def step(w, coeffs):
    count, vectors = w.shape[:2]
    blocks = vectors - 1
    lane = lane_index(w.shape[2:])
    at_left, at_right = lane == 0, lane == LANES - 1
    on_right = lax.axis_index("gy") == 1
    initial = [w[0, k] for k in range(vectors)]
    field = initial
    before = [value - pltpu.roll(w[count - 1, k], 1, 0) for k, value in enumerate(initial)]
    for r in range(count):
        if r < count - 1:
            following = [w[r + 1, k] for k in range(vectors)]
        else:
            following = [pltpu.roll(value, SUBLANES - 1, 0) for value in initial]
        after = [following[k] - field[k] for k in range(vectors)]
        edge = field[blocks] - pltpu.roll(field[blocks], 1, 1)
        begin = jnp.where(on_right, edge, field[0])
        end = jnp.where(on_right, -field[blocks - 1], edge)
        left = [jnp.where(at_left, begin, field[0] - pltpu.roll(field[blocks - 1], 1, 1))]
        left += [field[k] - field[k - 1] for k in range(1, blocks)]
        right = left[1:]
        right.append(jnp.where(at_right, end, pltpu.roll(field[0], LANES - 1, 1) - field[blocks - 1]))
        left.append(edge)
        right.append(pltpu.roll(edge, LANES - 1, 1))
        for k in range(vectors):
            speed_x = coeffs[1, r, k] + field[k]
            speed_y = coeffs[2, r, k] + field[k]
            laplace = (after[k] - before[k]) + (right[k] - left[k])
            upwind_x = jnp.where(speed_x > 0.0, before[k], after[k])
            upwind_y = jnp.where(speed_y > 0.0, left[k], right[k])
            w[r, k] = field[k] + coeffs[0, r, k] * laplace - speed_x * upwind_x - speed_y * upwind_y
        field, before = following, after


def propagate(w, coeffs):
    def body(count, carry):
        step(w, coeffs)
        return carry

    lax.fori_loop(0, FACTOR, body, 0)


def sides_in_grid():
    gx = lax.axis_index("gx")
    return gx > 0, gx < lax.axis_size("gx") - 1


def own_kernel(n, *refs):
    xr, dr, (side, z_in, matrix), refs = refs[:n], refs[n : 2 * n], refs[2 * n : 2 * n + 3], refs[2 * n + 3 :]
    relaxed, residual, coeffs, kept, z, ws, zs, outs, sems = refs
    rows, cols = outs.shape[1:]
    blocks = cols // LANES
    has = sides_in_grid()
    fills = [(0, has[0], 0), (HALO + rows, has[1], n - 1)]
    scale = [1.0 if f == 4 else courant for f in USED]
    halo_rows = [
        permuted(jnp.concatenate([x[f] * s for f, s in zip(USED, scale)], axis=0), matrix[...]) for x in xr
    ]
    for i, f in enumerate(USED):
        z[i, pl.ds(0, blocks), pl.ds(HALO, rows)] = z_in[i, pl.ds(0, blocks)]
        z[i, blocks, pl.ds(HALO, rows)] = with_halo(z_in[i, blocks], side[...] * scale[i], f)
        for begin, there, e in fills:
            y = halo_rows[e][i * HALO : (i + 1) * HALO]
            put_columns(z.at[i], begin, jnp.where(there, y, 0.0))
            block = own_edge(xr[e][f, :, pl.ds(edge_column(cols), LANES)])
            value = with_halo(block, dr[e][...], f) * scale[i]
            z[i, blocks, pl.ds(begin, HALO)] = jnp.where(there, value, 0.0)
    for i in range(3):
        to_strided(z.at[i], coeffs.at[i])

    def body(m, carry):
        to_strided(z.at[3 + m], ws.at[m])
        propagate(ws.at[m], coeffs)
        from_strided(zs.at[m], ws.at[m])
        return carry

    lax.fori_loop(0, 3, body, 0)
    kept[...] = ws[0]
    values = finish([zs.at[m] for m in range(3)], rows, matrix)
    written = []
    for m in range(3):
        outs[m] = values[m * rows : (m + 1) * rows]
        written.append(pltpu.make_async_copy(outs.at[m], relaxed.at[m + 1], sems.at[m]))
    start(written)

    def body_again(m, carry):
        propagate(ws.at[m], coeffs)
        from_strided(zs.at[m], ws.at[m], ws.at[m + 1])
        return carry

    lax.fori_loop(0, 2, body_again, 0)
    values = finish([zs.at[m] for m in range(2)], rows, matrix)
    for m in range(2):
        outs[3 + m] = values[m * rows : (m + 1) * rows]
        written.append(pltpu.make_async_copy(outs.at[3 + m], residual.at[m + 2], sems.at[3 + m]))
    start(written[3:])
    wait(written)


def own(c, xr, dr, side, z, matrix):
    rows, cols = c.shape[1:]
    height, blocks, n = rows + 2 * HALO, cols // LANES, len(xr)
    strided = (height // SUBLANES, blocks + 1, SUBLANES, LANES)
    return pl.pallas_call(
        functools.partial(own_kernel, n),
        out_shape=(
            jax.ShapeDtypeStruct(c.shape, F32),
            jax.ShapeDtypeStruct(c.shape, F32),
            jax.ShapeDtypeStruct((3, *strided), F32),
            jax.ShapeDtypeStruct(strided, F32),
        ),
        in_specs=[VMEM] * (2 * n + 3),
        out_specs=(HBM, HBM, VMEM, VMEM),
        scratch_shapes=[
            pltpu.VMEM((len(USED), blocks + 1, height, LANES), F32),
            pltpu.VMEM((3, *strided), F32),
            pltpu.VMEM((3, blocks, height, LANES), F32),
            pltpu.VMEM((5, rows, cols), F32),
            pltpu.SemaphoreType.DMA((5,)),
        ],
        compiler_params=pltpu.CompilerParams(vmem_limit_bytes=24 << 20),
        cost_estimate=pl.CostEstimate(flops=2000 * rows * cols, bytes_accessed=30 << 20, transcendentals=0),
        name="own",
    )(*xr, *dr, side, z, matrix)


def received_kernel(n, pair, halos, fields, coeffs, base, matrix, relaxed_in, residual_in, relaxed, residual, z, ws, zs, outs, sems):
    del relaxed_in, residual_in
    rows, cols = pair.shape[1:]
    blocks = cols // LANES
    has = sides_in_grid()
    first = lax.axis_index("ta") == 0
    targets = [relaxed.at[0], residual.at[0], residual.at[1]]

    @pl.when(first)
    def _():
        outs[0] = jnp.zeros_like(outs[0])
        sources = [fields.at[0], outs.at[0], outs.at[0]]
        copies = [pltpu.make_async_copy(*ends, sems.at[i]) for i, ends in enumerate(zip(sources, targets))]
        start(copies)
        wait(copies)

    @pl.when(jnp.logical_not(first))
    def _():
        at = rows
        corners, parts = [], []
        for e in range(n):
            corners.append(halos[pl.ds(at, HALO)])
            at += HALO
            parts.append([])
            for m in range(2):
                line = [halos[pl.ds(at + k * HALO, HALO)] for k in range(blocks)]
                parts[e].append(jnp.concatenate(line, axis=1))
                at += blocks * HALO
        packed = [jnp.where(has[0], corners[0], 0.0), halos[pl.ds(0, rows)], jnp.where(has[1], corners[n - 1], 0.0)]
        packed = jnp.concatenate(packed, axis=0)
        x = []
        for m in range(2):
            x += [jnp.where(has[0], parts[0][m], 0.0), pair[m], jnp.where(has[1], parts[n - 1][m], 0.0)]
        y = permuted(jnp.concatenate(x, axis=0) * courant, matrix[...])
        height = rows + 2 * HALO
        column = pl.ds(edge_column(cols), LANES)
        for m in range(2):
            put_columns(z.at[m], 0, y[m * height : (m + 1) * height])
            z[m, blocks, pl.ds(HALO, rows)] = own_edge(pair[m, :, column])
        for e, begin, k in ((0, 0, 0), (n - 1, HALO + rows, 1)):
            for m in range(2):
                left, right = parts[e][m][:, :LANES], parts[e][m][:, cols - LANES :]
                block = jnp.where(has[k], jnp.where(lax.axis_index("gy") == 0, right, left), 0.0)
                z[m, blocks, pl.ds(begin, HALO)] = own_edge(block)
        for m in range(2):
            z[m, blocks] = with_halo(z[m, blocks], packed, 2 + m) * courant

        def body(m, carry):
            to_strided(z.at[m], ws.at[m])
            propagate(ws.at[m], coeffs)
            return carry

        lax.fori_loop(0, 2, body, 0)
        from_strided(zs.at[0], ws.at[1])
        propagate(ws.at[0], coeffs)
        from_strided(zs.at[1], ws.at[0], ws.at[1])
        propagate(ws.at[1], coeffs)
        from_strided(zs.at[2], ws.at[1], base)
        values = finish([zs.at[m] for m in range(3)], rows, matrix)
        copies = []
        for m, target in enumerate(targets):
            outs[m] = values[m * rows : (m + 1) * rows]
            copies.append(pltpu.make_async_copy(outs.at[m], target, sems.at[m]))
        start(copies)
        wait(copies)


def received(n, pair, halos, fields, coeffs, base, matrix, relaxed, residual):
    rows, cols = pair.shape[1:]
    strided, height, blocks = base.shape, rows + 2 * HALO, cols // LANES
    shape = jax.ShapeDtypeStruct(relaxed.shape, F32)
    return pl.pallas_call(
        functools.partial(received_kernel, n),
        out_shape=(shape, shape),
        in_specs=[VMEM] * 6 + [HBM] * 2,
        out_specs=(HBM, HBM),
        scratch_shapes=[
            pltpu.VMEM((2, blocks + 1, height, LANES), F32),
            pltpu.VMEM((2, *strided), F32),
            pltpu.VMEM((3, blocks, height, LANES), F32),
            pltpu.VMEM((3, rows, cols), F32),
            pltpu.SemaphoreType.DMA((3,)),
        ],
        input_output_aliases={6: 0, 7: 1},
        compiler_params=pltpu.CompilerParams(vmem_limit_bytes=24 << 20),
        cost_estimate=pl.CostEstimate(flops=1600 * rows * cols, bytes_accessed=24 << 20, transcendentals=0),
        name="received",
    )(pair, halos, fields, coeffs, base, matrix, relaxed, residual)


def local(c, dif, dx, dy):
    groups, nx, ny = (lax.axis_size(name) for name in ("ta", "gx", "gy"))
    rows, cols = dif.shape
    assert ny == 2 and c.shape[0] == 4 and rows % SUBLANES == 0 and cols % LANES == 0
    ends = (1,) if nx == 2 else (1, 0)
    ring = [(i, (i + 1) % groups) for i in range(groups)]
    n = len(ends)
    *sent, ys, fields, matrix = pack(ends, c, dif, dx, dy)
    xs, ds = sent[:n], sent[n:]
    if nx == 2:
        xr = [lax.ppermute(xs[0], "gx", [(0, 1), (1, 0)])]
        dr = [lax.ppermute(ds[0], ("gx", "gy"), [(0, 3), (3, 0), (1, 2), (2, 1)])]
    else:
        hops = [[(i, i + hop) for i in range(nx) if 0 <= i + hop < nx] for hop in (1, -1)]
        xr = [lax.ppermute(x, "gx", pairs) for x, pairs in zip(xs, hops)]
        crossed = [[(i * 2 + s, j * 2 + 1 - s) for i, j in pairs for s in range(2)] for pairs in hops]
        dr = [lax.ppermute(d, ("gx", "gy"), pairs) for d, pairs in zip(ds, crossed)]
    side = lax.ppermute(ys, "gy", [(0, 1), (1, 0)])
    pair = lax.ppermute(take(fields), "ta", ring)
    z = prepare(fields, matrix, side)
    halos = lax.ppermute(bundle(side, z, xr, dr), "ta", ring)
    relaxed, residual, coeffs, kept = own(c, xr, dr, side, z, matrix)
    return received(n, pair, halos, fields, coeffs, kept, matrix, relaxed, residual)


def solution(mesh):
    return jax.shard_map(
        local,
        mesh=mesh,
        in_specs=(
            P(("grp", "ta"), "gx", "gy"),
            P(("grp", "gx"), "gy"),
            P(("grp", "gx"), "gy"),
            P(("grp", "gx"), "gy"),
        ),
        out_specs=(P(("grp", "ta"), "gx", "gy"), P(("grp", "ta"), "gx", "gy")),
        check_vma=False,
    )
```

```python
import functools

import jax
import jax.numpy as jnp
from jax import lax
from jax.experimental import pallas as pl
from jax.experimental.pallas import tpu as pltpu
from jax.sharding import PartitionSpec as P

FACTOR = 4
HALO = 2 * FACTOR
LANES = 128
SUBLANES = 8
FOLDS = LANES // (2 * HALO)
FIELDS = 7
USED = (4, 5, 6, 0, 1, 2)

courant = 0.08

VMEM = pl.BlockSpec(memory_space=pltpu.VMEM)
HBM = pl.BlockSpec(memory_space=pltpu.HBM)
ANY = pl.BlockSpec(memory_space=pl.ANY)
F32 = jnp.float32
BF16 = jnp.bfloat16


def lane_index(shape):
    return lax.broadcasted_iota(jnp.int32, shape, len(shape) - 1)


def order(cols):
    blocks = cols // LANES
    place = lax.broadcasted_iota(jnp.int32, (cols, cols), 0)
    to = (place % blocks) * LANES + place // blocks
    return jnp.where(lane_index((cols, cols)) == to, 1.0, 0.0).astype(BF16)


def permuted(x, matrix):
    high = x.astype(BF16)
    rest = x - high.astype(F32)
    middle = rest.astype(BF16)
    low = (rest - middle.astype(F32)).astype(BF16)
    product = functools.partial(jnp.dot, preferred_element_type=F32)
    return product(high, matrix) + (product(middle, matrix) + product(low, matrix))


def restored(x, matrix):
    high = x.astype(BF16)
    low = (x - high.astype(F32)).astype(BF16)
    dims = (((1,), (1,)), ((), ()))
    product = functools.partial(lax.dot_general, dimension_numbers=dims, preferred_element_type=F32)
    return product(high, matrix) + product(low, matrix)


def start(copies):
    for copy in copies:
        copy.start()


def wait(copies):
    for copy in copies:
        copy.wait()


def place():
    return lax.axis_index("gx"), lax.axis_index("gy")


def edge_column(cols, gy):
    return pl.multiple_of((1 - gy) * (cols - LANES), LANES)


def first_row(ends, e, rows, gx):
    if len(ends) == 1:
        return pl.multiple_of((1 - gx) * (rows - HALO), HALO)
    return ends[e] * (rows - HALO)


def pack_kernel(ends, c, fixed, *refs):
    n = len(ends)
    xs, ds, (ys, matrix) = refs[:n], refs[n : 2 * n], refs[2 * n :]
    rows, cols = fixed.shape[1:]
    gx, gy = place()
    fields = [*[c.at[f] for f in range(4)], *[fixed.at[i] for i in range(3)]]
    lane = lane_index((rows, LANES))
    packed = jnp.zeros((rows, LANES), F32)
    for f, field in enumerate(fields):
        for e, x in enumerate(xs):
            x[f] = field[pl.ds(first_row(ends, e, rows, gx), HALO), :]
        moved = pltpu.roll(field[:, pl.ds(edge_column(cols, gy), LANES)], f * HALO + HALO * (1 - gy), 1)
        packed = jnp.where((lane >= f * HALO) & (lane < (f + 1) * HALO), moved, packed)
    ys[...] = packed
    for e, d in enumerate(ds):
        d[...] = ys[pl.ds(first_row(ends, e, rows, gx), HALO), :]
    matrix[...] = order(cols)


def pack(ends, c, fixed):
    rows, cols = fixed.shape[1:]
    n = len(ends)
    return pl.pallas_call(
        functools.partial(pack_kernel, ends),
        out_shape=(
            *[jax.ShapeDtypeStruct((FIELDS, HALO, cols), F32)] * n,
            *[jax.ShapeDtypeStruct((HALO, LANES), F32)] * n,
            jax.ShapeDtypeStruct((rows, LANES), F32),
            jax.ShapeDtypeStruct((cols, cols), BF16),
        ),
        in_specs=[VMEM] * 2,
        out_specs=(VMEM,) * (2 * n + 2),
        compiler_params=pltpu.CompilerParams(vmem_limit_bytes=16 << 20),
        name="pack",
    )(c, fixed)


def take_kernel(c, dif, dx, dy, pair, fixed, sems):
    copies = [pltpu.make_async_copy(c.at[pl.ds(2, 2)], pair, sems.at[3])]
    copies += [pltpu.make_async_copy(ref, fixed.at[i], sems.at[i]) for i, ref in enumerate((dif, dx, dy))]
    start(copies)
    wait(copies)


def take(c, dif, dx, dy):
    return pl.pallas_call(
        take_kernel,
        out_shape=[jax.ShapeDtypeStruct((count, *dif.shape), F32) for count in (2, 3)],
        in_specs=[HBM] * 4,
        out_specs=[VMEM] * 2,
        scratch_shapes=[pltpu.SemaphoreType.DMA((4,))],
        compiler_params=pltpu.CompilerParams(vmem_limit_bytes=4 << 20),
        name="take",
    )(*[pltpu.with_memory_space_constraint(x, pltpu.HBM) for x in (c, dif, dx, dy)])


def bundle_kernel(n, side, z, *refs):
    del z
    xr, dr, out = refs[:n], refs[n : 2 * n], refs[2 * n]
    cols = xr[0].shape[2]
    fold = side.shape[0] // FOLDS
    lane = lane_index((fold, LANES))
    folded = jnp.zeros((fold, LANES), F32)
    for j in range(FOLDS):
        begin = 2 * HALO * j
        moved = pltpu.roll(side[pl.ds(j * fold, fold), :], (begin - 2 * HALO) % LANES, 1)
        folded = jnp.where((lane >= begin) & (lane < begin + 2 * HALO), moved, folded)
    out[pl.ds(0, fold)] = folded
    at = fold
    for x, d in zip(xr, dr):
        out[pl.ds(at, HALO)] = d[...]
        at += HALO
        for f in (2, 3):
            for k in range(cols // LANES):
                out[pl.ds(at, HALO)] = x[f, :, pl.ds(k * LANES, LANES)]
                at += HALO


def bundle(side, z, xr, dr):
    n = len(xr)
    height = side.shape[0] // FOLDS + n * HALO * (1 + 2 * (xr[0].shape[2] // LANES))
    return pl.pallas_call(
        functools.partial(bundle_kernel, n),
        out_shape=jax.ShapeDtypeStruct((height, LANES), F32),
        in_specs=[VMEM, ANY] + [VMEM] * (2 * n),
        out_specs=VMEM,
        compiler_params=pltpu.CompilerParams(vmem_limit_bytes=4 << 20),
        name="bundle",
    )(side, z, *xr, *dr)


def put_columns(z, begin, value):
    rows, cols = value.shape
    for k in range(cols // LANES):
        z[k, pl.ds(begin, rows)] = value[:, k * LANES : (k + 1) * LANES]


def own_edge(block, gy):
    return pltpu.roll(block, (1 - gy) * (LANES - 1), 1)


def with_halo(block, packed, f, gy):
    return inserted(block, moved_to_halo(packed, f * HALO, gy), gy)


def moved_to_halo(value, lane, gy):
    return pltpu.roll(value, (halo_lane(gy) - lane) % LANES, 1)


def halo_lane(gy):
    return (1 - gy) * (LANES - 1) + gy * (LANES - HALO)


def inserted(block, moved, gy):
    return jnp.where((lane_index(block.shape) - halo_lane(gy)) % LANES < HALO, moved, block)


def fills(n, rows, gx):
    if n == 1:
        return [(rows, None, 0)]
    return [(rows, gx < lax.axis_size("gx") - 1, 1), (rows + HALO, gx > 0, 0)]


def masked(there, value):
    return value if there is None else jnp.where(there, value, 0.0)


def prepare_kernel(c, fixed, matrix, z):
    _, gy = place()
    rows, cols = fixed.shape[1:]
    fields = [*[c.at[f] for f in range(4)], *[fixed.at[i] for i in range(3)]]
    column = pl.ds(edge_column(cols, gy), LANES)
    scales = [1.0 if f == 4 else courant for f in USED]
    for i in range(0, len(USED), 2):
        pair = [fields[USED[i + m]][...] * scales[i + m] for m in range(2)]
        y = permuted(jnp.concatenate(pair, axis=0), matrix[...])
        for m in range(2):
            put_columns(z.at[i + m], 0, y[m * rows : (m + 1) * rows])
            z[i + m, cols // LANES] = own_edge(fields[USED[i + m]][:, column], gy) * scales[i + m]


def prepare(c, fixed, matrix):
    rows, cols = fixed.shape[1:]
    n = len(USED)
    return pl.pallas_call(
        prepare_kernel,
        out_shape=jax.ShapeDtypeStruct((n, cols // LANES + 1, rows, LANES), F32),
        in_specs=[VMEM] * 3,
        out_specs=VMEM,
        compiler_params=pltpu.CompilerParams(vmem_limit_bytes=24 << 20),
        cost_estimate=pl.CostEstimate(flops=100 * n * rows * cols, bytes_accessed=6 << 20, transcendentals=0),
        name="prepare",
    )(c, fixed, matrix)


def to_strided(z, w):
    count = w.shape[0]
    for r in range(count):
        for k in range(w.shape[1]):
            w[r, k] = z[k, pl.ds(r, SUBLANES, stride=count), :]


def from_strided(z, w):
    count = w.shape[0]
    for r in range(count):
        for k in range(z.shape[0]):
            z[k, pl.ds(r, SUBLANES, stride=count), :] = w[r, k] * (1.0 / courant)


def finish(ws, targets, matrix, zs, outs, sems):
    rows = outs.shape[1]
    flat = []
    for i, w in enumerate(ws):
        from_strided(zs.at[i], w)
        flat.append(jnp.concatenate([zs[i, k, pl.ds(0, rows)] for k in range(zs.shape[1])], axis=1))
    values = restored(jnp.concatenate(flat, axis=0), matrix[...])
    copies = []
    for i, target in enumerate(targets):
        outs[i] = values[i * rows : (i + 1) * rows]
        copies.append(pltpu.make_async_copy(outs.at[i], target, sems.at[i]))
    start(copies)
    return copies


def step(rows, gx, gy, w, coeffs):
    count, vectors = w.shape[:2]
    blocks = vectors - 1
    lane, sublane = lane_index(w.shape[2:]), lax.broadcasted_iota(jnp.int32, w.shape[2:], 0)
    at_left, at_right = lane == 0, lane == LANES - 1
    on_right = gy == 1
    cut = lax.axis_size("gx") == 2
    last_sublane, last_row = divmod(rows - 1, count)
    assert last_row < count - 1
    none_above = sublane == jnp.where(gx == 0, 0, -1)
    none_below = sublane == jnp.where(gx == 1, last_sublane, -1)
    initial = [w[0, k] for k in range(vectors)]
    field = initial
    above = [pltpu.roll(w[count - 1, k], 1, 0) for k in range(vectors)]
    if cut:
        above = [jnp.where(none_above, 0.0, value) for value in above]
    before = [field[k] - above[k] for k in range(vectors)]
    for r in range(count):
        if r < count - 1:
            following = [w[r + 1, k] for k in range(vectors)]
        else:
            following = [pltpu.roll(value, SUBLANES - 1, 0) for value in initial]
        below = following
        if cut and r == last_row:
            below = [jnp.where(none_below, 0.0, value) for value in following]
        after = [below[k] - field[k] for k in range(vectors)]
        edge = field[blocks] - pltpu.roll(field[blocks], 1, 1)
        begin = jnp.where(on_right, edge, field[0])
        end = jnp.where(on_right, -field[blocks - 1], edge)
        left = [jnp.where(at_left, begin, field[0] - pltpu.roll(field[blocks - 1], 1, 1))]
        left += [field[k] - field[k - 1] for k in range(1, blocks)]
        right = left[1:]
        right.append(jnp.where(at_right, end, pltpu.roll(field[0], LANES - 1, 1) - field[blocks - 1]))
        left.append(edge)
        right.append(pltpu.roll(edge, LANES - 1, 1))
        for k in range(vectors):
            speed_x = coeffs[1, r, k] + field[k]
            speed_y = coeffs[2, r, k] + field[k]
            laplace = (after[k] - before[k]) + (right[k] - left[k])
            upwind_x = jnp.where(speed_x > 0.0, before[k], after[k])
            upwind_y = jnp.where(speed_y > 0.0, left[k], right[k])
            w[r, k] = field[k] + coeffs[0, r, k] * laplace - speed_x * upwind_x - speed_y * upwind_y
        field, before = following, after


def propagate(rows, gx, gy, w, coeffs):
    def body(count, carry):
        step(rows, gx, gy, w, coeffs)
        return carry

    lax.fori_loop(0, FACTOR, body, 0)


def layout(n, rows, cols):
    height = rows + n * HALO
    return height, (height // SUBLANES, cols // LANES + 1, SUBLANES, LANES)


def own_kernel(n, *refs):
    xr, dr, (side, z_in, matrix), refs = refs[:n], refs[n : 2 * n], refs[2 * n : 2 * n + 3], refs[2 * n + 3 :]
    coeffs, once, difference, relaxed, z, ws, zs, outs, sems = refs
    rows, cols = z_in.shape[2], matrix.shape[0]
    blocks = cols // LANES
    gx, gy = place()
    scale = [1.0 if f == 4 else courant for f in USED]
    halo_rows = [
        permuted(jnp.concatenate([x[f] * s for f, s in zip(USED, scale)], axis=0), matrix[...]) for x in xr
    ]
    for i, f in enumerate(USED):
        z[i, pl.ds(0, blocks), pl.ds(0, rows)] = z_in[i, pl.ds(0, blocks)]
        z[i, blocks, pl.ds(0, rows)] = with_halo(z_in[i, blocks], side[...] * scale[i], f, gy)
        for begin, there, which in fills(n, rows, gx):
            y = halo_rows[which][i * HALO : (i + 1) * HALO]
            put_columns(z.at[i], begin, masked(there, y))
            block = own_edge(xr[which][f, :, pl.ds(edge_column(cols, gy), LANES)], gy)
            z[i, blocks, pl.ds(begin, HALO)] = masked(there, with_halo(block, dr[which][...], f, gy) * scale[i])
    for i in range(3):
        to_strided(z.at[i], coeffs.at[i])

    def body(m, carry):
        to_strided(z.at[3 + m], ws.at[m])
        propagate(rows, gx, gy, ws.at[m], coeffs)
        once[m] = ws[m, :, pl.ds(0, blocks)]
        return carry

    lax.fori_loop(0, 3, body, 0)
    targets = [relaxed.at[m + 1] for m in range(3)]
    written = finish([once.at[m] for m in range(3)], targets, matrix, zs, outs, sems)

    def body_again(m, carry):
        propagate(rows, gx, gy, ws.at[m], coeffs)
        difference[m] = ws[m, :, pl.ds(0, blocks)] - once[m + 1]
        return carry

    lax.fori_loop(0, 2, body_again, 0)
    wait(written)


def own(xr, dr, side, z, matrix):
    n, (rows, cols) = len(xr), (z.shape[2], matrix.shape[0])
    height, strided = layout(n, rows, cols)
    body = (strided[0], strided[1] - 1, *strided[2:])
    return pl.pallas_call(
        functools.partial(own_kernel, n),
        out_shape=(
            jax.ShapeDtypeStruct((3, *strided), F32),
            jax.ShapeDtypeStruct((3, *body), F32),
            jax.ShapeDtypeStruct((2, *body), F32),
            jax.ShapeDtypeStruct((4, rows, cols), F32),
        ),
        in_specs=[VMEM] * (2 * n + 3),
        out_specs=(VMEM, VMEM, VMEM, HBM),
        scratch_shapes=[
            pltpu.VMEM((len(USED), strided[1], height, LANES), F32),
            pltpu.VMEM((3, *strided), F32),
            pltpu.VMEM((3, strided[1] - 1, height, LANES), F32),
            pltpu.VMEM((3, rows, cols), F32),
            pltpu.SemaphoreType.DMA((3,)),
        ],
        compiler_params=pltpu.CompilerParams(vmem_limit_bytes=24 << 20),
        cost_estimate=pl.CostEstimate(flops=2000 * rows * cols, bytes_accessed=30 << 20, transcendentals=0),
        name="own",
    )(*xr, *dr, side, z, matrix)


def received_kernel(n, pair, halos, c, coeffs, once, difference, matrix, relaxed_in, *refs):
    relaxed, residual, z, ws, late, zs, outs, sems = refs
    del relaxed_in
    rows, cols = pair.shape[1:]
    blocks, height = cols // LANES, z.shape[2]
    first = lax.axis_index("ta") == 0
    gx, gy = place()
    sources = [difference.at[m] for m in range(2)]
    targets = [residual.at[m + 2] for m in range(2)]
    count = len(sources)
    written = finish(sources, targets, matrix, zs, outs, sems)
    targets = [relaxed.at[0], residual.at[0], residual.at[1]]
    late_outs, late_sems = outs.at[pl.ds(count, 3)], sems.at[pl.ds(count, 3)]

    @pl.when(first)
    def _():
        late_outs[0] = c[0]
        late_outs[1] = jnp.zeros_like(late_outs[1])
        values = [late_outs.at[0], late_outs.at[1], late_outs.at[1]]
        copies = [pltpu.make_async_copy(*ends, late_sems.at[i]) for i, ends in enumerate(zip(values, targets))]
        start(copies)
        wait(copies)

    @pl.when(jnp.logical_not(first))
    def _():
        at = fold = rows // FOLDS
        folded = halos[pl.ds(0, fold)]
        corners, parts = [], []
        for e in range(n):
            corners.append(halos[pl.ds(at, HALO)])
            at += HALO
            parts.append([])
            for m in range(2):
                line = [halos[pl.ds(at + k * HALO, HALO)] for k in range(blocks)]
                parts[e].append(jnp.concatenate(line, axis=1))
                at += blocks * HALO
        places = fills(n, rows, gx)
        x = []
        for m in range(2):
            x += [pair[m]] + [masked(there, parts[which][m]) for _, there, which in places]
        y = permuted(jnp.concatenate(x, axis=0) * courant, matrix[...])
        for m in range(2):
            put_columns(z.at[m], 0, y[m * height : (m + 1) * height])
            block = [pair[m, :, pl.ds(edge_column(cols, gy), LANES)]]
            for _, there, which in places:
                left, right = parts[which][m][:, :LANES], parts[which][m][:, cols - LANES :]
                block.append(masked(there, jnp.where(gy == 0, right, left)))
            block = own_edge(jnp.concatenate(block, axis=0), gy)
            moved = [moved_to_halo(folded, (2 * j + m) * HALO, gy) for j in range(FOLDS)]
            for _, there, which in places:
                moved.append(masked(there, moved_to_halo(corners[which], (2 + m) * HALO, gy)))
            z[m, blocks] = inserted(block, jnp.concatenate(moved, axis=0), gy) * courant

        def body(m, carry):
            to_strided(z.at[m], ws.at[m])
            propagate(rows, gx, gy, ws.at[m], coeffs)
            return carry

        lax.fori_loop(0, 2, body, 0)
        body_part = pl.ds(0, blocks)
        late[0] = ws[1, :, body_part]

        def body_again(m, carry):
            propagate(rows, gx, gy, ws.at[m], coeffs)
            return carry

        lax.fori_loop(0, 2, body_again, 0)
        late[1] = ws[0, :, body_part] - late[0]
        late[2] = ws[1, :, body_part] - once[0]
        wait(finish([late.at[m] for m in range(3)], targets, matrix, zs, late_outs, late_sems))

    wait(written)


def received(n, pair, halos, c, coeffs, once, difference, matrix, relaxed):
    rows, cols = pair.shape[1:]
    blocks = cols // LANES
    height, strided = layout(n, rows, cols)
    shape = jax.ShapeDtypeStruct((4, rows, cols), F32)
    return pl.pallas_call(
        functools.partial(received_kernel, n),
        out_shape=(shape, shape),
        in_specs=[VMEM] * 7 + [HBM],
        out_specs=(HBM, HBM),
        input_output_aliases={7: 0},
        scratch_shapes=[
            pltpu.VMEM((2, blocks + 1, height, LANES), F32),
            pltpu.VMEM((2, *strided), F32),
            pltpu.VMEM((3, *once.shape[1:]), F32),
            pltpu.VMEM((3, blocks, height, LANES), F32),
            pltpu.VMEM((5, rows, cols), F32),
            pltpu.SemaphoreType.DMA((5,)),
        ],
        compiler_params=pltpu.CompilerParams(vmem_limit_bytes=24 << 20),
        cost_estimate=pl.CostEstimate(flops=1600 * rows * cols, bytes_accessed=24 << 20, transcendentals=0),
        name="received",
    )(pair, halos, c, coeffs, once, difference, matrix, relaxed)


def local(c, dif, dx, dy):
    groups, nx, ny = (lax.axis_size(name) for name in ("ta", "gx", "gy"))
    rows, cols = dif.shape
    assert ny == 2 and c.shape[0] == 4 and rows % SUBLANES == 0 and cols % LANES == 0
    ends = (1,) if nx == 2 else (1, 0)
    ring = [(i, (i + 1) % groups) for i in range(groups)]
    n = len(ends)
    pair, fixed = take(c, dif, dx, dy)
    *sent, ys, matrix = pack(ends, c, fixed)
    xs, ds = sent[:n], sent[n:]
    if nx == 2:
        xr = [lax.ppermute(xs[0], "gx", [(0, 1), (1, 0)])]
        dr = [lax.ppermute(ds[0], ("gx", "gy"), [(0, 3), (3, 0), (1, 2), (2, 1)])]
    else:
        hops = [[(i, i + hop) for i in range(nx) if 0 <= i + hop < nx] for hop in (1, -1)]
        xr = [lax.ppermute(x, "gx", pairs) for x, pairs in zip(xs, hops)]
        crossed = [[(i * 2 + s, j * 2 + 1 - s) for i, j in pairs for s in range(2)] for pairs in hops]
        dr = [lax.ppermute(d, ("gx", "gy"), pairs) for d, pairs in zip(ds, crossed)]
    side = lax.ppermute(ys, "gy", [(0, 1), (1, 0)])
    pair = lax.ppermute(pair, "ta", ring)
    z = prepare(c, fixed, matrix)
    halos = lax.ppermute(bundle(side, z, xr, dr), "ta", ring)
    coeffs, once, difference, relaxed = own(xr, dr, side, z, matrix)
    return received(n, pair, halos, c, coeffs, once, difference, matrix, relaxed)


def solution(mesh):
    return jax.shard_map(
        local,
        mesh=mesh,
        in_specs=(
            P(("grp", "ta"), "gx", "gy"),
            P(("grp", "gx"), "gy"),
            P(("grp", "gx"), "gy"),
            P(("grp", "gx"), "gy"),
        ),
        out_specs=(P(("grp", "ta"), "gx", "gy"), P(("grp", "ta"), "gx", "gy")),
        check_vma=False,
    )
```

```python
import functools

import jax
import jax.numpy as jnp
from jax import lax
from jax.experimental import pallas as pl
from jax.experimental.pallas import tpu as pltpu
from jax.sharding import PartitionSpec as P

FACTOR = 4
HALO = 2 * FACTOR
LANES = 128
SUBLANES = 8
SLOT = 2 * HALO
FOLDS = LANES // (2 * SLOT)
FIELDS = 7
USED = (4, 5, 6, 0, 1, 2)

courant = 0.08

VMEM = pl.BlockSpec(memory_space=pltpu.VMEM)
HBM = pl.BlockSpec(memory_space=pltpu.HBM)
F32 = jnp.float32
BF16 = jnp.bfloat16


def lane_index(shape):
    return lax.broadcasted_iota(jnp.int32, shape, len(shape) - 1)


def order(cols):
    blocks = cols // LANES
    place = lax.broadcasted_iota(jnp.int32, (cols, cols), 0)
    to = (place % blocks) * LANES + place // blocks
    return jnp.where(lane_index((cols, cols)) == to, 1.0, 0.0).astype(BF16)


def permuted(x, matrix):
    high = x.astype(BF16)
    rest = x - high.astype(F32)
    middle = rest.astype(BF16)
    low = (rest - middle.astype(F32)).astype(BF16)
    product = functools.partial(jnp.dot, preferred_element_type=F32)
    return product(high, matrix) + (product(middle, matrix) + product(low, matrix))


def restored(x, matrix):
    high = x.astype(BF16)
    low = (x - high.astype(F32)).astype(BF16)
    dims = (((1,), (1,)), ((), ()))
    product = functools.partial(lax.dot_general, dimension_numbers=dims, preferred_element_type=F32)
    return product(high, matrix) + product(low, matrix)


def start(copies):
    for copy in copies:
        copy.start()


def wait(copies):
    for copy in copies:
        copy.wait()


def place():
    return lax.axis_index("gx"), lax.axis_index("gy")


def edge_column(cols, gy):
    return pl.multiple_of((1 - gy) * (cols - LANES), LANES)


def first_row(ends, e, rows, gx):
    if len(ends) == 1:
        return pl.multiple_of((1 - gx) * (rows - HALO), HALO)
    return ends[e] * (rows - HALO)


def edges(blocks):
    lane = lane_index(blocks[0].shape)
    packed = jnp.zeros(lane.shape, F32)
    for slot, block in enumerate(blocks):
        begin = slot * SLOT
        packed = jnp.where((lane >= begin) & (lane < begin + SLOT), pltpu.roll(block, begin + HALO, 1), packed)
    return packed


def both_sides(own, other, gy):
    return jnp.where(lane_index(own.shape) // HALO % 2 == gy, own, other)


def aligned(value, slots, gy):
    return pltpu.roll(value, (gy - 1 - HALO - slots * SLOT) % LANES, 1)


def fixed_edges(value, gy):
    lane = (lane_index(value.shape) + HALO + 1 - gy) % LANES
    picked = []
    for i in range(4, FIELDS):
        twice = jnp.where(lane < SLOT, aligned(value, i, gy), aligned(value, i - 1, gy))
        picked.append(jnp.where(lane < 2 * SLOT, twice, 0.0))
    return [picked[0], picked[1] * courant, picked[2] * courant]


def state_edges(value, gy):
    return [aligned(value, 2 * i, gy) * courant for i in range(2)]


def pack_kernel(ends, fields, *refs):
    n = len(ends)
    xs, ds, (ys, matrix) = refs[:n], refs[n : 2 * n], refs[2 * n :]
    rows, cols = fields.shape[1:]
    gx, gy = place()
    for e, x in enumerate(xs):
        x[...] = fields[:, pl.ds(first_row(ends, e, rows, gx), HALO), :]
    ys[...] = edges([fields[f, :, pl.ds(edge_column(cols, gy), LANES)] for f in range(FIELDS)])
    for e, d in enumerate(ds):
        d[...] = ys[pl.ds(first_row(ends, e, rows, gx), HALO), :]
    matrix[...] = order(cols)


def pack(ends, fields):
    rows, cols = fields.shape[1:]
    n = len(ends)
    return pl.pallas_call(
        functools.partial(pack_kernel, ends),
        out_shape=(
            *[jax.ShapeDtypeStruct((FIELDS, HALO, cols), F32)] * n,
            *[jax.ShapeDtypeStruct((HALO, LANES), F32)] * n,
            jax.ShapeDtypeStruct((rows, LANES), F32),
            jax.ShapeDtypeStruct((cols, cols), BF16),
        ),
        in_specs=[VMEM],
        out_specs=(VMEM,) * (2 * n + 2),
        compiler_params=pltpu.CompilerParams(vmem_limit_bytes=16 << 20),
        name="pack",
    )(fields)


def take_kernel(c, dif, dx, dy, pair, fields, sems):
    copies = [
        pltpu.make_async_copy(c.at[pl.ds(2, 2)], fields.at[pl.ds(2, 2)], sems.at[0]),
        pltpu.make_async_copy(c.at[pl.ds(0, 2)], fields.at[pl.ds(0, 2)], sems.at[1]),
    ]
    copies += [pltpu.make_async_copy(ref, fields.at[4 + i], sems.at[2 + i]) for i, ref in enumerate((dif, dx, dy))]
    start(copies)
    wait(copies[:1])
    pair[...] = fields[pl.ds(2, 2)]
    wait(copies[1:])


def take(c, dif, dx, dy):
    return pl.pallas_call(
        take_kernel,
        out_shape=[jax.ShapeDtypeStruct((count, *dif.shape), F32) for count in (2, FIELDS)],
        in_specs=[HBM] * 4,
        out_specs=[VMEM] * 2,
        scratch_shapes=[pltpu.SemaphoreType.DMA((5,))],
        compiler_params=pltpu.CompilerParams(vmem_limit_bytes=4 << 20),
        name="take",
    )(*[pltpu.with_memory_space_constraint(x, pltpu.HBM) for x in (c, dif, dx, dy)])


def bundle_kernel(n, folded, corners, rows, out):
    at = folded.shape[0]
    out[pl.ds(0, at)] = folded[...]
    for e in range(n):
        out[pl.ds(at, HALO)] = corners[e]
        at += HALO
        for k in range(rows.shape[2] // LANES):
            out[pl.ds(at, 2 * HALO)] = rows[e, :, pl.ds(k * LANES, LANES)]
            at += 2 * HALO


def bundle(folded, corners, rows):
    n = len(corners)
    height = folded.shape[0] + n * HALO * (1 + 2 * (rows.shape[2] // LANES))
    return pl.pallas_call(
        functools.partial(bundle_kernel, n),
        out_shape=jax.ShapeDtypeStruct((height, LANES), F32),
        in_specs=[VMEM] * 3,
        out_specs=VMEM,
        compiler_params=pltpu.CompilerParams(vmem_limit_bytes=4 << 20),
        name="bundle",
    )(folded, corners, rows)


def put_columns(z, begin, value):
    rows, cols = value.shape
    for k in range(cols // LANES):
        z[k, pl.ds(begin, rows)] = value[:, k * LANES : (k + 1) * LANES]


def fills(n, rows, gx):
    if n == 1:
        return [(rows, None, 0)]
    return [(rows, gx < lax.axis_size("gx") - 1, 1), (rows + HALO, gx > 0, 0)]


def masked(there, value):
    return value if there is None else jnp.where(there, value, 0.0)


def layout(n, rows, cols):
    height = rows + n * HALO
    count = height // SUBLANES
    assert (SUBLANES - 1) * count <= rows and rows % (SUBLANES * FOLDS) == 0
    return height, (count, cols // LANES, SUBLANES, LANES), (count, SUBLANES, LANES)


def to_strided(z, w):
    count = w.shape[0]
    for r in range(count):
        for k in range(w.shape[1]):
            w[r, k] = z[k, pl.ds(r, SUBLANES, stride=count), :]


def prepare_kernel(fields, matrix, ys, side, bodies, edge, folded, z, t):
    _, gy = place()
    rows = fields.shape[1]
    count = edge.shape[1]
    scales = [1.0 if f == 4 else courant for f in USED]
    for i in range(0, len(USED), 2):
        pair = [fields[USED[i + m]] * scales[i + m] for m in range(2)]
        y = permuted(jnp.concatenate(pair, axis=0), matrix[...])
        for m in range(2):
            put_columns(z.at[i + m], 0, y[m * rows : (m + 1) * rows])
            to_strided(z.at[i + m], bodies.at[i + m])
    t[pl.ds(0, rows)] = both_sides(ys[...], side[...], gy)
    for r in range(count):
        value = t[pl.ds(r, SUBLANES, stride=count), :]
        for i, picked in enumerate(fixed_edges(value, gy) + state_edges(value, gy)):
            edge[i, r] = picked
    height = rows // FOLDS
    lane = lane_index((height, LANES))
    value = jnp.zeros((height, LANES), F32)
    for j in range(FOLDS):
        begin = 2 * SLOT * j
        moved = pltpu.roll(t[pl.ds(j * height, height), :], (begin - 2 * SLOT) % LANES, 1)
        value = jnp.where((lane >= begin) & (lane < begin + 2 * SLOT), moved, value)
    folded[...] = value


def prepare(n, fields, matrix, ys, side):
    rows, cols = fields.shape[1:]
    height, body, edge = layout(n, rows, cols)
    return pl.pallas_call(
        prepare_kernel,
        out_shape=(
            jax.ShapeDtypeStruct((len(USED), *body), F32),
            jax.ShapeDtypeStruct((5, *edge), F32),
            jax.ShapeDtypeStruct((rows // FOLDS, LANES), F32),
        ),
        in_specs=[VMEM] * 4,
        out_specs=(VMEM,) * 3,
        scratch_shapes=[
            pltpu.VMEM((len(USED), cols // LANES, height, LANES), F32),
            pltpu.VMEM((height, LANES), F32),
        ],
        compiler_params=pltpu.CompilerParams(vmem_limit_bytes=24 << 20),
        cost_estimate=pl.CostEstimate(flops=100 * FIELDS * rows * cols, bytes_accessed=6 << 20, transcendentals=0),
        name="prepare",
    )(fields, matrix, ys, side)


def from_strided(z, w):
    count = w.shape[0]
    for r in range(count):
        for k in range(z.shape[0]):
            z[k, pl.ds(r, SUBLANES, stride=count), :] = w[r, k] * (1.0 / courant)


def finish(ws, targets, matrix, zs, outs, sems):
    rows = outs.shape[1]
    flat = []
    for i, w in enumerate(ws):
        from_strided(zs.at[i], w)
        flat.append(jnp.concatenate([zs[i, k, pl.ds(0, rows)] for k in range(zs.shape[1])], axis=1))
    values = restored(jnp.concatenate(flat, axis=0), matrix[...])
    copies = []
    for i, target in enumerate(targets):
        outs[i] = values[i * rows : (i + 1) * rows]
        copies.append(pltpu.make_async_copy(outs.at[i], target, sems.at[i]))
        copies[i].start()
    return copies


def update(field, before, after, left, right, diffusion, drift_x, drift_y):
    speed_x = drift_x + field
    speed_y = drift_y + field
    laplace = (after - before) + (right - left)
    upwind_x = jnp.where(speed_x > 0.0, before, after)
    upwind_y = jnp.where(speed_y > 0.0, left, right)
    return field + diffusion * laplace - speed_x * upwind_x - speed_y * upwind_y


def step(rows, gx, gy, ws, edge, fixed, fixed_edge):
    n, count, blocks = ws.shape[:3]
    shape = (SUBLANES, LANES)
    lane, sublane = lane_index(shape), lax.broadcasted_iota(jnp.int32, shape, 0)
    at_left, at_right = lane == 0, lane == LANES - 1
    on_right = gy == 1
    cut = lax.axis_size("gx") == 2
    last_sublane, last_row = divmod(rows - 1, count)
    assert last_row < count - 1
    none_above = sublane == jnp.where(gx == 0, 0, -1)
    none_below = sublane == jnp.where(gx == 1, last_sublane, -1)

    def row(r):
        return [ws[m, r, k] for m in range(n) for k in range(blocks)] + [edge[r]]

    initial = field = row(0)
    above = [pltpu.roll(value, 1, 0) for value in row(count - 1)]
    if cut:
        above = [jnp.where(none_above, 0.0, value) for value in above]
    before = [value - other for value, other in zip(field, above)]
    for r in range(count):
        following = row(r + 1) if r < count - 1 else [pltpu.roll(value, SUBLANES - 1, 0) for value in initial]
        below = following
        if cut and r == last_row:
            below = [jnp.where(none_below, 0.0, value) for value in following]
        after = [other - value for value, other in zip(field, below)]
        border = field[-1] - pltpu.roll(field[-1], 1, 1)
        around = (before[-1], after[-1], border, pltpu.roll(border, LANES - 1, 1))
        edge[r] = update(field[-1], *around, *[fixed_edge[i, r] for i in range(3)])
        for m in range(n):
            part = slice(m * blocks, (m + 1) * blocks)
            body, body_before, body_after = field[part], before[part], after[part]
            across = pltpu.roll(border, LANES - m * SLOT, 1) if m else border
            begin = jnp.where(on_right, across, body[0])
            end = jnp.where(on_right, -body[-1], across)
            left = [jnp.where(at_left, begin, body[0] - pltpu.roll(body[-1], 1, 1))]
            left += [body[k] - body[k - 1] for k in range(1, blocks)]
            right = left[1:]
            right.append(jnp.where(at_right, end, pltpu.roll(body[0], LANES - 1, 1) - body[-1]))
            for k in range(blocks):
                around = (body_before[k], body_after[k], left[k], right[k])
                ws[m, r, k] = update(body[k], *around, *[fixed[i, r, k] for i in range(3)])
        field, before = following, after


def propagate(rows, gx, gy, ws, edge, fixed, fixed_edge):
    def one(count, carry):
        step(rows, gx, gy, ws, edge, fixed, fixed_edge)
        return carry

    lax.fori_loop(0, FACTOR, one, 0)


def once_kernel(n, *refs):
    xr, dr, (bodies, edge, matrix), refs = refs[:n], refs[n : 2 * n], refs[2 * n : 2 * n + 3], refs[2 * n + 3 :]
    corners, sent, fixed, fixed_edge, once, e_pair, e_last = refs
    cols = matrix.shape[0]
    count, blocks = once.shape[1:3]
    rows = count * SUBLANES - n * HALO
    gx, gy = place()
    fixed[...] = bodies[pl.ds(0, 3)]
    once[...] = bodies[pl.ds(3, 3)]
    fixed_edge[...] = edge[pl.ds(0, 3)]
    e_pair[...] = edge[3]
    e_last[...] = edge[4]
    for x, d, corner in zip(xr, dr, [corners.at[e] for e in range(n)]):
        own = edges([x[f, :, pl.ds(edge_column(cols, gy), LANES)] for f in range(FIELDS)])
        corner[...] = both_sides(own, d[...], gy)
    targets = [*[fixed.at[i] for i in range(3)], *[once.at[m] for m in range(3)]]
    edge_targets = [*[fixed_edge.at[i] for i in range(3)], e_pair, e_last]
    in_place = slice(SUBLANES - 1, SUBLANES)
    converted = []
    for e, x in enumerate(xr):
        value = jnp.concatenate([x[f] * (1.0 if f == 4 else courant) for f in (*USED, 3)], axis=0)
        converted.append(permuted(value, matrix[...]))
        sent[e] = converted[e][(len(USED) - 1) * HALO :]
    for begin, there, which in fills(n, rows, gx):
        y = masked(there, converted[which])
        values = fixed_edges(corners[which], gy) + state_edges(corners[which], gy)
        for j in range(HALO):
            r = begin + j - (SUBLANES - 1) * count
            for i, target in enumerate(targets):
                for k in range(blocks):
                    at = i * HALO + j
                    target[r, k, in_place] = y[at : at + 1, k * LANES : (k + 1) * LANES]
            for target, value in zip(edge_targets, values):
                target[r, in_place] = masked(there, value[j : j + 1])

    propagate(rows, gx, gy, once.at[pl.ds(0, 2)], e_pair, fixed, fixed_edge)
    propagate(rows, gx, gy, once.at[pl.ds(2, 1)], e_last, fixed, fixed_edge)


def propagate_once(xr, dr, bodies, edge, matrix):
    n = len(xr)
    body, edge_shape = bodies.shape[1:], edge.shape[1:]
    return pl.pallas_call(
        functools.partial(once_kernel, n),
        out_shape=(
            jax.ShapeDtypeStruct((n, HALO, LANES), F32),
            jax.ShapeDtypeStruct((n, 2 * HALO, matrix.shape[0]), F32),
            jax.ShapeDtypeStruct((3, *body), F32),
            jax.ShapeDtypeStruct((3, *edge_shape), F32),
            jax.ShapeDtypeStruct((3, *body), F32),
            jax.ShapeDtypeStruct(edge_shape, F32),
        ),
        in_specs=[VMEM] * (2 * n + 3),
        out_specs=(VMEM,) * 6,
        scratch_shapes=[pltpu.VMEM(edge_shape, F32)],
        compiler_params=pltpu.CompilerParams(vmem_limit_bytes=16 << 20),
        cost_estimate=pl.CostEstimate(flops=0, bytes_accessed=12 << 20, transcendentals=0),
        name="once",
    )(*xr, *dr, bodies, edge, matrix)


def twice_kernel(n, fixed, fixed_edge, once, edge, matrix, relaxed, difference, ws, e_pair, zs, outs, sems):
    rows = outs.shape[1]
    gx, gy = place()
    written = finish([once.at[m] for m in range(3)], [relaxed.at[m + 1] for m in range(3)], matrix, zs, outs, sems)
    ws[...] = once[pl.ds(0, 2)]
    e_pair[...] = edge[...]
    propagate(rows, gx, gy, ws, e_pair, fixed, fixed_edge)
    difference[...] = ws[...] - once[pl.ds(1, 2)]
    wait(written)


def propagate_twice(n, fixed, fixed_edge, once, edge, matrix):
    body, edge_shape, cols = once.shape[1:], edge.shape, matrix.shape[0]
    height = body[0] * SUBLANES
    rows = height - n * HALO
    return pl.pallas_call(
        functools.partial(twice_kernel, n),
        out_shape=(jax.ShapeDtypeStruct((4, rows, cols), F32), jax.ShapeDtypeStruct((2, *body), F32)),
        in_specs=[VMEM] * 5,
        out_specs=(HBM, VMEM),
        scratch_shapes=[
            pltpu.VMEM((2, *body), F32),
            pltpu.VMEM(edge_shape, F32),
            pltpu.VMEM((3, body[1], height, LANES), F32),
            pltpu.VMEM((3, rows, cols), F32),
            pltpu.SemaphoreType.DMA((3,)),
        ],
        compiler_params=pltpu.CompilerParams(vmem_limit_bytes=16 << 20),
        cost_estimate=pl.CostEstimate(flops=0, bytes_accessed=10 << 20, transcendentals=0),
        name="twice",
    )(fixed, fixed_edge, once, edge, matrix)


def convert_kernel(pair, difference, matrix, bodies, residual, z, zs, outs, sems):
    rows = pair.shape[1]
    sources = [difference.at[m] for m in range(2)]
    written = finish(sources, [residual.at[m + 2] for m in range(2)], matrix, zs, outs, sems)
    y = permuted(jnp.concatenate([pair[m] for m in range(2)], axis=0) * courant, matrix[...])
    for m in range(2):
        put_columns(z.at[m], 0, y[m * rows : (m + 1) * rows])
        to_strided(z.at[m], bodies.at[m])
    wait(written)


def convert(pair, difference, matrix):
    rows, cols = pair.shape[1:]
    body = difference.shape[1:]
    height = body[0] * SUBLANES
    return pl.pallas_call(
        convert_kernel,
        out_shape=(jax.ShapeDtypeStruct((2, *body), F32), jax.ShapeDtypeStruct((4, rows, cols), F32)),
        in_specs=[VMEM] * 3,
        out_specs=(VMEM, HBM),
        scratch_shapes=[
            pltpu.VMEM((2, body[1], height, LANES), F32),
            pltpu.VMEM((2, body[1], height, LANES), F32),
            pltpu.VMEM((2, rows, cols), F32),
            pltpu.SemaphoreType.DMA((2,)),
        ],
        compiler_params=pltpu.CompilerParams(vmem_limit_bytes=16 << 20),
        cost_estimate=pl.CostEstimate(flops=0, bytes_accessed=4 << 20, transcendentals=0),
        name="convert",
    )(pair, difference, matrix)


def received_kernel(n, bodies, halos, fields, fixed, fixed_edge, once, matrix, relaxed_in, residual_in, *refs):
    relaxed, residual, t, ws, edge, late, zs, outs, sems = refs
    del relaxed_in, residual_in
    rows = fields.shape[1]
    count, blocks = ws.shape[1:3]
    first = lax.axis_index("ta") == 0
    gx, gy = place()
    targets = [relaxed.at[0], residual.at[0], residual.at[1]]

    @pl.when(first)
    def _():
        outs[0] = fields[0]
        outs[1] = jnp.zeros_like(outs[1])
        values = [outs.at[0], outs.at[1], outs.at[1]]
        copies = [pltpu.make_async_copy(*ends, sems.at[i]) for i, ends in enumerate(zip(values, targets))]
        start(copies)
        wait(copies)

    @pl.when(jnp.logical_not(first))
    def _():
        fold = rows // FOLDS
        folded = halos[pl.ds(0, fold)]
        for j in range(FOLDS):
            t[pl.ds(j * fold, fold)] = aligned(folded, 2 * j, gy) * courant
        ws[...] = bodies[...]
        in_place = slice(SUBLANES - 1, SUBLANES)
        for begin, there, which in fills(n, rows, gx):
            at = fold + which * HALO * (1 + 2 * blocks)
            t[pl.ds(begin, HALO)] = masked(there, aligned(halos[pl.ds(at, HALO)], 2, gy) * courant)
            at += HALO
            for k in range(blocks):
                value = masked(there, halos[pl.ds(at + k * 2 * HALO, 2 * HALO)])
                for m in range(2):
                    for j in range(HALO):
                        row = m * HALO + j
                        ws[m, begin + j - (SUBLANES - 1) * count, k, in_place] = value[row : row + 1]
        for r in range(count):
            edge[r] = t[pl.ds(r, SUBLANES, stride=count), :]
        propagate(rows, gx, gy, ws, edge, fixed, fixed_edge)
        late[0] = ws[1]
        propagate(rows, gx, gy, ws, edge, fixed, fixed_edge)
        late[1] = ws[0] - late[0]
        late[2] = ws[1] - once[0]
        wait(finish([late.at[m] for m in range(3)], targets, matrix, zs, outs, sems))


def received(n, bodies, halos, fields, fixed, fixed_edge, once, matrix, relaxed, residual):
    rows, cols = fields.shape[1:]
    height, body, edge = layout(n, rows, cols)
    shape = jax.ShapeDtypeStruct((4, rows, cols), F32)
    return pl.pallas_call(
        functools.partial(received_kernel, n),
        out_shape=(shape, shape),
        in_specs=[VMEM] * 7 + [HBM] * 2,
        out_specs=(HBM, HBM),
        scratch_shapes=[
            pltpu.VMEM((height, LANES), F32),
            pltpu.VMEM((2, *body), F32),
            pltpu.VMEM(edge, F32),
            pltpu.VMEM((3, *body), F32),
            pltpu.VMEM((3, body[1], height, LANES), F32),
            pltpu.VMEM((3, rows, cols), F32),
            pltpu.SemaphoreType.DMA((3,)),
        ],
        input_output_aliases={7: 0, 8: 1},
        compiler_params=pltpu.CompilerParams(vmem_limit_bytes=24 << 20),
        cost_estimate=pl.CostEstimate(flops=1600 * rows * cols, bytes_accessed=24 << 20, transcendentals=0),
        name="received",
    )(bodies, halos, fields, fixed, fixed_edge, once, matrix, relaxed, residual)


def local(c, dif, dx, dy):
    groups, nx, ny = (lax.axis_size(name) for name in ("ta", "gx", "gy"))
    rows, cols = dif.shape
    assert ny == 2 and c.shape[0] == 4 and rows % SUBLANES == 0 and cols % LANES == 0
    ends = (1,) if nx == 2 else (1, 0)
    n = len(ends)
    ring = [(i, (i + 1) % groups) for i in range(groups)]
    pair, fields = take(c, dif, dx, dy)
    pair = lax.ppermute(pair, "ta", ring)
    *sent, ys, matrix = pack(ends, fields)
    xs, ds = sent[:n], sent[n:]
    if nx == 2:
        xr = [lax.ppermute(xs[0], "gx", [(0, 1), (1, 0)])]
        dr = [lax.ppermute(ds[0], ("gx", "gy"), [(0, 3), (3, 0), (1, 2), (2, 1)])]
    else:
        hops = [[(i, i + hop) for i in range(nx) if 0 <= i + hop < nx] for hop in (1, -1)]
        xr = [lax.ppermute(x, "gx", pairs) for x, pairs in zip(xs, hops)]
        crossed = [[(i * 2 + s, j * 2 + 1 - s) for i, j in pairs for s in range(2)] for pairs in hops]
        dr = [lax.ppermute(d, ("gx", "gy"), pairs) for d, pairs in zip(ds, crossed)]
    side = lax.ppermute(ys, "gy", [(0, 1), (1, 0)])
    bodies, edge, folded = prepare(n, fields, matrix, ys, side)
    corners, sent, fixed, fixed_edge, once, edge = propagate_once(xr, dr, bodies, edge, matrix)
    halos = lax.ppermute(bundle(folded, corners, sent), "ta", ring)
    relaxed, difference = propagate_twice(n, fixed, fixed_edge, once, edge, matrix)
    bodies, residual = convert(pair, difference, matrix)
    return received(n, bodies, halos, fields, fixed, fixed_edge, once, matrix, relaxed, residual)


def solution(mesh):
    return jax.shard_map(
        local,
        mesh=mesh,
        in_specs=(
            P(("grp", "ta"), "gx", "gy"),
            P(("grp", "gx"), "gy"),
            P(("grp", "gx"), "gy"),
            P(("grp", "gx"), "gy"),
        ),
        out_specs=(P(("grp", "ta"), "gx", "gy"), P(("grp", "ta"), "gx", "gy")),
        check_vma=False,
    )
```

```python
import functools

import jax
import jax.numpy as jnp
from jax import lax
from jax.experimental import pallas as pl
from jax.experimental.pallas import tpu as pltpu
from jax.sharding import PartitionSpec as P

FACTOR = 4
HALO = 2 * FACTOR
LANES = 128
SUBLANES = 8
SLOT = 2 * HALO
FOLDS = LANES // (2 * SLOT)
FIELDS = 7
USED = (4, 5, 6, 0, 1, 2)

courant = 0.08

VMEM = pl.BlockSpec(memory_space=pltpu.VMEM)
HBM = pl.BlockSpec(memory_space=pltpu.HBM)
F32 = jnp.float32
BF16 = jnp.bfloat16


def lane_index(shape):
    return lax.broadcasted_iota(jnp.int32, shape, len(shape) - 1)


def order(cols):
    blocks = cols // LANES
    place = lax.broadcasted_iota(jnp.int32, (cols, cols), 0)
    to = (place % blocks) * LANES + place // blocks
    return jnp.where(lane_index((cols, cols)) == to, 1.0, 0.0).astype(BF16)


def permuted(x, matrix):
    high = x.astype(BF16)
    rest = x - high.astype(F32)
    middle = rest.astype(BF16)
    low = (rest - middle.astype(F32)).astype(BF16)
    product = functools.partial(jnp.dot, preferred_element_type=F32)
    return product(high, matrix) + (product(middle, matrix) + product(low, matrix))


def restored(x, matrix):
    high = x.astype(BF16)
    low = (x - high.astype(F32)).astype(BF16)
    dims = (((1,), (1,)), ((), ()))
    product = functools.partial(lax.dot_general, dimension_numbers=dims, preferred_element_type=F32)
    return product(high, matrix) + product(low, matrix)


def start(copies):
    for copy in copies:
        copy.start()


def wait(copies):
    for copy in copies:
        copy.wait()


def place():
    return lax.axis_index("gx"), lax.axis_index("gy")


def edge_column(cols, gy):
    return pl.multiple_of((1 - gy) * (cols - LANES), LANES)


def first_row(ends, e, rows, gx):
    if len(ends) == 1:
        return pl.multiple_of((1 - gx) * (rows - HALO), HALO)
    return ends[e] * (rows - HALO)


def edges(blocks):
    lane = lane_index(blocks[0].shape)
    packed = jnp.zeros(lane.shape, F32)
    for slot, block in enumerate(blocks):
        begin = slot * SLOT
        packed = jnp.where((lane >= begin) & (lane < begin + SLOT), pltpu.roll(block, begin + HALO, 1), packed)
    return packed


def both_sides(own, other, gy):
    return jnp.where(lane_index(own.shape) // HALO % 2 == gy, own, other)


def aligned(value, slots, gy):
    return pltpu.roll(value, (2 * gy - 1 - HALO - slots * SLOT) % LANES, 1)


def fixed_edges(value, gy):
    lane = (lane_index(value.shape) + HALO + 1 - 2 * gy) % LANES
    picked = []
    for i in range(4, FIELDS):
        twice = jnp.where(lane < SLOT, aligned(value, i, gy), aligned(value, i - 1, gy))
        picked.append(jnp.where(lane < 2 * SLOT, twice, 0.0))
    return [picked[0], picked[1] * courant, picked[2] * courant]


def state_edges(value, gy):
    return [aligned(value, 2 * i, gy) * courant for i in range(2)]


def pack_kernel(ends, fields, *refs):
    n = len(ends)
    xs, ds, (ys, matrix) = refs[:n], refs[n : 2 * n], refs[2 * n :]
    rows, cols = fields.shape[1:]
    gx, gy = place()
    for e, x in enumerate(xs):
        x[...] = fields[:, pl.ds(first_row(ends, e, rows, gx), HALO), :]
    ys[...] = edges([fields[f, :, pl.ds(edge_column(cols, gy), LANES)] for f in range(FIELDS)])
    for e, d in enumerate(ds):
        d[...] = ys[pl.ds(first_row(ends, e, rows, gx), HALO), :]
    matrix[...] = order(cols)


def pack(ends, fields):
    rows, cols = fields.shape[1:]
    n = len(ends)
    return pl.pallas_call(
        functools.partial(pack_kernel, ends),
        out_shape=(
            *[jax.ShapeDtypeStruct((FIELDS, HALO, cols), F32)] * n,
            *[jax.ShapeDtypeStruct((HALO, LANES), F32)] * n,
            jax.ShapeDtypeStruct((rows, LANES), F32),
            jax.ShapeDtypeStruct((cols, cols), BF16),
        ),
        in_specs=[VMEM],
        out_specs=(VMEM,) * (2 * n + 2),
        compiler_params=pltpu.CompilerParams(vmem_limit_bytes=16 << 20),
        name="pack",
    )(fields)


def take_kernel(c, dif, dx, dy, pair, fields, sems):
    copies = [
        pltpu.make_async_copy(c.at[pl.ds(2, 2)], fields.at[pl.ds(2, 2)], sems.at[0]),
        pltpu.make_async_copy(c.at[pl.ds(0, 2)], fields.at[pl.ds(0, 2)], sems.at[1]),
    ]
    copies += [pltpu.make_async_copy(ref, fields.at[4 + i], sems.at[2 + i]) for i, ref in enumerate((dif, dx, dy))]
    start(copies)
    wait(copies[:1])
    pair[...] = fields[pl.ds(2, 2)]
    wait(copies[1:])


def take(c, dif, dx, dy):
    return pl.pallas_call(
        take_kernel,
        out_shape=[jax.ShapeDtypeStruct((count, *dif.shape), F32) for count in (2, FIELDS)],
        in_specs=[HBM] * 4,
        out_specs=[VMEM] * 2,
        scratch_shapes=[pltpu.SemaphoreType.DMA((5,))],
        compiler_params=pltpu.CompilerParams(vmem_limit_bytes=4 << 20),
        name="take",
    )(*[pltpu.with_memory_space_constraint(x, pltpu.HBM) for x in (c, dif, dx, dy)])


def bundle_kernel(n, folded, corners, rows, out):
    at = folded.shape[0]
    out[pl.ds(0, at)] = folded[...]
    for e in range(n):
        out[pl.ds(at, HALO)] = corners[e]
        at += HALO
        for k in range(rows.shape[2] // LANES):
            out[pl.ds(at, 2 * HALO)] = rows[e, :, pl.ds(k * LANES, LANES)]
            at += 2 * HALO


def bundle(folded, corners, rows):
    n = len(corners)
    height = folded.shape[0] + n * HALO * (1 + 2 * (rows.shape[2] // LANES))
    return pl.pallas_call(
        functools.partial(bundle_kernel, n),
        out_shape=jax.ShapeDtypeStruct((height, LANES), F32),
        in_specs=[VMEM] * 3,
        out_specs=VMEM,
        compiler_params=pltpu.CompilerParams(vmem_limit_bytes=4 << 20),
        name="bundle",
    )(folded, corners, rows)


def put_columns(z, begin, value):
    rows, cols = value.shape
    for k in range(cols // LANES):
        z[k, pl.ds(begin, rows)] = value[:, k * LANES : (k + 1) * LANES]


def fills(n, rows, gx):
    if n == 1:
        return [(rows, None, 0)]
    return [(rows, gx < lax.axis_size("gx") - 1, 1), (rows + HALO, gx > 0, 0)]


def masked(there, value):
    return value if there is None else jnp.where(there, value, 0.0)


def layout(n, rows, cols):
    height = rows + n * HALO
    count = height // SUBLANES
    assert (SUBLANES - 1) * count <= rows and rows % (SUBLANES * FOLDS) == 0
    return height, (count, cols // LANES, SUBLANES, LANES), (count, SUBLANES, LANES)


def to_strided(z, w):
    count = w.shape[0]
    for r in range(count):
        for k in range(w.shape[1]):
            w[r, k] = z[k, pl.ds(r, SUBLANES, stride=count), :]


def prepare_kernel(fields, matrix, ys, side, bodies, edge, folded, z, t):
    _, gy = place()
    rows = fields.shape[1]
    count = edge.shape[1]
    scales = [1.0 if f == 4 else courant for f in USED]
    for i in range(0, len(USED), 2):
        pair = [fields[USED[i + m]] * scales[i + m] for m in range(2)]
        y = permuted(jnp.concatenate(pair, axis=0), matrix[...])
        for m in range(2):
            put_columns(z.at[i + m], 0, y[m * rows : (m + 1) * rows])
            to_strided(z.at[i + m], bodies.at[i + m])
    t[pl.ds(0, rows)] = both_sides(ys[...], side[...], gy)
    for r in range(count):
        value = t[pl.ds(r, SUBLANES, stride=count), :]
        for i, picked in enumerate(fixed_edges(value, gy) + state_edges(value, gy)):
            edge[i, r] = picked
    height = rows // FOLDS
    lane = lane_index((height, LANES))
    value = jnp.zeros((height, LANES), F32)
    for j in range(FOLDS):
        begin = 2 * SLOT * j
        moved = pltpu.roll(t[pl.ds(j * height, height), :], (begin - 2 * SLOT) % LANES, 1)
        value = jnp.where((lane >= begin) & (lane < begin + 2 * SLOT), moved, value)
    folded[...] = value


def prepare(n, fields, matrix, ys, side):
    rows, cols = fields.shape[1:]
    height, body, edge = layout(n, rows, cols)
    return pl.pallas_call(
        prepare_kernel,
        out_shape=(
            jax.ShapeDtypeStruct((len(USED), *body), F32),
            jax.ShapeDtypeStruct((5, *edge), F32),
            jax.ShapeDtypeStruct((rows // FOLDS, LANES), F32),
        ),
        in_specs=[VMEM] * 4,
        out_specs=(VMEM,) * 3,
        scratch_shapes=[
            pltpu.VMEM((len(USED), cols // LANES, height, LANES), F32),
            pltpu.VMEM((height, LANES), F32),
        ],
        compiler_params=pltpu.CompilerParams(vmem_limit_bytes=24 << 20),
        cost_estimate=pl.CostEstimate(flops=100 * FIELDS * rows * cols, bytes_accessed=6 << 20, transcendentals=0),
        name="prepare",
    )(fields, matrix, ys, side)


def from_strided(z, w):
    count = w.shape[0]
    for r in range(count):
        for k in range(z.shape[0]):
            z[k, pl.ds(r, SUBLANES, stride=count), :] = w[r, k] * (1.0 / courant)


def restore(ws, matrix, zs, outs):
    rows = outs.shape[1]
    flat = []
    for i, w in enumerate(ws):
        from_strided(zs.at[i], w)
        flat.append(jnp.concatenate([zs[i, k, pl.ds(0, rows)] for k in range(zs.shape[1])], axis=1))
    values = restored(jnp.concatenate(flat, axis=0), matrix[...])
    for i in range(len(ws)):
        outs[i] = values[i * rows : (i + 1) * rows]


def write(outs, targets, sems):
    copies = [pltpu.make_async_copy(outs.at[i], target, sems.at[i]) for i, target in enumerate(targets)]
    start(copies)
    return copies


def update(field, before, after, left, right, diffusion, drift_x, drift_y):
    speed_x = drift_x + field
    speed_y = drift_y + field
    laplace = (after - before) + (right - left)
    upwind_x = jnp.where(speed_x > 0.0, before, after)
    upwind_y = jnp.where(speed_y > 0.0, left, right)
    return field + diffusion * laplace - speed_x * upwind_x - speed_y * upwind_y


def step(rows, gx, gy, ws, edge, fixed, fixed_edge):
    n, count, blocks = ws.shape[:3]
    shape = (SUBLANES, LANES)
    lane, sublane = lane_index(shape), lax.broadcasted_iota(jnp.int32, shape, 0)
    at_left, at_right = lane == 0, lane == LANES - 1
    nearest = lane == jnp.where(gy == 1, 0, LANES - 1)
    cut = lax.axis_size("gx") == 2
    last_sublane, last_row = divmod(rows - 1, count)
    assert last_row < count - 1
    none_above = sublane == jnp.where(gx == 0, 0, -1)
    none_below = sublane == jnp.where(gx == 1, last_sublane, -1)

    def row(r):
        return [ws[m, r, k] for m in range(n) for k in range(blocks)] + [edge[r]]

    initial = field = row(0)
    above = [pltpu.roll(value, 1, 0) for value in row(count - 1)]
    if cut:
        above = [jnp.where(none_above, 0.0, value) for value in above]
    before = [value - other for value, other in zip(field, above)]
    for r in range(count):
        following = row(r + 1) if r < count - 1 else [pltpu.roll(value, SUBLANES - 1, 0) for value in initial]
        below = following
        if cut and r == last_row:
            below = [jnp.where(none_below, 0.0, value) for value in following]
        after = [other - value for value, other in zip(field, below)]
        border = field[-1] - pltpu.roll(field[-1], 1, 1)
        around = (before[-1], after[-1], border, pltpu.roll(border, LANES - 1, 1))
        edge[r] = update(field[-1], *around, *[fixed_edge[i, r] for i in range(3)])
        for m in range(n):
            part = slice(m * blocks, (m + 1) * blocks)
            body, body_before, body_after = field[part], before[part], after[part]
            across = jnp.where(nearest, pltpu.roll(field[-1], LANES - m * SLOT, 1) if m else field[-1], 0.0)
            left = [body[0] - jnp.where(at_left, across, pltpu.roll(body[-1], 1, 1))]
            left += [body[k] - body[k - 1] for k in range(1, blocks)]
            right = left[1:]
            right.append(jnp.where(at_right, across, pltpu.roll(body[0], LANES - 1, 1)) - body[-1])
            for k in range(blocks):
                around = (body_before[k], body_after[k], left[k], right[k])
                ws[m, r, k] = update(body[k], *around, *[fixed[i, r, k] for i in range(3)])
        field, before = following, after


def propagate(rows, gx, gy, ws, edge, fixed, fixed_edge, beside=None):
    def one(count, carry):
        step(rows, gx, gy, ws, edge, fixed, fixed_edge)
        return carry

    if beside is not None:
        beside()
        one(0, 0)
    lax.fori_loop(0, FACTOR - (beside is not None), one, 0)


def once_kernel(n, *refs):
    xr, dr, (bodies, edge, matrix), refs = refs[:n], refs[n : 2 * n], refs[2 * n : 2 * n + 3], refs[2 * n + 3 :]
    corners, sent, fixed, fixed_edge, once, e_pair, e_last = refs
    cols = matrix.shape[0]
    count, blocks = once.shape[1:3]
    rows = count * SUBLANES - n * HALO
    gx, gy = place()
    fixed[...] = bodies[pl.ds(0, 3)]
    once[...] = bodies[pl.ds(3, 3)]
    fixed_edge[...] = edge[pl.ds(0, 3)]
    e_pair[...] = edge[3]
    e_last[...] = edge[4]
    for x, d, corner in zip(xr, dr, [corners.at[e] for e in range(n)]):
        own = edges([x[f, :, pl.ds(edge_column(cols, gy), LANES)] for f in range(FIELDS)])
        corner[...] = both_sides(own, d[...], gy)
    targets = [*[fixed.at[i] for i in range(3)], *[once.at[m] for m in range(3)]]
    edge_targets = [*[fixed_edge.at[i] for i in range(3)], e_pair, e_last]
    in_place = slice(SUBLANES - 1, SUBLANES)
    converted = []
    for e, x in enumerate(xr):
        value = jnp.concatenate([x[f] * (1.0 if f == 4 else courant) for f in (*USED, 3)], axis=0)
        converted.append(permuted(value, matrix[...]))
        sent[e] = converted[e][(len(USED) - 1) * HALO :]
    for begin, there, which in fills(n, rows, gx):
        y = masked(there, converted[which])
        values = fixed_edges(corners[which], gy) + state_edges(corners[which], gy)
        for j in range(HALO):
            r = begin + j - (SUBLANES - 1) * count
            for i, target in enumerate(targets):
                for k in range(blocks):
                    at = i * HALO + j
                    target[r, k, in_place] = y[at : at + 1, k * LANES : (k + 1) * LANES]
            for target, value in zip(edge_targets, values):
                target[r, in_place] = masked(there, value[j : j + 1])

    propagate(rows, gx, gy, once.at[pl.ds(0, 2)], e_pair, fixed, fixed_edge)
    propagate(rows, gx, gy, once.at[pl.ds(2, 1)], e_last, fixed, fixed_edge)


def propagate_once(xr, dr, bodies, edge, matrix):
    n = len(xr)
    body, edge_shape = bodies.shape[1:], edge.shape[1:]
    return pl.pallas_call(
        functools.partial(once_kernel, n),
        out_shape=(
            jax.ShapeDtypeStruct((n, HALO, LANES), F32),
            jax.ShapeDtypeStruct((n, 2 * HALO, matrix.shape[0]), F32),
            jax.ShapeDtypeStruct((3, *body), F32),
            jax.ShapeDtypeStruct((3, *edge_shape), F32),
            jax.ShapeDtypeStruct((3, *body), F32),
            jax.ShapeDtypeStruct(edge_shape, F32),
        ),
        in_specs=[VMEM] * (2 * n + 3),
        out_specs=(VMEM,) * 6,
        scratch_shapes=[pltpu.VMEM(edge_shape, F32)],
        compiler_params=pltpu.CompilerParams(vmem_limit_bytes=16 << 20),
        cost_estimate=pl.CostEstimate(flops=0, bytes_accessed=12 << 20, transcendentals=0),
        name="once",
    )(*xr, *dr, bodies, edge, matrix)


def twice_kernel(n, fixed, fixed_edge, once, edge, matrix, relaxed, difference, ws, e_pair, zs, outs, sems):
    rows = outs.shape[1]
    gx, gy = place()
    restore([once.at[m] for m in range(3)], matrix, zs, outs)
    written = write(outs, [relaxed.at[m + 1] for m in range(3)], sems)
    ws[...] = once[pl.ds(0, 2)]
    e_pair[...] = edge[...]
    propagate(rows, gx, gy, ws, e_pair, fixed, fixed_edge)
    difference[...] = ws[...] - once[pl.ds(1, 2)]
    wait(written)


def propagate_twice(n, fixed, fixed_edge, once, edge, matrix):
    body, edge_shape, cols = once.shape[1:], edge.shape, matrix.shape[0]
    height = body[0] * SUBLANES
    rows = height - n * HALO
    return pl.pallas_call(
        functools.partial(twice_kernel, n),
        out_shape=(jax.ShapeDtypeStruct((4, rows, cols), F32), jax.ShapeDtypeStruct((2, *body), F32)),
        in_specs=[VMEM] * 5,
        out_specs=(HBM, VMEM),
        scratch_shapes=[
            pltpu.VMEM((2, *body), F32),
            pltpu.VMEM(edge_shape, F32),
            pltpu.VMEM((3, body[1], height, LANES), F32),
            pltpu.VMEM((3, rows, cols), F32),
            pltpu.SemaphoreType.DMA((3,)),
        ],
        compiler_params=pltpu.CompilerParams(vmem_limit_bytes=16 << 20),
        cost_estimate=pl.CostEstimate(flops=0, bytes_accessed=10 << 20, transcendentals=0),
        name="twice",
    )(fixed, fixed_edge, once, edge, matrix)


def convert_kernel(pair, matrix, bodies, z):
    rows = pair.shape[1]
    y = permuted(jnp.concatenate([pair[m] for m in range(2)], axis=0) * courant, matrix[...])
    for m in range(2):
        put_columns(z.at[m], 0, y[m * rows : (m + 1) * rows])
        to_strided(z.at[m], bodies.at[m])


def convert(pair, matrix, body):
    height = body[0] * SUBLANES
    return pl.pallas_call(
        convert_kernel,
        out_shape=jax.ShapeDtypeStruct((2, *body), F32),
        in_specs=[VMEM] * 2,
        out_specs=VMEM,
        scratch_shapes=[pltpu.VMEM((2, body[1], height, LANES), F32)],
        compiler_params=pltpu.CompilerParams(vmem_limit_bytes=16 << 20),
        cost_estimate=pl.CostEstimate(flops=0, bytes_accessed=3 << 20, transcendentals=0),
        name="convert",
    )(pair, matrix)


def received_kernel(n, bodies, halos, fields, fixed, fixed_edge, once, difference, matrix, relaxed_in, *refs):
    relaxed, residual, t, ws, edge, late, zs, outs, sems = refs
    del relaxed_in
    rows = fields.shape[1]
    count, blocks = ws.shape[1:3]
    first = lax.axis_index("ta") == 0
    gx, gy = place()
    targets = [residual.at[2], residual.at[3], relaxed.at[0], residual.at[0], residual.at[1]]

    def restore_own():
        restore([difference.at[m] for m in range(2)], matrix, zs, outs)

    @pl.when(jnp.logical_not(first))
    def _():
        fold = rows // FOLDS
        folded = halos[pl.ds(0, fold)]
        for j in range(FOLDS):
            t[pl.ds(j * fold, fold)] = aligned(folded, 2 * j, gy) * courant
        ws[...] = bodies[...]
        in_place = slice(SUBLANES - 1, SUBLANES)
        for begin, there, which in fills(n, rows, gx):
            at = fold + which * HALO * (1 + 2 * blocks)
            t[pl.ds(begin, HALO)] = masked(there, aligned(halos[pl.ds(at, HALO)], 2, gy) * courant)
            at += HALO
            for k in range(blocks):
                value = masked(there, halos[pl.ds(at + k * 2 * HALO, 2 * HALO)])
                for m in range(2):
                    for j in range(HALO):
                        row = m * HALO + j
                        ws[m, begin + j - (SUBLANES - 1) * count, k, in_place] = value[row : row + 1]
        for r in range(count):
            edge[r] = t[pl.ds(r, SUBLANES, stride=count), :]
        propagate(rows, gx, gy, ws, edge, fixed, fixed_edge, restore_own)
        written = write(outs, targets[:2], sems)
        late[0] = ws[1]

        def restore_first():
            restore([late.at[0]], matrix, zs, outs.at[pl.ds(2, 1)])

        propagate(rows, gx, gy, ws, edge, fixed, fixed_edge, restore_first)
        written += write(outs.at[pl.ds(2, 1)], targets[2:3], sems.at[pl.ds(2, 1)])
        late[1] = ws[0] - late[0]
        late[2] = ws[1] - once[0]
        restore([late.at[1], late.at[2]], matrix, zs, outs.at[pl.ds(3, 2)])
        wait(written + write(outs.at[pl.ds(3, 2)], targets[3:], sems.at[pl.ds(3, 2)]))

    @pl.when(first)
    def _():
        restore_own()
        outs[2] = fields[0]
        for m in (3, 4):
            outs[m] = jnp.zeros(outs.shape[1:], F32)
        wait(write(outs, targets, sems))


def received(n, bodies, halos, fields, fixed, fixed_edge, once, difference, matrix, relaxed):
    rows, cols = fields.shape[1:]
    height, body, edge = layout(n, rows, cols)
    shape = jax.ShapeDtypeStruct((4, rows, cols), F32)
    return pl.pallas_call(
        functools.partial(received_kernel, n),
        out_shape=(shape, shape),
        in_specs=[VMEM] * 8 + [HBM],
        out_specs=(HBM, HBM),
        scratch_shapes=[
            pltpu.VMEM((height, LANES), F32),
            pltpu.VMEM((2, *body), F32),
            pltpu.VMEM(edge, F32),
            pltpu.VMEM((3, *body), F32),
            pltpu.VMEM((2, body[1], height, LANES), F32),
            pltpu.VMEM((5, rows, cols), F32),
            pltpu.SemaphoreType.DMA((5,)),
        ],
        input_output_aliases={8: 0},
        compiler_params=pltpu.CompilerParams(vmem_limit_bytes=24 << 20),
        cost_estimate=pl.CostEstimate(flops=1600 * rows * cols, bytes_accessed=24 << 20, transcendentals=0),
        name="received",
    )(bodies, halos, fields, fixed, fixed_edge, once, difference, matrix, relaxed)


def local(c, dif, dx, dy):
    groups, nx, ny = (lax.axis_size(name) for name in ("ta", "gx", "gy"))
    rows, cols = dif.shape
    assert ny == 2 and c.shape[0] == 4 and rows % SUBLANES == 0 and cols % LANES == 0
    ends = (1,) if nx == 2 else (1, 0)
    n = len(ends)
    ring = [(i, (i + 1) % groups) for i in range(groups)]
    pair, fields = take(c, dif, dx, dy)
    pair = lax.ppermute(pair, "ta", ring)
    *sent, ys, matrix = pack(ends, fields)
    xs, ds = sent[:n], sent[n:]
    if nx == 2:
        xr = [lax.ppermute(xs[0], "gx", [(0, 1), (1, 0)])]
        dr = [lax.ppermute(ds[0], ("gx", "gy"), [(0, 3), (3, 0), (1, 2), (2, 1)])]
    else:
        hops = [[(i, i + hop) for i in range(nx) if 0 <= i + hop < nx] for hop in (1, -1)]
        xr = [lax.ppermute(x, "gx", pairs) for x, pairs in zip(xs, hops)]
        crossed = [[(i * 2 + s, j * 2 + 1 - s) for i, j in pairs for s in range(2)] for pairs in hops]
        dr = [lax.ppermute(d, ("gx", "gy"), pairs) for d, pairs in zip(ds, crossed)]
    side = lax.ppermute(ys, "gy", [(0, 1), (1, 0)])
    bodies, edge, folded = prepare(n, fields, matrix, ys, side)
    corners, sent, fixed, fixed_edge, once, edge = propagate_once(xr, dr, bodies, edge, matrix)
    halos = lax.ppermute(bundle(folded, corners, sent), "ta", ring)
    relaxed, difference = propagate_twice(n, fixed, fixed_edge, once, edge, matrix)
    bodies = convert(pair, matrix, once.shape[1:])
    return received(n, bodies, halos, fields, fixed, fixed_edge, once, difference, matrix, relaxed)


def solution(mesh):
    return jax.shard_map(
        local,
        mesh=mesh,
        in_specs=(
            P(("grp", "ta"), "gx", "gy"),
            P(("grp", "gx"), "gy"),
            P(("grp", "gx"), "gy"),
            P(("grp", "gx"), "gy"),
        ),
        out_specs=(P(("grp", "ta"), "gx", "gy"), P(("grp", "ta"), "gx", "gy")),
        check_vma=False,
    )
```

```python
import functools

import jax
import jax.numpy as jnp
from jax import lax
from jax.experimental import pallas as pl
from jax.experimental.pallas import tpu as pltpu
from jax.sharding import PartitionSpec as P

FACTOR = 4
HALO = 2 * FACTOR
LANES = 128
SUBLANES = 8
SLOT = 2 * HALO
FOLDS = LANES // (2 * HALO)
FIELDS = 7
USED = (4, 5, 6, 0, 1, 2)

courant = 0.08

VMEM = pl.BlockSpec(memory_space=pltpu.VMEM)
HBM = pl.BlockSpec(memory_space=pltpu.HBM)
F32 = jnp.float32
BF16 = jnp.bfloat16


def lane_index(shape):
    return lax.broadcasted_iota(jnp.int32, shape, len(shape) - 1)


def order(cols):
    blocks = cols // LANES
    place = lax.broadcasted_iota(jnp.int32, (cols, cols), 0)
    to = (place % blocks) * LANES + place // blocks
    return jnp.where(lane_index((cols, cols)) == to, 1.0, 0.0).astype(BF16)


def permuted(x, matrix):
    high = x.astype(BF16)
    rest = x - high.astype(F32)
    middle = rest.astype(BF16)
    low = (rest - middle.astype(F32)).astype(BF16)
    product = functools.partial(jnp.dot, preferred_element_type=F32)
    return product(high, matrix) + (product(middle, matrix) + product(low, matrix))


def restored(x, matrix):
    high = x.astype(BF16)
    low = (x - high.astype(F32)).astype(BF16)
    dims = (((1,), (1,)), ((), ()))
    product = functools.partial(lax.dot_general, dimension_numbers=dims, preferred_element_type=F32)
    return product(high, matrix) + product(low, matrix)


def start(copies):
    for copy in copies:
        copy.start()


def wait(copies):
    for copy in copies:
        copy.wait()


def place():
    return lax.axis_index("gx"), lax.axis_index("gy")


def edge_column(cols, gy):
    return pl.multiple_of((1 - gy) * (cols - LANES), LANES)


def first_row(ends, e, rows, gx):
    if len(ends) == 1:
        return pl.multiple_of((1 - gx) * (rows - HALO), HALO)
    return ends[e] * (rows - HALO)


def edges(blocks):
    lane = lane_index(blocks[0].shape)
    packed = jnp.zeros(lane.shape, F32)
    for slot, block in enumerate(blocks):
        begin = slot * SLOT
        packed = jnp.where((lane >= begin) & (lane < begin + SLOT), pltpu.roll(block, begin + HALO, 1), packed)
    return packed


def both_sides(own, other, gy):
    return jnp.where(lane_index(own.shape) // HALO % 2 == gy, own, other)


def aligned(value, slots, gy):
    return pltpu.roll(value, (2 * gy - 1 - HALO - slots * SLOT) % LANES, 1)


def turned_lane(shape, gy):
    return (lane_index(shape) + HALO + 1 - 2 * gy) % LANES


def fixed_edges(value, gy):
    lane = turned_lane(value.shape, gy)
    picked = []
    for i in range(4, FIELDS):
        twice = jnp.where(lane < SLOT, aligned(value, i, gy), aligned(value, i - 1, gy))
        picked.append(jnp.where(lane < 2 * SLOT, twice, 0.0))
    return [picked[0], picked[1] * courant, picked[2] * courant]


def state_edges(value, gy):
    return [aligned(value, 2 * i, gy) * courant for i in range(2)]


def pack_kernel(ends, fields, *refs):
    n = len(ends)
    xs, ds, (ys, matrix) = refs[:n], refs[n : 2 * n], refs[2 * n :]
    rows, cols = fields.shape[1:]
    gx, gy = place()
    for e, x in enumerate(xs):
        x[...] = fields[:, pl.ds(first_row(ends, e, rows, gx), HALO), :]
    ys[...] = edges([fields[f, :, pl.ds(edge_column(cols, gy), LANES)] for f in range(FIELDS)])
    for e, d in enumerate(ds):
        d[...] = ys[pl.ds(first_row(ends, e, rows, gx), HALO), :]
    matrix[...] = order(cols)


def pack(ends, fields):
    rows, cols = fields.shape[1:]
    n = len(ends)
    return pl.pallas_call(
        functools.partial(pack_kernel, ends),
        out_shape=(
            *[jax.ShapeDtypeStruct((FIELDS, HALO, cols), F32)] * n,
            *[jax.ShapeDtypeStruct((HALO, LANES), F32)] * n,
            jax.ShapeDtypeStruct((rows, LANES), F32),
            jax.ShapeDtypeStruct((cols, cols), BF16),
        ),
        in_specs=[VMEM],
        out_specs=(VMEM,) * (2 * n + 2),
        compiler_params=pltpu.CompilerParams(vmem_limit_bytes=16 << 20),
        name="pack",
    )(fields)


def take_kernel(c, dif, dx, dy, pair, fields, sems):
    copies = [
        pltpu.make_async_copy(c.at[pl.ds(2, 2)], fields.at[pl.ds(2, 2)], sems.at[0]),
        pltpu.make_async_copy(c.at[pl.ds(0, 2)], fields.at[pl.ds(0, 2)], sems.at[1]),
    ]
    copies += [pltpu.make_async_copy(ref, fields.at[4 + i], sems.at[2 + i]) for i, ref in enumerate((dif, dx, dy))]
    start(copies)
    wait(copies[:1])
    pair[...] = fields[pl.ds(2, 2)]
    wait(copies[1:])


def take(c, dif, dx, dy):
    return pl.pallas_call(
        take_kernel,
        out_shape=[jax.ShapeDtypeStruct((count, *dif.shape), F32) for count in (2, FIELDS)],
        in_specs=[HBM] * 4,
        out_specs=[VMEM] * 2,
        scratch_shapes=[pltpu.SemaphoreType.DMA((5,))],
        compiler_params=pltpu.CompilerParams(vmem_limit_bytes=4 << 20),
        name="take",
    )(*[pltpu.with_memory_space_constraint(x, pltpu.HBM) for x in (c, dif, dx, dy)])


def bundle_kernel(n, folded, corners, rows, out):
    at = folded.shape[0]
    out[pl.ds(0, at)] = folded[...]
    for e in range(n):
        out[pl.ds(at, HALO)] = corners[e]
        at += HALO
        for k in range(rows.shape[2] // LANES):
            out[pl.ds(at, 2 * HALO)] = rows[e, :, pl.ds(k * LANES, LANES)]
            at += 2 * HALO


def bundle(folded, corners, rows):
    n = len(corners)
    height = folded.shape[0] + n * HALO * (1 + 2 * (rows.shape[2] // LANES))
    return pl.pallas_call(
        functools.partial(bundle_kernel, n),
        out_shape=jax.ShapeDtypeStruct((height, LANES), F32),
        in_specs=[VMEM] * 3,
        out_specs=VMEM,
        compiler_params=pltpu.CompilerParams(vmem_limit_bytes=4 << 20),
        name="bundle",
    )(folded, corners, rows)


def put_columns(z, begin, value):
    rows, cols = value.shape
    for k in range(cols // LANES):
        z[k, pl.ds(begin, rows)] = value[:, k * LANES : (k + 1) * LANES]


def fills(n, rows, gx):
    if n == 1:
        return [(rows, None, 0)]
    return [(rows, gx < lax.axis_size("gx") - 1, 1), (rows + HALO, gx > 0, 0)]


def masked(there, value):
    return value if there is None else jnp.where(there, value, 0.0)


def layout(n, rows, cols):
    height = rows + n * HALO
    count = height // SUBLANES
    assert (SUBLANES - 1) * count <= rows and rows % (SUBLANES * FOLDS) == 0
    return height, (count, cols // LANES, SUBLANES, LANES), (count, SUBLANES, LANES)


def to_strided(z, w):
    count = w.shape[0]
    for r in range(count):
        for k in range(w.shape[1]):
            w[r, k] = z[k, pl.ds(r, SUBLANES, stride=count), :]


def prepare_kernel(fields, matrix, ys, side, bodies, edge, folded, z, t):
    _, gy = place()
    rows = fields.shape[1]
    count = edge.shape[1]
    scales = [1.0 if f == 4 else courant for f in USED]
    for i in range(0, len(USED), 2):
        pair = [fields[USED[i + m]] * scales[i + m] for m in range(2)]
        y = permuted(jnp.concatenate(pair, axis=0), matrix[...])
        for m in range(2):
            put_columns(z.at[i + m], 0, y[m * rows : (m + 1) * rows])
            to_strided(z.at[i + m], bodies.at[i + m])
    t[pl.ds(0, rows)] = both_sides(ys[...], side[...], gy)
    for r in range(count):
        value = t[pl.ds(r, SUBLANES, stride=count), :]
        for i, picked in enumerate(fixed_edges(value, gy) + state_edges(value, gy)):
            edge[i, r] = picked
    height = rows // FOLDS
    lane = lane_index((height, LANES))
    value = jnp.zeros((height, LANES), F32)
    for j in range(FOLDS):
        for m in range(2):
            begin = 2 * HALO * j + HALO * m
            moved = pltpu.roll(side[pl.ds(j * height, height), :], (begin - (2 + m) * SLOT - HALO * (1 - gy)) % LANES, 1)
            value = jnp.where((lane >= begin) & (lane < begin + HALO), moved, value)
    folded[...] = value


def prepare(n, fields, matrix, ys, side):
    rows, cols = fields.shape[1:]
    height, body, edge = layout(n, rows, cols)
    return pl.pallas_call(
        prepare_kernel,
        out_shape=(
            jax.ShapeDtypeStruct((len(USED), *body), F32),
            jax.ShapeDtypeStruct((5, *edge), F32),
            jax.ShapeDtypeStruct((rows // FOLDS, LANES), F32),
        ),
        in_specs=[VMEM] * 4,
        out_specs=(VMEM,) * 3,
        scratch_shapes=[
            pltpu.VMEM((len(USED), cols // LANES, height, LANES), F32),
            pltpu.VMEM((height, LANES), F32),
        ],
        compiler_params=pltpu.CompilerParams(vmem_limit_bytes=24 << 20),
        cost_estimate=pl.CostEstimate(flops=100 * FIELDS * rows * cols, bytes_accessed=6 << 20, transcendentals=0),
        name="prepare",
    )(fields, matrix, ys, side)


def from_strided(z, w):
    count = w.shape[0]
    for r in range(count):
        for k in range(z.shape[0]):
            z[k, pl.ds(r, SUBLANES, stride=count), :] = w[r, k] * (1.0 / courant)


def restore(ws, matrix, zs, outs):
    rows = outs.shape[1]
    flat = []
    for i, w in enumerate(ws):
        from_strided(zs.at[i], w)
        flat.append(jnp.concatenate([zs[i, k, pl.ds(0, rows)] for k in range(zs.shape[1])], axis=1))
    values = restored(jnp.concatenate(flat, axis=0), matrix[...])
    for i in range(len(ws)):
        outs[i] = values[i * rows : (i + 1) * rows]


def write(outs, targets, sems):
    copies = [pltpu.make_async_copy(outs.at[i], target, sems.at[i]) for i, target in enumerate(targets)]
    start(copies)
    return copies


def update(field, before, after, left, right, diffusion, drift_x, drift_y):
    speed_x = drift_x + field
    speed_y = drift_y + field
    laplace = (after - before) + (right - left)
    upwind_x = jnp.where(speed_x > 0.0, before, after)
    upwind_y = jnp.where(speed_y > 0.0, left, right)
    return field + diffusion * laplace - speed_x * upwind_x - speed_y * upwind_y


def step(rows, gx, gy, ws, edge, fixed, fixed_edge):
    n, count, blocks = ws.shape[:3]
    shape = (SUBLANES, LANES)
    lane, sublane = lane_index(shape), lax.broadcasted_iota(jnp.int32, shape, 0)
    at_left, at_right = lane == 0, lane == LANES - 1
    nearest = lane == jnp.where(gy == 1, 0, LANES - 1)
    cut = lax.axis_size("gx") == 2
    last_sublane, last_row = divmod(rows - 1, count)
    assert last_row < count - 1
    none_above = sublane == jnp.where(gx == 0, 0, -1)
    none_below = sublane == jnp.where(gx == 1, last_sublane, -1)

    def row(r):
        return [ws[m, r, k] for m in range(n) for k in range(blocks)] + [edge[r]]

    initial = field = row(0)
    above = [pltpu.roll(value, 1, 0) for value in row(count - 1)]
    if cut:
        above = [jnp.where(none_above, 0.0, value) for value in above]
    before = [value - other for value, other in zip(field, above)]
    for r in range(count):
        following = row(r + 1) if r < count - 1 else [pltpu.roll(value, SUBLANES - 1, 0) for value in initial]
        below = following
        if cut and r == last_row:
            below = [jnp.where(none_below, 0.0, value) for value in following]
        after = [other - value for value, other in zip(field, below)]
        border = field[-1] - pltpu.roll(field[-1], 1, 1)
        around = (before[-1], after[-1], border, pltpu.roll(border, LANES - 1, 1))
        edge[r] = update(field[-1], *around, *[fixed_edge[i, r] for i in range(3)])
        for m in range(n):
            part = slice(m * blocks, (m + 1) * blocks)
            body, body_before, body_after = field[part], before[part], after[part]
            across = jnp.where(nearest, pltpu.roll(field[-1], LANES - m * SLOT, 1) if m else field[-1], 0.0)
            left = [body[0] - jnp.where(at_left, across, pltpu.roll(body[-1], 1, 1))]
            left += [body[k] - body[k - 1] for k in range(1, blocks)]
            right = left[1:]
            right.append(jnp.where(at_right, across, pltpu.roll(body[0], LANES - 1, 1)) - body[-1])
            for k in range(blocks):
                around = (body_before[k], body_after[k], left[k], right[k])
                ws[m, r, k] = update(body[k], *around, *[fixed[i, r, k] for i in range(3)])
        field, before = following, after


def propagate(rows, gx, gy, ws, edge, fixed, fixed_edge, beside=None):
    def one(count, carry):
        step(rows, gx, gy, ws, edge, fixed, fixed_edge)
        return carry

    if beside is not None:
        beside()
        one(0, 0)
    lax.fori_loop(0, FACTOR - (beside is not None), one, 0)


def once_kernel(n, *refs):
    xr, dr, (bodies, edge, matrix), refs = refs[:n], refs[n : 2 * n], refs[2 * n : 2 * n + 3], refs[2 * n + 3 :]
    corners, sent, fixed, fixed_edge, once, e_pair, e_last = refs
    cols = matrix.shape[0]
    count, blocks = once.shape[1:3]
    rows = count * SUBLANES - n * HALO
    gx, gy = place()
    fixed[...] = bodies[pl.ds(0, 3)]
    once[...] = bodies[pl.ds(3, 3)]
    fixed_edge[...] = edge[pl.ds(0, 3)]
    e_pair[...] = edge[3]
    e_last[...] = edge[4]
    for x, d, corner in zip(xr, dr, [corners.at[e] for e in range(n)]):
        own = edges([x[f, :, pl.ds(edge_column(cols, gy), LANES)] for f in range(FIELDS)])
        corner[...] = both_sides(own, d[...], gy)
    targets = [*[fixed.at[i] for i in range(3)], *[once.at[m] for m in range(3)]]
    edge_targets = [*[fixed_edge.at[i] for i in range(3)], e_pair, e_last]
    in_place = slice(SUBLANES - 1, SUBLANES)
    converted = []
    for e, x in enumerate(xr):
        value = jnp.concatenate([x[f] * (1.0 if f == 4 else courant) for f in (*USED, 3)], axis=0)
        converted.append(permuted(value, matrix[...]))
        sent[e] = converted[e][(len(USED) - 1) * HALO :]
    for begin, there, which in fills(n, rows, gx):
        y = masked(there, converted[which])
        values = fixed_edges(corners[which], gy) + state_edges(corners[which], gy)
        for j in range(HALO):
            r = begin + j - (SUBLANES - 1) * count
            for i, target in enumerate(targets):
                for k in range(blocks):
                    at = i * HALO + j
                    target[r, k, in_place] = y[at : at + 1, k * LANES : (k + 1) * LANES]
            for target, value in zip(edge_targets, values):
                target[r, in_place] = masked(there, value[j : j + 1])

    propagate(rows, gx, gy, once.at[pl.ds(0, 2)], e_pair, fixed, fixed_edge)
    propagate(rows, gx, gy, once.at[pl.ds(2, 1)], e_last, fixed, fixed_edge)


def propagate_once(xr, dr, bodies, edge, matrix):
    n = len(xr)
    body, edge_shape = bodies.shape[1:], edge.shape[1:]
    return pl.pallas_call(
        functools.partial(once_kernel, n),
        out_shape=(
            jax.ShapeDtypeStruct((n, HALO, LANES), F32),
            jax.ShapeDtypeStruct((n, 2 * HALO, matrix.shape[0]), F32),
            jax.ShapeDtypeStruct((3, *body), F32),
            jax.ShapeDtypeStruct((3, *edge_shape), F32),
            jax.ShapeDtypeStruct((3, *body), F32),
            jax.ShapeDtypeStruct(edge_shape, F32),
        ),
        in_specs=[VMEM] * (2 * n + 3),
        out_specs=(VMEM,) * 6,
        scratch_shapes=[pltpu.VMEM(edge_shape, F32)],
        compiler_params=pltpu.CompilerParams(vmem_limit_bytes=16 << 20),
        cost_estimate=pl.CostEstimate(flops=0, bytes_accessed=12 << 20, transcendentals=0),
        name="once",
    )(*xr, *dr, bodies, edge, matrix)


def twice_kernel(n, fixed, fixed_edge, once, edge, matrix, relaxed, difference, ws, e_pair, zs, outs, sems):
    rows = outs.shape[1]
    gx, gy = place()
    restore([once.at[m] for m in range(3)], matrix, zs, outs)
    written = write(outs, [relaxed.at[m + 1] for m in range(3)], sems)
    ws[...] = once[pl.ds(0, 2)]
    e_pair[...] = edge[...]
    propagate(rows, gx, gy, ws, e_pair, fixed, fixed_edge)
    difference[...] = ws[...] - once[pl.ds(1, 2)]
    wait(written)


def propagate_twice(n, fixed, fixed_edge, once, edge, matrix):
    body, edge_shape, cols = once.shape[1:], edge.shape, matrix.shape[0]
    height = body[0] * SUBLANES
    rows = height - n * HALO
    return pl.pallas_call(
        functools.partial(twice_kernel, n),
        out_shape=(jax.ShapeDtypeStruct((4, rows, cols), F32), jax.ShapeDtypeStruct((2, *body), F32)),
        in_specs=[VMEM] * 5,
        out_specs=(HBM, VMEM),
        scratch_shapes=[
            pltpu.VMEM((2, *body), F32),
            pltpu.VMEM(edge_shape, F32),
            pltpu.VMEM((3, body[1], height, LANES), F32),
            pltpu.VMEM((3, rows, cols), F32),
            pltpu.SemaphoreType.DMA((3,)),
        ],
        compiler_params=pltpu.CompilerParams(vmem_limit_bytes=16 << 20),
        cost_estimate=pl.CostEstimate(flops=0, bytes_accessed=10 << 20, transcendentals=0),
        name="twice",
    )(fixed, fixed_edge, once, edge, matrix)


def convert_kernel(pair, matrix, bodies, edge, z):
    rows, cols = pair.shape[1:]
    _, gy = place()
    y = permuted(jnp.concatenate([pair[m] for m in range(2)], axis=0) * courant, matrix[...])
    for m in range(2):
        put_columns(z.at[m], 0, y[m * rows : (m + 1) * rows])
        to_strided(z.at[m], bodies.at[m])
    column = pl.ds(edge_column(cols, gy), LANES)
    moved = [pltpu.roll(pair[m, :, column], (m * SLOT - 1 + 2 * gy) % LANES, 1) for m in range(2)]
    edge[...] = jnp.where(turned_lane(moved[0].shape, gy) < SLOT, moved[0], moved[1]) * courant


def convert(pair, matrix, body):
    height = body[0] * SUBLANES
    edge = jax.ShapeDtypeStruct((pair.shape[1], LANES), F32)
    return pl.pallas_call(
        convert_kernel,
        out_shape=(jax.ShapeDtypeStruct((2, *body), F32), edge),
        in_specs=[VMEM] * 2,
        out_specs=(VMEM, VMEM),
        scratch_shapes=[pltpu.VMEM((2, body[1], height, LANES), F32)],
        compiler_params=pltpu.CompilerParams(vmem_limit_bytes=16 << 20),
        cost_estimate=pl.CostEstimate(flops=0, bytes_accessed=3 << 20, transcendentals=0),
        name="convert",
    )(pair, matrix)


def received_kernel(n, bodies, own_edge, halos, fields, fixed, fixed_edge, once, difference, matrix, relaxed_in, *refs):
    relaxed, residual, t, ws, edge, late, zs, outs, sems = refs
    del relaxed_in
    rows = fields.shape[1]
    count, blocks = ws.shape[1:3]
    first = lax.axis_index("ta") == 0
    gx, gy = place()
    targets = [residual.at[2], residual.at[3], relaxed.at[0], residual.at[0], residual.at[1]]

    def restore_own():
        restore([difference.at[m] for m in range(2)], matrix, zs, outs)

    @pl.when(jnp.logical_not(first))
    def _():
        fold = rows // FOLDS
        folded = halos[pl.ds(0, fold)]
        lane = turned_lane((fold, LANES), gy)
        for j in range(FOLDS):
            shift = -2 * HALO * j - 1 - 6 * gy
            moved = [pltpu.roll(folded, (HALO * m + shift) % LANES, 1) for m in range(2)]
            other = jnp.where(lane < SLOT, moved[0], moved[1]) * courant
            place_of = pl.ds(j * fold, fold)
            t[place_of] = jnp.where(lane // HALO % 2 == gy, own_edge[place_of], other)
        ws[...] = bodies[...]
        in_place = slice(SUBLANES - 1, SUBLANES)
        for begin, there, which in fills(n, rows, gx):
            at = fold + which * HALO * (1 + 2 * blocks)
            t[pl.ds(begin, HALO)] = masked(there, aligned(halos[pl.ds(at, HALO)], 2, gy) * courant)
            at += HALO
            for k in range(blocks):
                value = masked(there, halos[pl.ds(at + k * 2 * HALO, 2 * HALO)])
                for m in range(2):
                    for j in range(HALO):
                        row = m * HALO + j
                        ws[m, begin + j - (SUBLANES - 1) * count, k, in_place] = value[row : row + 1]
        for r in range(count):
            edge[r] = t[pl.ds(r, SUBLANES, stride=count), :]
        propagate(rows, gx, gy, ws, edge, fixed, fixed_edge, restore_own)
        written = write(outs, targets[:2], sems)
        late[0] = ws[1]

        def restore_first():
            restore([late.at[0]], matrix, zs, outs.at[pl.ds(2, 1)])

        propagate(rows, gx, gy, ws, edge, fixed, fixed_edge, restore_first)
        written += write(outs.at[pl.ds(2, 1)], targets[2:3], sems.at[pl.ds(2, 1)])
        late[1] = ws[0] - late[0]
        late[2] = ws[1] - once[0]
        restore([late.at[1], late.at[2]], matrix, zs, outs.at[pl.ds(3, 2)])
        wait(written + write(outs.at[pl.ds(3, 2)], targets[3:], sems.at[pl.ds(3, 2)]))

    @pl.when(first)
    def _():
        restore_own()
        outs[2] = fields[0]
        for m in (3, 4):
            outs[m] = jnp.zeros(outs.shape[1:], F32)
        wait(write(outs, targets, sems))


def received(n, bodies, own_edge, halos, fields, fixed, fixed_edge, once, difference, matrix, relaxed):
    rows, cols = fields.shape[1:]
    height, body, edge = layout(n, rows, cols)
    shape = jax.ShapeDtypeStruct((4, rows, cols), F32)
    return pl.pallas_call(
        functools.partial(received_kernel, n),
        out_shape=(shape, shape),
        in_specs=[VMEM] * 9 + [HBM],
        out_specs=(HBM, HBM),
        scratch_shapes=[
            pltpu.VMEM((height, LANES), F32),
            pltpu.VMEM((2, *body), F32),
            pltpu.VMEM(edge, F32),
            pltpu.VMEM((3, *body), F32),
            pltpu.VMEM((2, body[1], height, LANES), F32),
            pltpu.VMEM((5, rows, cols), F32),
            pltpu.SemaphoreType.DMA((5,)),
        ],
        input_output_aliases={9: 0},
        compiler_params=pltpu.CompilerParams(vmem_limit_bytes=24 << 20),
        cost_estimate=pl.CostEstimate(flops=1600 * rows * cols, bytes_accessed=24 << 20, transcendentals=0),
        name="received",
    )(bodies, own_edge, halos, fields, fixed, fixed_edge, once, difference, matrix, relaxed)


def local(c, dif, dx, dy):
    groups, nx, ny = (lax.axis_size(name) for name in ("ta", "gx", "gy"))
    rows, cols = dif.shape
    assert ny == 2 and c.shape[0] == 4 and rows % SUBLANES == 0 and cols % LANES == 0
    ends = (1,) if nx == 2 else (1, 0)
    n = len(ends)
    ring = [(i, (i + 1) % groups) for i in range(groups)]
    pair, fields = take(c, dif, dx, dy)
    pair = lax.ppermute(pair, "ta", ring)
    *sent, ys, matrix = pack(ends, fields)
    xs, ds = sent[:n], sent[n:]
    if nx == 2:
        xr = [lax.ppermute(xs[0], "gx", [(0, 1), (1, 0)])]
        dr = [lax.ppermute(ds[0], ("gx", "gy"), [(0, 3), (3, 0), (1, 2), (2, 1)])]
    else:
        hops = [[(i, i + hop) for i in range(nx) if 0 <= i + hop < nx] for hop in (1, -1)]
        xr = [lax.ppermute(x, "gx", pairs) for x, pairs in zip(xs, hops)]
        crossed = [[(i * 2 + s, j * 2 + 1 - s) for i, j in pairs for s in range(2)] for pairs in hops]
        dr = [lax.ppermute(d, ("gx", "gy"), pairs) for d, pairs in zip(ds, crossed)]
    side = lax.ppermute(ys, "gy", [(0, 1), (1, 0)])
    bodies, edge, folded = prepare(n, fields, matrix, ys, side)
    corners, sent, fixed, fixed_edge, once, edge = propagate_once(xr, dr, bodies, edge, matrix)
    halos = lax.ppermute(bundle(folded, corners, sent), "ta", ring)
    relaxed, difference = propagate_twice(n, fixed, fixed_edge, once, edge, matrix)
    bodies, own_edge = convert(pair, matrix, once.shape[1:])
    return received(n, bodies, own_edge, halos, fields, fixed, fixed_edge, once, difference, matrix, relaxed)


def solution(mesh):
    return jax.shard_map(
        local,
        mesh=mesh,
        in_specs=(
            P(("grp", "ta"), "gx", "gy"),
            P(("grp", "gx"), "gy"),
            P(("grp", "gx"), "gy"),
            P(("grp", "gx"), "gy"),
        ),
        out_specs=(P(("grp", "ta"), "gx", "gy"), P(("grp", "ta"), "gx", "gy")),
        check_vma=False,
    )
```

```python
import functools

import jax
import jax.numpy as jnp
from jax import lax
from jax.experimental import pallas as pl
from jax.experimental.pallas import tpu as pltpu
from jax.sharding import PartitionSpec as P

FACTOR = 4
HALO = 2 * FACTOR
LANES = 128
SUBLANES = 8
SLOT = 2 * HALO
FOLDS = LANES // (2 * HALO)
FIELDS = 7
USED = (4, 5, 6, 0, 1, 2)

courant = 0.08

VMEM = pl.BlockSpec(memory_space=pltpu.VMEM)
HBM = pl.BlockSpec(memory_space=pltpu.HBM)
F32 = jnp.float32
BF16 = jnp.bfloat16


def lane_index(shape):
    return lax.broadcasted_iota(jnp.int32, shape, len(shape) - 1)


def order(cols):
    blocks = cols // LANES
    place = lax.broadcasted_iota(jnp.int32, (cols, cols), 0)
    to = (place % blocks) * LANES + place // blocks
    return jnp.where(lane_index((cols, cols)) == to, 1.0, 0.0).astype(BF16)


def permuted(x, matrix):
    high = x.astype(BF16)
    rest = x - high.astype(F32)
    middle = rest.astype(BF16)
    low = (rest - middle.astype(F32)).astype(BF16)
    product = functools.partial(jnp.dot, preferred_element_type=F32)
    return product(high, matrix) + (product(middle, matrix) + product(low, matrix))


def restored(x, matrix):
    high = x.astype(BF16)
    low = (x - high.astype(F32)).astype(BF16)
    dims = (((1,), (1,)), ((), ()))
    product = functools.partial(lax.dot_general, dimension_numbers=dims, preferred_element_type=F32)
    return product(high, matrix) + product(low, matrix)


def start(copies):
    for copy in copies:
        copy.start()


def wait(copies):
    for copy in copies:
        copy.wait()


def place():
    return lax.axis_index("gx"), lax.axis_index("gy")


def edge_column(cols, gy):
    return pl.multiple_of((1 - gy) * (cols - LANES), LANES)


def first_row(ends, e, rows, gx):
    if len(ends) == 1:
        return pl.multiple_of((1 - gx) * (rows - HALO), HALO)
    return ends[e] * (rows - HALO)


def edges(blocks):
    lane = lane_index(blocks[0].shape)
    packed = jnp.zeros(lane.shape, F32)
    for slot, block in enumerate(blocks):
        begin = slot * SLOT
        packed = jnp.where((lane >= begin) & (lane < begin + SLOT), pltpu.roll(block, begin + HALO, 1), packed)
    return packed


def both_sides(own, other, gy):
    return jnp.where(lane_index(own.shape) // HALO % 2 == gy, own, other)


def aligned(value, slots, gy):
    return pltpu.roll(value, (2 * gy - 1 - HALO - slots * SLOT) % LANES, 1)


def turned_lane(shape, gy):
    return (lane_index(shape) + HALO + 1 - 2 * gy) % LANES


def fixed_edges(value, gy):
    lane = turned_lane(value.shape, gy)
    picked = []
    for i in range(4, FIELDS):
        twice = jnp.where(lane < SLOT, aligned(value, i, gy), aligned(value, i - 1, gy))
        picked.append(jnp.where(lane < 2 * SLOT, twice, 0.0))
    return [picked[0], picked[1] * courant, picked[2] * courant]


def state_edges(value, gy):
    return [aligned(value, 2 * i, gy) * courant for i in range(2)]


def pack_kernel(ends, fields, *refs):
    n = len(ends)
    xs, ds, (ys, matrix) = refs[:n], refs[n : 2 * n], refs[2 * n :]
    rows, cols = fields.shape[1:]
    gx, gy = place()
    for e, x in enumerate(xs):
        x[...] = fields[:, pl.ds(first_row(ends, e, rows, gx), HALO), :]
    ys[...] = edges([fields[f, :, pl.ds(edge_column(cols, gy), LANES)] for f in range(FIELDS)])
    for e, d in enumerate(ds):
        d[...] = ys[pl.ds(first_row(ends, e, rows, gx), HALO), :]
    matrix[...] = order(cols)


def pack(ends, fields):
    rows, cols = fields.shape[1:]
    n = len(ends)
    return pl.pallas_call(
        functools.partial(pack_kernel, ends),
        out_shape=(
            *[jax.ShapeDtypeStruct((FIELDS, HALO, cols), F32)] * n,
            *[jax.ShapeDtypeStruct((HALO, LANES), F32)] * n,
            jax.ShapeDtypeStruct((rows, LANES), F32),
            jax.ShapeDtypeStruct((cols, cols), BF16),
        ),
        in_specs=[VMEM],
        out_specs=(VMEM,) * (2 * n + 2),
        compiler_params=pltpu.CompilerParams(vmem_limit_bytes=16 << 20),
        name="pack",
    )(fields)


def take_kernel(c, dif, dx, dy, pair, fields, sems):
    copies = [
        pltpu.make_async_copy(c.at[pl.ds(2, 2)], fields.at[pl.ds(2, 2)], sems.at[0]),
        pltpu.make_async_copy(c.at[pl.ds(0, 2)], fields.at[pl.ds(0, 2)], sems.at[1]),
    ]
    copies += [pltpu.make_async_copy(ref, fields.at[4 + i], sems.at[2 + i]) for i, ref in enumerate((dif, dx, dy))]
    start(copies)
    wait(copies[:1])
    pair[...] = fields[pl.ds(2, 2)]
    wait(copies[1:])


def take(c, dif, dx, dy):
    return pl.pallas_call(
        take_kernel,
        out_shape=[jax.ShapeDtypeStruct((count, *dif.shape), F32) for count in (2, FIELDS)],
        in_specs=[HBM] * 4,
        out_specs=[VMEM] * 2,
        scratch_shapes=[pltpu.SemaphoreType.DMA((5,))],
        compiler_params=pltpu.CompilerParams(vmem_limit_bytes=4 << 20),
        name="take",
    )(*[pltpu.with_memory_space_constraint(x, pltpu.HBM) for x in (c, dif, dx, dy)])


def bundle_kernel(n, folded, corners, rows, out):
    at = folded.shape[0]
    out[pl.ds(0, at)] = folded[...]
    for e in range(n):
        out[pl.ds(at, HALO)] = corners[e]
        at += HALO
        for k in range(rows.shape[2] // LANES):
            out[pl.ds(at, 2 * HALO)] = rows[e, :, pl.ds(k * LANES, LANES)]
            at += 2 * HALO


def bundle(folded, corners, rows):
    n = len(corners)
    height = folded.shape[0] + n * HALO * (1 + 2 * (rows.shape[2] // LANES))
    return pl.pallas_call(
        functools.partial(bundle_kernel, n),
        out_shape=jax.ShapeDtypeStruct((height, LANES), F32),
        in_specs=[VMEM] * 3,
        out_specs=VMEM,
        compiler_params=pltpu.CompilerParams(vmem_limit_bytes=4 << 20),
        name="bundle",
    )(folded, corners, rows)


def put_columns(z, begin, value):
    rows, cols = value.shape
    for k in range(cols // LANES):
        z[k, pl.ds(begin, rows)] = value[:, k * LANES : (k + 1) * LANES]


def fills(n, rows, gx):
    if n == 1:
        return [(rows, None, 0)]
    return [(rows, gx < lax.axis_size("gx") - 1, 1), (rows + HALO, gx > 0, 0)]


def masked(there, value):
    return value if there is None else jnp.where(there, value, 0.0)


def layout(n, rows, cols):
    height = rows + n * HALO
    count = height // SUBLANES
    assert (SUBLANES - 1) * count <= rows and rows % (SUBLANES * FOLDS) == 0
    return height, (count, cols // LANES, SUBLANES, LANES), (count, SUBLANES, LANES)


def to_strided(z, w):
    count = w.shape[0]
    for r in range(count):
        for k in range(w.shape[1]):
            w[r, k] = z[k, pl.ds(r, SUBLANES, stride=count), :]


def prepare_kernel(fields, matrix, ys, side, bodies, edge, folded, z, t):
    _, gy = place()
    rows = fields.shape[1]
    count = edge.shape[1]
    scales = [1.0 if f == 4 else courant for f in USED]
    for i in range(0, len(USED), 2):
        pair = [fields[USED[i + m]] * scales[i + m] for m in range(2)]
        y = permuted(jnp.concatenate(pair, axis=0), matrix[...])
        for m in range(2):
            put_columns(z.at[i + m], 0, y[m * rows : (m + 1) * rows])
            to_strided(z.at[i + m], bodies.at[i + m])
    t[pl.ds(0, rows)] = both_sides(ys[...], side[...], gy)
    for r in range(count):
        value = t[pl.ds(r, SUBLANES, stride=count), :]
        for i, picked in enumerate(fixed_edges(value, gy) + state_edges(value, gy)):
            edge[i, r] = picked
    height = rows // FOLDS
    lane = lane_index((height, LANES))
    value = jnp.zeros((height, LANES), F32)
    for j in range(FOLDS):
        for m in range(2):
            begin = 2 * HALO * j + HALO * m
            moved = pltpu.roll(side[pl.ds(j * height, height), :], (begin - (2 + m) * SLOT - HALO * (1 - gy)) % LANES, 1)
            value = jnp.where((lane >= begin) & (lane < begin + HALO), moved, value)
    folded[...] = value


def prepare(n, fields, matrix, ys, side):
    rows, cols = fields.shape[1:]
    height, body, edge = layout(n, rows, cols)
    return pl.pallas_call(
        prepare_kernel,
        out_shape=(
            jax.ShapeDtypeStruct((len(USED), *body), F32),
            jax.ShapeDtypeStruct((5, *edge), F32),
            jax.ShapeDtypeStruct((rows // FOLDS, LANES), F32),
        ),
        in_specs=[VMEM] * 4,
        out_specs=(VMEM,) * 3,
        scratch_shapes=[
            pltpu.VMEM((len(USED), cols // LANES, height, LANES), F32),
            pltpu.VMEM((height, LANES), F32),
        ],
        compiler_params=pltpu.CompilerParams(vmem_limit_bytes=24 << 20),
        cost_estimate=pl.CostEstimate(flops=100 * FIELDS * rows * cols, bytes_accessed=6 << 20, transcendentals=0),
        name="prepare",
    )(fields, matrix, ys, side)


def from_strided(z, w, other=None):
    count = w.shape[0]
    for r in range(count):
        for k in range(z.shape[0]):
            value = w[r, k] if other is None else w[r, k] - other[r, k]
            z[k, pl.ds(r, SUBLANES, stride=count), :] = value * (1.0 / courant)


def restore(ws, matrix, zs, outs, others=None):
    rows = outs.shape[1]
    flat = []
    for i, w in enumerate(ws):
        from_strided(zs.at[i], w, None if others is None else others[i])
        flat.append(jnp.concatenate([zs[i, k, pl.ds(0, rows)] for k in range(zs.shape[1])], axis=1))
    values = restored(jnp.concatenate(flat, axis=0), matrix[...])
    for i in range(len(ws)):
        outs[i] = values[i * rows : (i + 1) * rows]


def write(outs, targets, sems):
    copies = [pltpu.make_async_copy(outs.at[i], target, sems.at[i]) for i, target in enumerate(targets)]
    start(copies)
    return copies


def update(field, before, after, left, right, diffusion, drift_x, drift_y):
    speed_x = drift_x + field
    speed_y = drift_y + field
    laplace = (after - before) + (right - left)
    upwind_x = jnp.where(speed_x > 0.0, before, after)
    upwind_y = jnp.where(speed_y > 0.0, left, right)
    return field + diffusion * laplace - speed_x * upwind_x - speed_y * upwind_y


def step(rows, gx, gy, ws, edge, fixed, fixed_edge):
    n, count, blocks = ws.shape[:3]
    shape = (SUBLANES, LANES)
    lane, sublane = lane_index(shape), lax.broadcasted_iota(jnp.int32, shape, 0)
    at_left, at_right = lane == 0, lane == LANES - 1
    nearest = lane == jnp.where(gy == 1, 0, LANES - 1)
    cut = lax.axis_size("gx") == 2
    last_sublane, last_row = divmod(rows - 1, count)
    assert last_row < count - 1
    none_above = sublane == jnp.where(gx == 0, 0, -1)
    none_below = sublane == jnp.where(gx == 1, last_sublane, -1)

    def row(r):
        return [ws[m, r, k] for m in range(n) for k in range(blocks)] + [edge[r]]

    initial = field = row(0)
    above = [pltpu.roll(value, 1, 0) for value in row(count - 1)]
    if cut:
        above = [jnp.where(none_above, 0.0, value) for value in above]
    before = [value - other for value, other in zip(field, above)]
    for r in range(count):
        following = row(r + 1) if r < count - 1 else [pltpu.roll(value, SUBLANES - 1, 0) for value in initial]
        below = following
        if cut and r == last_row:
            below = [jnp.where(none_below, 0.0, value) for value in following]
        after = [other - value for value, other in zip(field, below)]
        border = field[-1] - pltpu.roll(field[-1], 1, 1)
        around = (before[-1], after[-1], border, pltpu.roll(border, LANES - 1, 1))
        edge[r] = update(field[-1], *around, *[fixed_edge[i, r] for i in range(3)])
        for m in range(n):
            part = slice(m * blocks, (m + 1) * blocks)
            body, body_before, body_after = field[part], before[part], after[part]
            across = jnp.where(nearest, pltpu.roll(field[-1], LANES - m * SLOT, 1) if m else field[-1], 0.0)
            left = [body[0] - jnp.where(at_left, across, pltpu.roll(body[-1], 1, 1))]
            left += [body[k] - body[k - 1] for k in range(1, blocks)]
            right = left[1:]
            right.append(jnp.where(at_right, across, pltpu.roll(body[0], LANES - 1, 1)) - body[-1])
            for k in range(blocks):
                around = (body_before[k], body_after[k], left[k], right[k])
                ws[m, r, k] = update(body[k], *around, *[fixed[i, r, k] for i in range(3)])
        field, before = following, after


def propagate(rows, gx, gy, ws, edge, fixed, fixed_edge, beside=None):
    def one(count, carry):
        step(rows, gx, gy, ws, edge, fixed, fixed_edge)
        return carry

    if beside is not None:
        beside()
        one(0, 0)
    lax.fori_loop(0, FACTOR - (beside is not None), one, 0)


def once_kernel(n, *refs):
    xr, dr, (bodies, edge, matrix), refs = refs[:n], refs[n : 2 * n], refs[2 * n : 2 * n + 3], refs[2 * n + 3 :]
    corners, sent, fixed, fixed_edge, once, e_pair, restored_once, e_last, zs = refs
    cols = matrix.shape[0]
    count, blocks = once.shape[1:3]
    rows = count * SUBLANES - n * HALO
    gx, gy = place()
    fixed[...] = bodies[pl.ds(0, 3)]
    once[...] = bodies[pl.ds(3, 3)]
    fixed_edge[...] = edge[pl.ds(0, 3)]
    e_pair[...] = edge[3]
    e_last[...] = edge[4]
    for x, d, corner in zip(xr, dr, [corners.at[e] for e in range(n)]):
        own = edges([x[f, :, pl.ds(edge_column(cols, gy), LANES)] for f in range(FIELDS)])
        corner[...] = both_sides(own, d[...], gy)
    targets = [*[fixed.at[i] for i in range(3)], *[once.at[m] for m in range(3)]]
    edge_targets = [*[fixed_edge.at[i] for i in range(3)], e_pair, e_last]
    in_place = slice(SUBLANES - 1, SUBLANES)
    converted = []
    for e, x in enumerate(xr):
        value = jnp.concatenate([x[f] * (1.0 if f == 4 else courant) for f in (*USED, 3)], axis=0)
        converted.append(permuted(value, matrix[...]))
        sent[e] = converted[e][(len(USED) - 1) * HALO :]
    for begin, there, which in fills(n, rows, gx):
        y = masked(there, converted[which])
        values = fixed_edges(corners[which], gy) + state_edges(corners[which], gy)
        for j in range(HALO):
            r = begin + j - (SUBLANES - 1) * count
            for i, target in enumerate(targets):
                for k in range(blocks):
                    at = i * HALO + j
                    target[r, k, in_place] = y[at : at + 1, k * LANES : (k + 1) * LANES]
            for target, value in zip(edge_targets, values):
                target[r, in_place] = masked(there, value[j : j + 1])

    propagate(rows, gx, gy, once.at[pl.ds(0, 2)], e_pair, fixed, fixed_edge)
    propagate(rows, gx, gy, once.at[pl.ds(2, 1)], e_last, fixed, fixed_edge)
    restore([once.at[m] for m in range(3)], matrix, zs, restored_once)


def propagate_once(xr, dr, bodies, edge, matrix):
    n = len(xr)
    body, edge_shape = bodies.shape[1:], edge.shape[1:]
    return pl.pallas_call(
        functools.partial(once_kernel, n),
        out_shape=(
            jax.ShapeDtypeStruct((n, HALO, LANES), F32),
            jax.ShapeDtypeStruct((n, 2 * HALO, matrix.shape[0]), F32),
            jax.ShapeDtypeStruct((3, *body), F32),
            jax.ShapeDtypeStruct((3, *edge_shape), F32),
            jax.ShapeDtypeStruct((3, *body), F32),
            jax.ShapeDtypeStruct(edge_shape, F32),
            jax.ShapeDtypeStruct((3, body[0] * SUBLANES - n * HALO, matrix.shape[0]), F32),
        ),
        in_specs=[VMEM] * (2 * n + 3),
        out_specs=(VMEM,) * 7,
        scratch_shapes=[
            pltpu.VMEM(edge_shape, F32),
            pltpu.VMEM((3, body[1], body[0] * SUBLANES, LANES), F32),
        ],
        compiler_params=pltpu.CompilerParams(vmem_limit_bytes=16 << 20),
        cost_estimate=pl.CostEstimate(flops=0, bytes_accessed=12 << 20, transcendentals=0),
        name="once",
    )(*xr, *dr, bodies, edge, matrix)


def twice_kernel(n, fixed, fixed_edge, once, edge, outs, relaxed, difference, ws, e_pair, sems):
    rows = outs.shape[1]
    gx, gy = place()
    written = write(outs, [relaxed.at[m + 1] for m in range(3)], sems)
    ws[...] = once[pl.ds(0, 2)]
    e_pair[...] = edge[...]
    propagate(rows, gx, gy, ws, e_pair, fixed, fixed_edge)
    difference[...] = ws[...] - once[pl.ds(1, 2)]
    wait(written)


def propagate_twice(n, fixed, fixed_edge, once, edge, outs):
    body, edge_shape = once.shape[1:], edge.shape
    rows, cols = outs.shape[1:]
    return pl.pallas_call(
        functools.partial(twice_kernel, n),
        out_shape=(jax.ShapeDtypeStruct((4, rows, cols), F32), jax.ShapeDtypeStruct((2, *body), F32)),
        in_specs=[VMEM] * 5,
        out_specs=(HBM, VMEM),
        scratch_shapes=[
            pltpu.VMEM((2, *body), F32),
            pltpu.VMEM(edge_shape, F32),
            pltpu.SemaphoreType.DMA((3,)),
        ],
        compiler_params=pltpu.CompilerParams(vmem_limit_bytes=16 << 20),
        cost_estimate=pl.CostEstimate(flops=0, bytes_accessed=10 << 20, transcendentals=0),
        name="twice",
    )(fixed, fixed_edge, once, edge, outs)


def convert_kernel(pair, matrix, bodies, edge, z):
    rows, cols = pair.shape[1:]
    _, gy = place()
    y = permuted(jnp.concatenate([pair[m] for m in range(2)], axis=0) * courant, matrix[...])
    for m in range(2):
        put_columns(z.at[m], 0, y[m * rows : (m + 1) * rows])
        to_strided(z.at[m], bodies.at[m])
    column = pl.ds(edge_column(cols, gy), LANES)
    moved = [pltpu.roll(pair[m, :, column], (m * SLOT - 1 + 2 * gy) % LANES, 1) for m in range(2)]
    edge[...] = jnp.where(turned_lane(moved[0].shape, gy) < SLOT, moved[0], moved[1]) * courant


def convert(pair, matrix, body):
    height = body[0] * SUBLANES
    edge = jax.ShapeDtypeStruct((pair.shape[1], LANES), F32)
    return pl.pallas_call(
        convert_kernel,
        out_shape=(jax.ShapeDtypeStruct((2, *body), F32), edge),
        in_specs=[VMEM] * 2,
        out_specs=(VMEM, VMEM),
        scratch_shapes=[pltpu.VMEM((2, body[1], height, LANES), F32)],
        compiler_params=pltpu.CompilerParams(vmem_limit_bytes=16 << 20),
        cost_estimate=pl.CostEstimate(flops=0, bytes_accessed=3 << 20, transcendentals=0),
        name="convert",
    )(pair, matrix)


def received_kernel(n, bodies, own_edge, halos, fields, fixed, fixed_edge, once, difference, matrix, relaxed_in, *refs):
    relaxed, residual, t, ws, edge, late, zs, outs, sems = refs
    del relaxed_in
    rows = fields.shape[1]
    count, blocks = ws.shape[1:3]
    first = lax.axis_index("ta") == 0
    gx, gy = place()
    targets = [residual.at[2], residual.at[3], relaxed.at[0], residual.at[0], residual.at[1]]

    def restore_own():
        restore([difference.at[m] for m in range(2)], matrix, zs, outs)

    @pl.when(jnp.logical_not(first))
    def _():
        fold = rows // FOLDS
        folded = halos[pl.ds(0, fold)]
        lane = turned_lane((fold, LANES), gy)
        for j in range(FOLDS):
            shift = -2 * HALO * j - 1 - 6 * gy
            moved = [pltpu.roll(folded, (HALO * m + shift) % LANES, 1) for m in range(2)]
            other = jnp.where(lane < SLOT, moved[0], moved[1]) * courant
            place_of = pl.ds(j * fold, fold)
            t[place_of] = jnp.where(lane // HALO % 2 == gy, own_edge[place_of], other)
        ws[...] = bodies[...]
        in_place = slice(SUBLANES - 1, SUBLANES)
        for begin, there, which in fills(n, rows, gx):
            at = fold + which * HALO * (1 + 2 * blocks)
            t[pl.ds(begin, HALO)] = masked(there, aligned(halos[pl.ds(at, HALO)], 2, gy) * courant)
            at += HALO
            for k in range(blocks):
                value = masked(there, halos[pl.ds(at + k * 2 * HALO, 2 * HALO)])
                for m in range(2):
                    for j in range(HALO):
                        row = m * HALO + j
                        ws[m, begin + j - (SUBLANES - 1) * count, k, in_place] = value[row : row + 1]
        for r in range(count):
            edge[r] = t[pl.ds(r, SUBLANES, stride=count), :]
        propagate(rows, gx, gy, ws, edge, fixed, fixed_edge, restore_own)
        written = write(outs, targets[:2], sems)
        late[0] = ws[1]

        def restore_first():
            restore([late.at[0]], matrix, zs, outs.at[pl.ds(2, 1)])

        propagate(rows, gx, gy, ws, edge, fixed, fixed_edge, restore_first)
        written += write(outs.at[pl.ds(2, 1)], targets[2:3], sems.at[pl.ds(2, 1)])
        restore([ws.at[0], ws.at[1]], matrix, zs, outs.at[pl.ds(3, 2)], [late.at[0], once.at[0]])
        wait(written + write(outs.at[pl.ds(3, 2)], targets[3:], sems.at[pl.ds(3, 2)]))

    @pl.when(first)
    def _():
        restore_own()
        outs[2] = fields[0]
        for m in (3, 4):
            outs[m] = jnp.zeros(outs.shape[1:], F32)
        wait(write(outs, targets, sems))


def received(n, bodies, own_edge, halos, fields, fixed, fixed_edge, once, difference, matrix, relaxed):
    rows, cols = fields.shape[1:]
    height, body, edge = layout(n, rows, cols)
    shape = jax.ShapeDtypeStruct((4, rows, cols), F32)
    return pl.pallas_call(
        functools.partial(received_kernel, n),
        out_shape=(shape, shape),
        in_specs=[VMEM] * 9 + [HBM],
        out_specs=(HBM, HBM),
        scratch_shapes=[
            pltpu.VMEM((height, LANES), F32),
            pltpu.VMEM((2, *body), F32),
            pltpu.VMEM(edge, F32),
            pltpu.VMEM((1, *body), F32),
            pltpu.VMEM((2, body[1], height, LANES), F32),
            pltpu.VMEM((5, rows, cols), F32),
            pltpu.SemaphoreType.DMA((5,)),
        ],
        input_output_aliases={9: 0},
        compiler_params=pltpu.CompilerParams(vmem_limit_bytes=24 << 20),
        cost_estimate=pl.CostEstimate(flops=1600 * rows * cols, bytes_accessed=24 << 20, transcendentals=0),
        name="received",
    )(bodies, own_edge, halos, fields, fixed, fixed_edge, once, difference, matrix, relaxed)


def local(c, dif, dx, dy):
    groups, nx, ny = (lax.axis_size(name) for name in ("ta", "gx", "gy"))
    rows, cols = dif.shape
    assert ny == 2 and c.shape[0] == 4 and rows % SUBLANES == 0 and cols % LANES == 0
    ends = (1,) if nx == 2 else (1, 0)
    n = len(ends)
    ring = [(i, (i + 1) % groups) for i in range(groups)]
    pair, fields = take(c, dif, dx, dy)
    pair = lax.ppermute(pair, "ta", ring)
    *sent, ys, matrix = pack(ends, fields)
    xs, ds = sent[:n], sent[n:]
    if nx == 2:
        xr = [lax.ppermute(xs[0], "gx", [(0, 1), (1, 0)])]
        dr = [lax.ppermute(ds[0], ("gx", "gy"), [(0, 3), (3, 0), (1, 2), (2, 1)])]
    else:
        hops = [[(i, i + hop) for i in range(nx) if 0 <= i + hop < nx] for hop in (1, -1)]
        xr = [lax.ppermute(x, "gx", pairs) for x, pairs in zip(xs, hops)]
        crossed = [[(i * 2 + s, j * 2 + 1 - s) for i, j in pairs for s in range(2)] for pairs in hops]
        dr = [lax.ppermute(d, ("gx", "gy"), pairs) for d, pairs in zip(ds, crossed)]
    side = lax.ppermute(ys, "gy", [(0, 1), (1, 0)])
    bodies, edge, folded = prepare(n, fields, matrix, ys, side)
    corners, sent, fixed, fixed_edge, once, edge, outs = propagate_once(xr, dr, bodies, edge, matrix)
    halos = lax.ppermute(bundle(folded, corners, sent), "ta", ring)
    relaxed, difference = propagate_twice(n, fixed, fixed_edge, once, edge, outs)
    bodies, own_edge = convert(pair, matrix, once.shape[1:])
    return received(n, bodies, own_edge, halos, fields, fixed, fixed_edge, once, difference, matrix, relaxed)


def solution(mesh):
    return jax.shard_map(
        local,
        mesh=mesh,
        in_specs=(
            P(("grp", "ta"), "gx", "gy"),
            P(("grp", "gx"), "gy"),
            P(("grp", "gx"), "gy"),
            P(("grp", "gx"), "gy"),
        ),
        out_specs=(P(("grp", "ta"), "gx", "gy"), P(("grp", "ta"), "gx", "gy")),
        check_vma=False,
    )
```

```python
import functools

import jax
import jax.numpy as jnp
from jax import lax
from jax.experimental import pallas as pl
from jax.experimental.pallas import tpu as pltpu
from jax.sharding import PartitionSpec as P

FACTOR = 4
HALO = 2 * FACTOR
LANES = 128
SUBLANES = 8
SLOT = 2 * HALO
FOLDS = LANES // (2 * HALO)
FIELDS = 7
USED = (4, 5, 6, 0, 1, 2)

courant = 0.08

VMEM = pl.BlockSpec(memory_space=pltpu.VMEM)
HBM = pl.BlockSpec(memory_space=pltpu.HBM)
F32 = jnp.float32
BF16 = jnp.bfloat16


def lane_index(shape):
    return lax.broadcasted_iota(jnp.int32, shape, len(shape) - 1)


def order(cols):
    blocks = cols // LANES
    place = lax.broadcasted_iota(jnp.int32, (cols, cols), 0)
    to = (place % blocks) * LANES + place // blocks
    return jnp.where(lane_index((cols, cols)) == to, 1.0, 0.0).astype(BF16)


def permuted(x, matrix):
    high = x.astype(BF16)
    rest = x - high.astype(F32)
    middle = rest.astype(BF16)
    low = (rest - middle.astype(F32)).astype(BF16)
    product = functools.partial(jnp.dot, preferred_element_type=F32)
    return product(high, matrix) + (product(middle, matrix) + product(low, matrix))


def restored(x, matrix):
    high = x.astype(BF16)
    low = (x - high.astype(F32)).astype(BF16)
    dims = (((1,), (1,)), ((), ()))
    product = functools.partial(lax.dot_general, dimension_numbers=dims, preferred_element_type=F32)
    return product(high, matrix) + product(low, matrix)


def start(copies):
    for copy in copies:
        copy.start()


def wait(copies):
    for copy in copies:
        copy.wait()


def place():
    return lax.axis_index("gx"), lax.axis_index("gy")


def edge_column(cols, gy):
    return pl.multiple_of((1 - gy) * (cols - LANES), LANES)


def first_row(ends, e, rows, gx):
    if len(ends) == 1:
        return pl.multiple_of((1 - gx) * (rows - HALO), HALO)
    return ends[e] * (rows - HALO)


def edges(blocks):
    lane = lane_index(blocks[0].shape)
    packed = jnp.zeros(lane.shape, F32)
    for slot, block in enumerate(blocks):
        begin = slot * SLOT
        packed = jnp.where((lane >= begin) & (lane < begin + SLOT), pltpu.roll(block, begin + HALO, 1), packed)
    return packed


def both_sides(own, other, gy):
    return jnp.where(lane_index(own.shape) // HALO % 2 == gy, own, other)


def aligned(value, slots, gy):
    return pltpu.roll(value, (2 * gy - 1 - HALO - slots * SLOT) % LANES, 1)


def turned_lane(shape, gy):
    return (lane_index(shape) + HALO + 1 - 2 * gy) % LANES


def fixed_edges(value, gy):
    lane = turned_lane(value.shape, gy)
    picked = []
    for i in range(4, FIELDS):
        twice = jnp.where(lane < SLOT, aligned(value, i, gy), aligned(value, i - 1, gy))
        picked.append(jnp.where(lane < 2 * SLOT, twice, 0.0))
    return [picked[0], picked[1] * courant, picked[2] * courant]


def state_edges(value, gy):
    return [aligned(value, 2 * i, gy) * courant for i in range(2)]


def pack_kernel(ends, fields, *refs):
    n = len(ends)
    xs, ds, (ys, matrix) = refs[:n], refs[n : 2 * n], refs[2 * n :]
    rows, cols = fields.shape[1:]
    gx, gy = place()
    for e, x in enumerate(xs):
        x[...] = fields[:, pl.ds(first_row(ends, e, rows, gx), HALO), :]
    ys[...] = edges([fields[f, :, pl.ds(edge_column(cols, gy), LANES)] for f in range(FIELDS)])
    for e, d in enumerate(ds):
        d[...] = ys[pl.ds(first_row(ends, e, rows, gx), HALO), :]
    matrix[...] = order(cols)


def pack(ends, fields):
    rows, cols = fields.shape[1:]
    n = len(ends)
    return pl.pallas_call(
        functools.partial(pack_kernel, ends),
        out_shape=(
            *[jax.ShapeDtypeStruct((FIELDS, HALO, cols), F32)] * n,
            *[jax.ShapeDtypeStruct((HALO, LANES), F32)] * n,
            jax.ShapeDtypeStruct((rows, LANES), F32),
            jax.ShapeDtypeStruct((cols, cols), BF16),
        ),
        in_specs=[VMEM],
        out_specs=(VMEM,) * (2 * n + 2),
        compiler_params=pltpu.CompilerParams(vmem_limit_bytes=16 << 20),
        name="pack",
    )(fields)


def take_kernel(c, dif, dx, dy, pair, fields, sems):
    copies = [
        pltpu.make_async_copy(c.at[pl.ds(2, 2)], fields.at[pl.ds(2, 2)], sems.at[0]),
        pltpu.make_async_copy(c.at[pl.ds(0, 2)], fields.at[pl.ds(0, 2)], sems.at[1]),
    ]
    copies += [pltpu.make_async_copy(ref, fields.at[4 + i], sems.at[2 + i]) for i, ref in enumerate((dif, dx, dy))]
    start(copies)
    wait(copies[:1])
    pair[...] = fields[pl.ds(2, 2)]
    wait(copies[1:])


def take(c, dif, dx, dy):
    return pl.pallas_call(
        take_kernel,
        out_shape=[jax.ShapeDtypeStruct((count, *dif.shape), F32) for count in (2, FIELDS)],
        in_specs=[HBM] * 4,
        out_specs=[VMEM] * 2,
        scratch_shapes=[pltpu.SemaphoreType.DMA((5,))],
        compiler_params=pltpu.CompilerParams(vmem_limit_bytes=4 << 20),
        name="take",
    )(*[pltpu.with_memory_space_constraint(x, pltpu.HBM) for x in (c, dif, dx, dy)])


def bundle_kernel(n, folded, corners, rows, out):
    at = folded.shape[0]
    out[pl.ds(0, at)] = folded[...]
    for e in range(n):
        out[pl.ds(at, HALO)] = corners[e]
        at += HALO
        for k in range(rows.shape[2] // LANES):
            out[pl.ds(at, 2 * HALO)] = rows[e, :, pl.ds(k * LANES, LANES)]
            at += 2 * HALO


def bundle(folded, corners, rows):
    n = len(corners)
    height = folded.shape[0] + n * HALO * (1 + 2 * (rows.shape[2] // LANES))
    return pl.pallas_call(
        functools.partial(bundle_kernel, n),
        out_shape=jax.ShapeDtypeStruct((height, LANES), F32),
        in_specs=[VMEM] * 3,
        out_specs=VMEM,
        compiler_params=pltpu.CompilerParams(vmem_limit_bytes=4 << 20),
        name="bundle",
    )(folded, corners, rows)


def put_columns(z, begin, value):
    rows, cols = value.shape
    for k in range(cols // LANES):
        z[k, pl.ds(begin, rows)] = value[:, k * LANES : (k + 1) * LANES]


def fills(n, rows, gx):
    if n == 1:
        return [(rows, None, 0)]
    return [(rows, gx < lax.axis_size("gx") - 1, 1), (rows + HALO, gx > 0, 0)]


def masked(there, value):
    return value if there is None else jnp.where(there, value, 0.0)


def layout(n, rows, cols):
    height = rows + n * HALO
    count = height // SUBLANES
    assert (SUBLANES - 1) * count <= rows and rows % (SUBLANES * FOLDS) == 0
    return height, (count, cols // LANES, SUBLANES, LANES), (count, SUBLANES, LANES)


def to_strided(z, w):
    count = w.shape[0]
    for r in range(count):
        for k in range(w.shape[1]):
            w[r, k] = z[k, pl.ds(r, SUBLANES, stride=count), :]


def prepare_kernel(fields, matrix, ys, side, bodies, edge, folded, z, t):
    _, gy = place()
    rows = fields.shape[1]
    count = edge.shape[1]
    scales = [1.0 if f == 4 else courant for f in USED]
    for i in range(0, len(USED), 2):
        pair = [fields[USED[i + m]] * scales[i + m] for m in range(2)]
        y = permuted(jnp.concatenate(pair, axis=0), matrix[...])
        for m in range(2):
            put_columns(z.at[i + m], 0, y[m * rows : (m + 1) * rows])
            to_strided(z.at[i + m], bodies.at[i + m])
    t[pl.ds(0, rows)] = both_sides(ys[...], side[...], gy)
    for r in range(count):
        value = t[pl.ds(r, SUBLANES, stride=count), :]
        for i, picked in enumerate(fixed_edges(value, gy) + state_edges(value, gy)):
            edge[i, r] = picked
    height = rows // FOLDS
    lane = lane_index((height, LANES))
    value = jnp.zeros((height, LANES), F32)
    for j in range(FOLDS):
        for m in range(2):
            begin = 2 * HALO * j + HALO * m
            moved = pltpu.roll(side[pl.ds(j * height, height), :], (begin - (2 + m) * SLOT - HALO * (1 - gy)) % LANES, 1)
            value = jnp.where((lane >= begin) & (lane < begin + HALO), moved, value)
    folded[...] = value


def prepare(n, fields, matrix, ys, side):
    rows, cols = fields.shape[1:]
    height, body, edge = layout(n, rows, cols)
    return pl.pallas_call(
        prepare_kernel,
        out_shape=(
            jax.ShapeDtypeStruct((len(USED), *body), F32),
            jax.ShapeDtypeStruct((5, *edge), F32),
            jax.ShapeDtypeStruct((rows // FOLDS, LANES), F32),
        ),
        in_specs=[VMEM] * 4,
        out_specs=(VMEM,) * 3,
        scratch_shapes=[
            pltpu.VMEM((len(USED), cols // LANES, height, LANES), F32),
            pltpu.VMEM((height, LANES), F32),
        ],
        compiler_params=pltpu.CompilerParams(vmem_limit_bytes=24 << 20),
        cost_estimate=pl.CostEstimate(flops=100 * FIELDS * rows * cols, bytes_accessed=6 << 20, transcendentals=0),
        name="prepare",
    )(fields, matrix, ys, side)


def from_strided(z, w, other=None):
    count = w.shape[0]
    for r in range(count):
        for k in range(z.shape[0]):
            value = w[r, k] if other is None else w[r, k] - other[r, k]
            z[k, pl.ds(r, SUBLANES, stride=count), :] = value * (1.0 / courant)


def restore(ws, matrix, zs, outs, others=None, then=None):
    rows = outs.shape[1]
    flat = []
    for i, w in enumerate(ws):
        from_strided(zs.at[i], w, None if others is None else others[i])
        flat.append(jnp.concatenate([zs[i, k, pl.ds(0, rows)] for k in range(zs.shape[1])], axis=1))
    values = restored(jnp.concatenate(flat, axis=0), matrix[...])
    for i in range(len(ws)):
        outs[i] = values[i * rows : (i + 1) * rows]
        if then is not None:
            then(i)


def write(outs, targets, sems):
    copies = [pltpu.make_async_copy(outs.at[i], target, sems.at[i]) for i, target in enumerate(targets)]
    start(copies)
    return copies


def update(field, before, after, left, right, diffusion, drift_x, drift_y):
    speed_x = drift_x + field
    speed_y = drift_y + field
    laplace = (after - before) + (right - left)
    upwind_x = jnp.where(speed_x > 0.0, before, after)
    upwind_y = jnp.where(speed_y > 0.0, left, right)
    return field + diffusion * laplace - speed_x * upwind_x - speed_y * upwind_y


def step(rows, gx, gy, ws, edge, fixed, fixed_edge, last=False):
    n, count, blocks = ws.shape[:3]
    shape = (SUBLANES, LANES)
    lane, sublane = lane_index(shape), lax.broadcasted_iota(jnp.int32, shape, 0)
    at_left, at_right = lane == 0, lane == LANES - 1
    nearest = lane == jnp.where(gy == 1, 0, LANES - 1)
    cut = lax.axis_size("gx") == 2
    last_sublane, last_row = divmod(rows - 1, count)
    assert last_row < count - 1
    none_above = sublane == jnp.where(gx == 0, 0, -1)
    none_below = sublane == jnp.where(gx == 1, last_sublane, -1)

    def row(r):
        return [ws[m, r, k] for m in range(n) for k in range(blocks)] + [edge[r]]

    initial = field = row(0)
    above = [pltpu.roll(value, 1, 0) for value in row(count - 1)]
    if cut:
        above = [jnp.where(none_above, 0.0, value) for value in above]
    before = [value - other for value, other in zip(field, above)]
    for r in range(count):
        following = row(r + 1) if r < count - 1 else [pltpu.roll(value, SUBLANES - 1, 0) for value in initial]
        below = following
        if cut and r == last_row:
            below = [jnp.where(none_below, 0.0, value) for value in following]
        after = [other - value for value, other in zip(field, below)]
        if not last:
            border = field[-1] - pltpu.roll(field[-1], 1, 1)
            around = (before[-1], after[-1], border, pltpu.roll(border, LANES - 1, 1))
            edge[r] = update(field[-1], *around, *[fixed_edge[i, r] for i in range(3)])
        for m in range(n):
            part = slice(m * blocks, (m + 1) * blocks)
            body, body_before, body_after = field[part], before[part], after[part]
            across = jnp.where(nearest, pltpu.roll(field[-1], LANES - m * SLOT, 1) if m else field[-1], 0.0)
            left = [body[0] - jnp.where(at_left, across, pltpu.roll(body[-1], 1, 1))]
            left += [body[k] - body[k - 1] for k in range(1, blocks)]
            right = left[1:]
            right.append(jnp.where(at_right, across, pltpu.roll(body[0], LANES - 1, 1)) - body[-1])
            for k in range(blocks):
                around = (body_before[k], body_after[k], left[k], right[k])
                ws[m, r, k] = update(body[k], *around, *[fixed[i, r, k] for i in range(3)])
        field, before = following, after


def propagate(rows, gx, gy, ws, edge, fixed, fixed_edge, beside=None, last=False):
    def one(count, carry):
        step(rows, gx, gy, ws, edge, fixed, fixed_edge)
        return carry

    if beside is not None:
        beside()
        one(0, 0)
    lax.fori_loop(0, FACTOR - (beside is not None) - last, one, 0)
    if last:
        step(rows, gx, gy, ws, edge, fixed, fixed_edge, True)


def once_kernel(n, *refs):
    xr, dr, (bodies, edge, matrix), refs = refs[:n], refs[n : 2 * n], refs[2 * n : 2 * n + 3], refs[2 * n + 3 :]
    corners, sent, fixed, fixed_edge, once, e_pair, restored_once, e_last, zs = refs
    cols = matrix.shape[0]
    count, blocks = once.shape[1:3]
    rows = count * SUBLANES - n * HALO
    gx, gy = place()
    fixed[...] = bodies[pl.ds(0, 3)]
    once[...] = bodies[pl.ds(3, 3)]
    fixed_edge[...] = edge[pl.ds(0, 3)]
    e_pair[...] = edge[3]
    e_last[...] = edge[4]
    for x, d, corner in zip(xr, dr, [corners.at[e] for e in range(n)]):
        own = edges([x[f, :, pl.ds(edge_column(cols, gy), LANES)] for f in range(FIELDS)])
        corner[...] = both_sides(own, d[...], gy)
    targets = [*[fixed.at[i] for i in range(3)], *[once.at[m] for m in range(3)]]
    edge_targets = [*[fixed_edge.at[i] for i in range(3)], e_pair, e_last]
    in_place = slice(SUBLANES - 1, SUBLANES)
    converted = []
    for e, x in enumerate(xr):
        value = jnp.concatenate([x[f] * (1.0 if f == 4 else courant) for f in (*USED, 3)], axis=0)
        converted.append(permuted(value, matrix[...]))
        sent[e] = converted[e][(len(USED) - 1) * HALO :]
    for begin, there, which in fills(n, rows, gx):
        y = masked(there, converted[which])
        values = fixed_edges(corners[which], gy) + state_edges(corners[which], gy)
        for j in range(HALO):
            r = begin + j - (SUBLANES - 1) * count
            for i, target in enumerate(targets):
                for k in range(blocks):
                    at = i * HALO + j
                    target[r, k, in_place] = y[at : at + 1, k * LANES : (k + 1) * LANES]
            for target, value in zip(edge_targets, values):
                target[r, in_place] = masked(there, value[j : j + 1])

    propagate(rows, gx, gy, once.at[pl.ds(0, 2)], e_pair, fixed, fixed_edge)
    propagate(rows, gx, gy, once.at[pl.ds(2, 1)], e_last, fixed, fixed_edge)
    restore([once.at[m] for m in range(3)], matrix, zs, restored_once)


def propagate_once(xr, dr, bodies, edge, matrix):
    n = len(xr)
    body, edge_shape = bodies.shape[1:], edge.shape[1:]
    return pl.pallas_call(
        functools.partial(once_kernel, n),
        out_shape=(
            jax.ShapeDtypeStruct((n, HALO, LANES), F32),
            jax.ShapeDtypeStruct((n, 2 * HALO, matrix.shape[0]), F32),
            jax.ShapeDtypeStruct((3, *body), F32),
            jax.ShapeDtypeStruct((3, *edge_shape), F32),
            jax.ShapeDtypeStruct((3, *body), F32),
            jax.ShapeDtypeStruct(edge_shape, F32),
            jax.ShapeDtypeStruct((3, body[0] * SUBLANES - n * HALO, matrix.shape[0]), F32),
        ),
        in_specs=[VMEM] * (2 * n + 3),
        out_specs=(VMEM,) * 7,
        scratch_shapes=[
            pltpu.VMEM(edge_shape, F32),
            pltpu.VMEM((3, body[1], body[0] * SUBLANES, LANES), F32),
        ],
        compiler_params=pltpu.CompilerParams(vmem_limit_bytes=16 << 20),
        cost_estimate=pl.CostEstimate(flops=0, bytes_accessed=12 << 20, transcendentals=0),
        name="once",
    )(*xr, *dr, bodies, edge, matrix)


def twice_kernel(n, fixed, fixed_edge, once, edge, outs, relaxed, difference, ws, e_pair, sems):
    rows = outs.shape[1]
    gx, gy = place()
    written = write(outs, [relaxed.at[m + 1] for m in range(3)], sems)
    ws[...] = once[pl.ds(0, 2)]
    e_pair[...] = edge[...]
    propagate(rows, gx, gy, ws, e_pair, fixed, fixed_edge)
    difference[...] = ws[...] - once[pl.ds(1, 2)]
    wait(written)


def propagate_twice(n, fixed, fixed_edge, once, edge, outs):
    body, edge_shape = once.shape[1:], edge.shape
    rows, cols = outs.shape[1:]
    return pl.pallas_call(
        functools.partial(twice_kernel, n),
        out_shape=(jax.ShapeDtypeStruct((4, rows, cols), F32), jax.ShapeDtypeStruct((2, *body), F32)),
        in_specs=[VMEM] * 5,
        out_specs=(HBM, VMEM),
        scratch_shapes=[
            pltpu.VMEM((2, *body), F32),
            pltpu.VMEM(edge_shape, F32),
            pltpu.SemaphoreType.DMA((3,)),
        ],
        compiler_params=pltpu.CompilerParams(vmem_limit_bytes=16 << 20),
        cost_estimate=pl.CostEstimate(flops=0, bytes_accessed=10 << 20, transcendentals=0),
        name="twice",
    )(fixed, fixed_edge, once, edge, outs)


def convert_kernel(pair, matrix, bodies, edge, z):
    rows, cols = pair.shape[1:]
    _, gy = place()
    y = permuted(jnp.concatenate([pair[m] for m in range(2)], axis=0) * courant, matrix[...])
    for m in range(2):
        put_columns(z.at[m], 0, y[m * rows : (m + 1) * rows])
        to_strided(z.at[m], bodies.at[m])
    column = pl.ds(edge_column(cols, gy), LANES)
    moved = [pltpu.roll(pair[m, :, column], (m * SLOT - 1 + 2 * gy) % LANES, 1) for m in range(2)]
    edge[...] = jnp.where(turned_lane(moved[0].shape, gy) < SLOT, moved[0], moved[1]) * courant


def convert(pair, matrix, body):
    height = body[0] * SUBLANES
    edge = jax.ShapeDtypeStruct((pair.shape[1], LANES), F32)
    return pl.pallas_call(
        convert_kernel,
        out_shape=(jax.ShapeDtypeStruct((2, *body), F32), edge),
        in_specs=[VMEM] * 2,
        out_specs=(VMEM, VMEM),
        scratch_shapes=[pltpu.VMEM((2, body[1], height, LANES), F32)],
        compiler_params=pltpu.CompilerParams(vmem_limit_bytes=16 << 20),
        cost_estimate=pl.CostEstimate(flops=0, bytes_accessed=3 << 20, transcendentals=0),
        name="convert",
    )(pair, matrix)


def received_kernel(n, bodies, own_edge, halos, fields, fixed, fixed_edge, once, difference, matrix, relaxed_in, *refs):
    relaxed, residual, t, ws, edge, late, zs, outs, sems = refs
    del relaxed_in
    rows = fields.shape[1]
    count, blocks = ws.shape[1:3]
    first = lax.axis_index("ta") == 0
    gx, gy = place()
    targets = [residual.at[2], residual.at[3], relaxed.at[0], residual.at[0], residual.at[1]]

    def restore_own():
        restore([difference.at[m] for m in range(2)], matrix, zs, outs)

    @pl.when(jnp.logical_not(first))
    def _():
        fold = rows // FOLDS
        folded = halos[pl.ds(0, fold)]
        lane = turned_lane((fold, LANES), gy)
        for j in range(FOLDS):
            shift = -2 * HALO * j - 1 - 6 * gy
            moved = [pltpu.roll(folded, (HALO * m + shift) % LANES, 1) for m in range(2)]
            other = jnp.where(lane < SLOT, moved[0], moved[1]) * courant
            place_of = pl.ds(j * fold, fold)
            t[place_of] = jnp.where(lane // HALO % 2 == gy, own_edge[place_of], other)
        ws[...] = bodies[...]
        in_place = slice(SUBLANES - 1, SUBLANES)
        for begin, there, which in fills(n, rows, gx):
            at = fold + which * HALO * (1 + 2 * blocks)
            t[pl.ds(begin, HALO)] = masked(there, aligned(halos[pl.ds(at, HALO)], 2, gy) * courant)
            at += HALO
            for k in range(blocks):
                value = masked(there, halos[pl.ds(at + k * 2 * HALO, 2 * HALO)])
                for m in range(2):
                    for j in range(HALO):
                        row = m * HALO + j
                        ws[m, begin + j - (SUBLANES - 1) * count, k, in_place] = value[row : row + 1]
        for r in range(count):
            edge[r] = t[pl.ds(r, SUBLANES, stride=count), :]
        propagate(rows, gx, gy, ws, edge, fixed, fixed_edge, restore_own)
        written = write(outs, targets[:2], sems)
        late[0] = ws[1]

        def restore_first():
            restore([late.at[0]], matrix, zs, outs.at[pl.ds(2, 1)])

        propagate(rows, gx, gy, ws, edge, fixed, fixed_edge, restore_first, True)
        written += write(outs.at[pl.ds(2, 1)], targets[2:3], sems.at[pl.ds(2, 1)])

        def write_one(i):
            written.extend(write(outs.at[pl.ds(3 + i, 1)], targets[3 + i : 4 + i], sems.at[pl.ds(3 + i, 1)]))

        restore([ws.at[0], ws.at[1]], matrix, zs, outs.at[pl.ds(3, 2)], [late.at[0], once.at[0]], write_one)
        wait(written)

    @pl.when(first)
    def _():
        restore_own()
        outs[2] = fields[0]
        for m in (3, 4):
            outs[m] = jnp.zeros(outs.shape[1:], F32)
        wait(write(outs, targets, sems))


def received(n, bodies, own_edge, halos, fields, fixed, fixed_edge, once, difference, matrix, relaxed):
    rows, cols = fields.shape[1:]
    height, body, edge = layout(n, rows, cols)
    shape = jax.ShapeDtypeStruct((4, rows, cols), F32)
    return pl.pallas_call(
        functools.partial(received_kernel, n),
        out_shape=(shape, shape),
        in_specs=[VMEM] * 9 + [HBM],
        out_specs=(HBM, HBM),
        scratch_shapes=[
            pltpu.VMEM((height, LANES), F32),
            pltpu.VMEM((2, *body), F32),
            pltpu.VMEM(edge, F32),
            pltpu.VMEM((1, *body), F32),
            pltpu.VMEM((2, body[1], height, LANES), F32),
            pltpu.VMEM((5, rows, cols), F32),
            pltpu.SemaphoreType.DMA((5,)),
        ],
        input_output_aliases={9: 0},
        compiler_params=pltpu.CompilerParams(vmem_limit_bytes=24 << 20),
        cost_estimate=pl.CostEstimate(flops=1600 * rows * cols, bytes_accessed=24 << 20, transcendentals=0),
        name="received",
    )(bodies, own_edge, halos, fields, fixed, fixed_edge, once, difference, matrix, relaxed)


def local(c, dif, dx, dy):
    groups, nx, ny = (lax.axis_size(name) for name in ("ta", "gx", "gy"))
    rows, cols = dif.shape
    assert ny == 2 and c.shape[0] == 4 and rows % SUBLANES == 0 and cols % LANES == 0
    ends = (1,) if nx == 2 else (1, 0)
    n = len(ends)
    ring = [(i, (i + 1) % groups) for i in range(groups)]
    pair, fields = take(c, dif, dx, dy)
    pair = lax.ppermute(pair, "ta", ring)
    *sent, ys, matrix = pack(ends, fields)
    xs, ds = sent[:n], sent[n:]
    if nx == 2:
        xr = [lax.ppermute(xs[0], "gx", [(0, 1), (1, 0)])]
        dr = [lax.ppermute(ds[0], ("gx", "gy"), [(0, 3), (3, 0), (1, 2), (2, 1)])]
    else:
        hops = [[(i, i + hop) for i in range(nx) if 0 <= i + hop < nx] for hop in (1, -1)]
        xr = [lax.ppermute(x, "gx", pairs) for x, pairs in zip(xs, hops)]
        crossed = [[(i * 2 + s, j * 2 + 1 - s) for i, j in pairs for s in range(2)] for pairs in hops]
        dr = [lax.ppermute(d, ("gx", "gy"), pairs) for d, pairs in zip(ds, crossed)]
    side = lax.ppermute(ys, "gy", [(0, 1), (1, 0)])
    bodies, edge, folded = prepare(n, fields, matrix, ys, side)
    corners, sent, fixed, fixed_edge, once, edge, outs = propagate_once(xr, dr, bodies, edge, matrix)
    halos = lax.ppermute(bundle(folded, corners, sent), "ta", ring)
    relaxed, difference = propagate_twice(n, fixed, fixed_edge, once, edge, outs)
    bodies, own_edge = convert(pair, matrix, once.shape[1:])
    return received(n, bodies, own_edge, halos, fields, fixed, fixed_edge, once, difference, matrix, relaxed)


def solution(mesh):
    return jax.shard_map(
        local,
        mesh=mesh,
        in_specs=(
            P(("grp", "ta"), "gx", "gy"),
            P(("grp", "gx"), "gy"),
            P(("grp", "gx"), "gy"),
            P(("grp", "gx"), "gy"),
        ),
        out_specs=(P(("grp", "ta"), "gx", "gy"), P(("grp", "ta"), "gx", "gy")),
        check_vma=False,
    )
```
